32 devices in a mesh: clip: 2 (over y), seq: 4 (over z), blk: 4 (over x, core).
Axes of the slice: x: 2, y: 2, z: 4, core: 2. Of those that a mesh axis runs over, the one named last changes fastest.
Arguments:
- queries: bfloat16 [4096, 2048], P(('clip', 'seq', 'blk')), parts along dimension 0, may hold values from -6 to 6
- keys: bfloat16 [4096, 2048], P(('clip', 'seq', 'blk')), parts along dimension 0, may hold values from -6 to 6
- values: bfloat16 [4096, 2048], P(('clip', 'seq', 'blk')), parts along dimension 0, may hold values from -4 to 4
- kept: int32 [16, 16, 16], replicated, may hold values from 0 to 15, as said below
- dense_class: int32 [16], replicated, may hold values 0 or 1
Outputs:
- attended: bfloat16 [4096, 2048], P(('clip', 'seq', 'blk')), parts along dimension 0
The draws below stay inside these ranges and needn't reach their ends.
There are 2 independent parts, one for each index of `clip`. The reference program is written for one: setup_inputs(seed, part) draws one part's arguments, and reference() takes and returns one part's arrays. A program takes and returns all parts, laid end to end along the dimension named above; an argument that names none is the same for every part. Nothing has to cross between parts.
Inputs may be any that keep to these rules, and one draw needn't show every extreme that they name: For each head h, query block b and span c, kept[h, b, c * 4 + s] for s < 4 are 4 different blocks k with k % 4 == c; in the span of b itself the first of them is b.
All inputs are finite; a program needn't handle non-finite values.
Results may differ from the reference program's by a relative error of at most 0.0046.
Values may be sent and summed in bfloat16 or wider, within the bound.
No kernel may reach another device: no remote copies, remote signals or barrier semaphores. Data moves between devices by JAX's collectives and lax.ppermute only.
A program may use at most 128 MiB of HBM per device.

```python
import math
import jax
import jax.numpy as jnp
from jax import lax

HEADS = 16
HD = 128
BLOCK = 128
KEEP = 4
LIGHT = 2
TOK_DEV = 128
SEQ = 2048
NBLOCKS = 16
SPANS = 4


def draw_queries(key, part):
    key = jax.random.fold_in(key, 3)
    first_key = jax.random.fold_in(key, 0)
    attention_output = jnp.clip(jax.random.normal(first_key, (SEQ, HEADS, HD), jnp.float32), -4.0, 4.0)
    return attention_output.reshape(SEQ, HEADS * HD).astype(jnp.bfloat16)


def draw_keys(key, part):
    key = jax.random.fold_in(key, 4)
    first_key = jax.random.fold_in(key, 0)
    attention_output = jnp.clip(jax.random.normal(first_key, (SEQ, HEADS, HD), jnp.float32), -4.0, 4.0)
    return attention_output.reshape(SEQ, HEADS * HD).astype(jnp.bfloat16)


def draw_kept(key, part):
    key = jax.random.fold_in(key, 5)
    local_blocks = TOK_DEV // BLOCK
    per_span = NBLOCKS // SPANS
    random_keys = jax.random.randint(key, (HEADS, NBLOCKS, SPANS, per_span), 0, 1 << 16)
    slot_index = jnp.arange(per_span, dtype=jnp.int32)
    distinct = random_keys * per_span + slot_index
    query_block = jnp.arange(NBLOCKS, dtype=jnp.int32)
    own_span = query_block // local_blocks % SPANS
    own_slot = query_block // (local_blocks * SPANS) * local_blocks + query_block % local_blocks
    span_index = jnp.arange(SPANS, dtype=jnp.int32)
    is_self = jnp.logical_and(span_index[None, :, None] == own_span[:, None, None], slot_index[None, None, :] == own_slot[:, None, None])
    boosted = jnp.where(is_self[None], 1 << 30, distinct)
    picked = lax.top_k(boosted, KEEP)[1].astype(jnp.int32)
    block_ids = (picked // local_blocks * SPANS + span_index[None, None, :, None]) * local_blocks + picked % local_blocks
    return block_ids.reshape(HEADS, NBLOCKS, SPANS * KEEP).astype(jnp.int32)


def plant(entries, key, low, top_value):
    extent = entries.shape
    index_at = [jax.random.randint(jax.random.fold_in(key, axis), (), 0, extent[axis]) for axis in range(len(extent))]
    entries = entries.at[tuple(index_at)].set(low)
    longest = extent.index(max(extent))
    index_at[longest] = (index_at[longest] + 1) % extent[longest]
    return entries.at[tuple(index_at)].set(top_value)


def shard_levels(own_key, shape, cuts, low, high):
    def one(dim, parts):
        heights = jax.random.uniform(jax.random.fold_in(jax.random.fold_in(own_key, 6), dim), (parts,), jnp.float32, low / len(cuts), high / len(cuts))
        return jnp.repeat(jnp.exp(heights), shape[dim] // parts).reshape((-1,) + (1,) * (len(shape) - dim - 1))

    loudness = one(*cuts[0])
    for cut in cuts[1:]:
        loudness = loudness * one(*cut)
    return loudness


def scatter_about(stream_key, shape, spread, bound, pieces=(), held_as=jnp.bfloat16):
    drawn = jax.random.normal(stream_key, shape, jnp.float32) * spread
    if len(pieces) > 0:
        drawn = shard_levels(stream_key, shape, pieces, -0.22, 0.18) * drawn
    return jnp.clip(drawn, min=-bound, max=bound).astype(held_as)


def setup_inputs(seed: int = 0, part: int = 0) -> dict:
    splits = jax.random.split(jax.random.key(seed), 6)
    part_keys = jax.random.split(jax.random.fold_in(splits[5], part), 6)
    queries = draw_queries(jax.random.fold_in(jax.random.fold_in(splits[5], part), 71), part)
    keys = draw_keys(jax.random.fold_in(jax.random.fold_in(splits[5], part), 71), part)
    values = scatter_about(part_keys[2], (SEQ, HEADS * HD), 1.0, 4.0, ((0, 16),))
    kept = draw_kept(jax.random.fold_in(splits[5], 71), part)
    dense_class = plant((jax.random.randint(splits[4], (HEADS,), 0, 4) < 1).astype(jnp.int32), jax.random.fold_in(splits[4], 1), 0, 1)
    return dict(queries=queries, keys=keys, values=values, kept=kept, dense_class=dense_class)


def reference(queries, keys, values, kept, dense_class):
    total_rows = queries.shape[0]
    block_count = total_rows // BLOCK

    def by_head(array):
        return array.reshape(block_count, BLOCK, HEADS, HD).transpose(2, 0, 1, 3)
    slot_light = jnp.arange(KEEP) < LIGHT
    logit_scale_factor = 1.0 / math.sqrt(HD)

    def one_head(operands):
        query_per_head, head_k, value_per_head, head_kept, head_class = operands
        chosen = head_kept.reshape(block_count, SPANS, KEEP)
        collected_key_blocks = head_k[chosen].reshape(block_count, SPANS, KEEP * BLOCK, HD).astype(jnp.float32)
        gathered_v = value_per_head[chosen].reshape(block_count, SPANS, KEEP * BLOCK, HD).astype(jnp.float32)
        attention_logits = jnp.einsum('eoz,eptz->epot', query_per_head.astype(jnp.float32), collected_key_blocks) * logit_scale_factor
        usable = jnp.repeat(jnp.logical_or(head_class == 1, slot_light), BLOCK)
        attention_logits = jnp.where(usable, attention_logits, -jnp.inf)
        span_max = lax.optimization_barrier(jnp.max(attention_logits, axis=-1))
        weights = jnp.exp(attention_logits - span_max[..., None])
        span_total = lax.optimization_barrier(jnp.sum(weights, axis=-1))
        rounded = lax.optimization_barrier(weights.astype(jnp.bfloat16))
        span_out = jnp.einsum('bcqk,bckd->bcqd', rounded.astype(jnp.float32), gathered_v)
        largest = lax.optimization_barrier(jnp.max(span_max, axis=1, keepdims=True))
        factor = jnp.exp(span_max - largest)
        numerator = lax.optimization_barrier(jnp.sum(factor[..., None] * span_out, axis=1))
        denominator = lax.optimization_barrier(jnp.sum(factor * span_total, axis=1))
        return (numerator / denominator[..., None]).astype(jnp.bfloat16)
    per_head = lax.map(one_head, (by_head(queries), by_head(keys), by_head(values), kept, dense_class))
    return per_head.transpose(1, 2, 0, 3).reshape(total_rows, HEADS * HD)
```

```python
import math

import jax
import jax.numpy as jnp
from jax import lax
from jax.experimental import pallas as pl
from jax.experimental.pallas import tpu as pltpu
from jax.sharding import PartitionSpec as P

HEADS = 16
HD = 128
BLOCK = 128
KEEP = 4
LIGHT = 2


def combine_spans(partial_out, maxima, totals, along):
    largest = jnp.max(maxima, axis=along, keepdims=True)
    factor = jnp.exp(maxima - largest)
    numerator = jnp.sum(factor[..., None] * partial_out, axis=along)
    denominator = jnp.sum(factor * totals, axis=along)
    return (numerator / denominator[..., None]).astype(jnp.bfloat16)


def attend_blocks(query_rows, key_blocks, blocked_value_rows, local_ids, slot_count):
    query_blocks, part_rows, head_depth = query_rows.shape
    group_size = query_blocks
    while group_size * part_rows > 512 and group_size % 2 == 0:
        group_size = group_size // 2
    logit_scale_factor = 1.0 / math.sqrt(head_depth)
    block_rows = key_blocks.shape[1]

    def one_group(operands):
        queries_group, ids_group = operands
        collected_key_blocks = key_blocks[ids_group].reshape(
            group_size, slot_count * block_rows, head_depth
        )
        gathered_v = blocked_value_rows[ids_group].reshape(
            group_size, slot_count * block_rows, head_depth
        )
        attention_logits = (
            jnp.einsum(
                "gpd,gkd->gpk",
                queries_group,
                collected_key_blocks,
                preferred_element_type=jnp.float32,
            )
            * logit_scale_factor
        )
        maxima = jnp.max(attention_logits, axis=-1)
        weights = jnp.exp(attention_logits - maxima[..., None])
        totals = jnp.sum(weights, axis=-1)
        partial_out = jnp.einsum(
            "gpk,gkd->gpd",
            weights.astype(jnp.bfloat16),
            gathered_v,
            preferred_element_type=jnp.float32,
        )
        return (partial_out, maxima, totals)

    grouped_q = query_rows.reshape(query_blocks // group_size, group_size, part_rows, head_depth)
    grouped_ids = local_ids[:, :slot_count].reshape(
        query_blocks // group_size, group_size, slot_count
    )
    partial_out, maxima, totals = lax.map(one_group, (grouped_q, grouped_ids))
    return (
        partial_out.reshape(query_blocks, part_rows, head_depth),
        maxima.reshape(query_blocks, part_rows),
        totals.reshape(query_blocks, part_rows),
    )


def arrange_heads(stacked):
    swapped = jnp.swapaxes(stacked, 0, 1)
    return swapped.reshape((-1,) + stacked.shape[2:])


def spans_by_device(queries, keys, values, kept, dense_class):
    seq_devices = lax.axis_size("seq")
    span_count = lax.axis_size("blk")
    local_rows = queries.shape[0]
    head_count = HEADS
    head_depth = HD
    local_blocks = local_rows // BLOCK
    row_parts = max(1, 2 * seq_devices // head_count)
    part_rows = BLOCK // row_parts
    item_count = head_count * row_parts
    per_device = item_count // seq_devices
    seq_place = lax.axis_index("seq")
    blk_place = lax.axis_index("blk")
    every_item = jnp.arange(item_count, dtype=jnp.int32)
    all_item_heads = every_item // row_parts
    item_heads = lax.dynamic_slice_in_dim(all_item_heads, seq_place * per_device, per_device)
    grid_q = queries.reshape(local_blocks, row_parts, part_rows, head_count, head_depth).transpose(
        1, 3, 0, 2, 4
    )
    grid_q = grid_q.reshape(row_parts, head_count, local_blocks * part_rows, head_depth)
    head_keys = keys.reshape(local_rows, head_count, head_depth).transpose(1, 0, 2)
    head_values = values.reshape(local_rows, head_count, head_depth).transpose(1, 0, 2)
    send_q = arrange_heads(grid_q)
    q_items = lax.all_to_all(send_q, "seq", split_axis=0, concat_axis=1, tiled=True)
    stride = 1
    grid_k = jnp.broadcast_to(head_keys[None], (row_parts, head_count, local_rows, head_depth))
    grid_v = jnp.broadcast_to(head_values[None], (row_parts, head_count, local_rows, head_depth))
    send_k = arrange_heads(grid_k)
    send_v = arrange_heads(grid_v)
    k_held, v_held = (
        lax.all_to_all(send_k, "seq", split_axis=0, concat_axis=1, tiled=True),
        lax.all_to_all(send_v, "seq", split_axis=0, concat_axis=1, tiled=True),
    )
    key_blocks = k_held.reshape(per_device, seq_devices * local_blocks, BLOCK, head_depth)
    blocked_value_rows = v_held.reshape(per_device, seq_devices * local_blocks, BLOCK, head_depth)
    item_slot = jnp.arange(per_device, dtype=jnp.int32) // stride
    item_class = jnp.take(dense_class, item_heads)
    item_kept = jnp.take(kept, item_heads, axis=0)
    source_index = jnp.arange(seq_devices, dtype=jnp.int32)
    block_index = jnp.arange(local_blocks, dtype=jnp.int32)
    span_index = jnp.arange(span_count, dtype=jnp.int32)
    all_ids = (
        (source_index[None, :, None] * span_count + span_index[:, None, None]) * local_blocks
        + block_index[None, None, :]
    ).reshape(-1)
    all_kept = jnp.take(item_kept, all_ids, axis=1)
    span_ids = lax.dynamic_slice_in_dim(all_kept, blk_place * KEEP, KEEP, axis=2)
    q_all = lax.all_gather(q_items, "blk", axis=1, tiled=True)
    query_rows = q_all.reshape(
        per_device, span_count * seq_devices * local_blocks, part_rows, head_depth
    )

    def one_item(operands):
        rows_item, ids_item, class_item, slot_item = operands
        keys_item = lax.dynamic_index_in_dim(key_blocks, slot_item, 0, keepdims=False)
        values_item = lax.dynamic_index_in_dim(blocked_value_rows, slot_item, 0, keepdims=False)
        return lax.cond(
            class_item == 1,
            lambda: attend_blocks(rows_item, keys_item, values_item, ids_item, KEEP),
            lambda: attend_blocks(rows_item, keys_item, values_item, ids_item, LIGHT),
        )

    partial_out, maxima, totals = lax.map(
        one_item,
        (
            query_rows,
            span_ids // (local_blocks * span_count) * local_blocks + span_ids % local_blocks,
            item_class,
            item_slot,
        ),
    )
    own_blocks = seq_devices * local_blocks
    shaped_out = partial_out.reshape(per_device, span_count, own_blocks, part_rows, head_depth)
    shaped_max = maxima.reshape(per_device, span_count, own_blocks, part_rows)
    shaped_total = totals.reshape(per_device, span_count, own_blocks, part_rows)
    got_out, got_max, got_total = (
        lax.all_to_all(shaped_out, "blk", split_axis=1, concat_axis=1, tiled=True),
        lax.all_to_all(shaped_max, "blk", split_axis=1, concat_axis=1, tiled=True),
        lax.all_to_all(shaped_total, "blk", split_axis=1, concat_axis=1, tiled=True),
    )
    attended_items = combine_spans(got_out, got_max, got_total, 1)
    attended_items = attended_items.reshape(
        per_device, seq_devices * local_blocks * part_rows, head_depth
    )
    returned = lax.all_to_all(attended_items, "seq", split_axis=1, concat_axis=0, tiled=True)
    grid_out = returned.reshape(head_count, row_parts, local_blocks, part_rows, head_depth)
    grid_out = jnp.swapaxes(grid_out, 0, 1)
    return grid_out.transpose(2, 0, 3, 1, 4).reshape(local_rows, head_count * head_depth)


def head_kernel(axes, kept_hbm, class_ref, qkv_ref, out_ref, kept_ref, v_all, k_few, v_few, kept_sem):
    block_count = qkv_ref.shape[0]
    head_count = class_ref.shape[0]
    head = 0
    for axis in axes:
        head = head * lax.axis_size(axis) + lax.axis_index(axis)
    kept_copy = pltpu.make_async_copy(kept_hbm.at[head], kept_ref, kept_sem)
    kept_copy.start()
    kept_copy.wait()
    exponent_scale = math.log2(math.e) / math.sqrt(HD)

    def attend(query_rows, key_rows, value_rows):
        logits = lax.dot_general(
            query_rows, key_rows, (((1,), (1,)), ((), ())), preferred_element_type=jnp.float32
        )
        largest = jnp.max(logits, axis=-1, keepdims=True)
        weights = jnp.exp2((logits - largest) * exponent_scale).astype(jnp.bfloat16)
        summed = jnp.dot(weights, value_rows, preferred_element_type=jnp.float32)
        return (summed[:, :HD] / summed[:, HD:]).astype(jnp.bfloat16)

    @pl.when(class_ref[head] == 1)
    def _():
        v_all[:, :, :HD] = qkv_ref[:, 2]
        v_all[:, :, HD:] = jnp.ones((block_count, BLOCK, HD), jnp.bfloat16)
        key_rows = qkv_ref[:, 1].reshape(block_count * BLOCK, HD)
        value_rows = v_all[...].reshape(block_count * BLOCK, 2 * HD)
        group = 2

        def step(i, carry):
            query_rows = qkv_ref[pl.ds(i * group, group), 0].reshape(group * BLOCK, HD)
            out = attend(query_rows, key_rows, value_rows)
            out_ref[pl.ds(i * group, group)] = out.reshape(group, BLOCK, HD)
            return carry

        lax.fori_loop(0, block_count // group, step, 0)

    @pl.when(class_ref[head] != 1)
    def _():
        v_few[:, HD:] = jnp.ones((v_few.shape[0], HD), jnp.bfloat16)

        def step(b, carry):
            place = 0
            for span in range(kept_ref.shape[1] // KEEP):
                for slot in range(LIGHT):
                    block = kept_ref[b, span * KEEP + slot]
                    k_few[place * BLOCK : (place + 1) * BLOCK, :] = qkv_ref[block, 1]
                    v_few[place * BLOCK : (place + 1) * BLOCK, :HD] = qkv_ref[block, 2]
                    place += 1
            out_ref[b] = attend(qkv_ref[b, 0], k_few[...], v_few[...])
            return carry

        lax.fori_loop(0, block_count, step, 0)


def heads_by_device(queries, keys, values, kept, dense_class):
    axes = ("seq", "blk")
    local_rows = queries.shape[0]
    stacked = jnp.stack([queries, keys, values]).reshape(3, local_rows, HEADS, HD)
    send = stacked.transpose(2, 0, 1, 3)
    held = lax.all_to_all(send, axes, split_axis=0, concat_axis=0, tiled=True)
    block_count = kept.shape[1]
    few = kept.shape[2] // KEEP * LIGHT
    attended = pl.pallas_call(
        lambda *refs: head_kernel(axes, *refs),
        out_shape=jax.ShapeDtypeStruct((block_count, BLOCK, HD), jnp.bfloat16),
        in_specs=[
            pl.BlockSpec(memory_space=pl.ANY),
            pl.BlockSpec(memory_space=pltpu.SMEM),
            pl.BlockSpec(memory_space=pltpu.VMEM),
        ],
        out_specs=pl.BlockSpec(memory_space=pltpu.VMEM),
        scratch_shapes=[
            pltpu.SMEM(kept.shape[1:], jnp.int32),
            pltpu.VMEM((block_count, BLOCK, 2 * HD), jnp.bfloat16),
            pltpu.VMEM((few * BLOCK, HD), jnp.bfloat16),
            pltpu.VMEM((few * BLOCK, 2 * HD), jnp.bfloat16),
            pltpu.SemaphoreType.DMA,
        ],
        compiler_params=pltpu.CompilerParams(vmem_limit_bytes=48 * 1024 * 1024),
        name="attend_head",
    )(kept, dense_class, held)
    returned = lax.all_to_all(attended, axes, split_axis=0, concat_axis=0, tiled=True)
    return returned.transpose(1, 0, 2).reshape(local_rows, HEADS * HD)


def shards(queries, keys, values, kept, dense_class):
    devices = lax.axis_size("seq") * lax.axis_size("blk")
    one_head_each = devices == HEADS
    one_block_each = queries.shape[0] == BLOCK
    every_block_kept = kept.shape[1] == kept.shape[2]
    if one_head_each and one_block_each and every_block_kept:
        return heads_by_device(queries, keys, values, kept, dense_class)
    return spans_by_device(queries, keys, values, kept, dense_class)


def solution(mesh):
    return jax.shard_map(
        shards,
        mesh=mesh,
        in_specs=(
            P(("clip", "seq", "blk"), None),
            P(("clip", "seq", "blk"), None),
            P(("clip", "seq", "blk"), None),
            P(),
            P(),
        ),
        out_specs=P(("clip", "seq", "blk"), None),
        check_vma=False,
    )
```

```python
import math

import jax
import jax.numpy as jnp
from jax import lax
from jax.experimental import pallas as pl
from jax.experimental.pallas import tpu as pltpu
from jax.sharding import PartitionSpec as P

HEADS = 16
HD = 128
BLOCK = 128
KEEP = 4
LIGHT = 2


def combine_spans(partial_out, maxima, totals, along):
    largest = jnp.max(maxima, axis=along, keepdims=True)
    factor = jnp.exp(maxima - largest)
    numerator = jnp.sum(factor[..., None] * partial_out, axis=along)
    denominator = jnp.sum(factor * totals, axis=along)
    return (numerator / denominator[..., None]).astype(jnp.bfloat16)


def attend_blocks(query_rows, key_blocks, blocked_value_rows, local_ids, slot_count):
    query_blocks, part_rows, head_depth = query_rows.shape
    group_size = query_blocks
    while group_size * part_rows > 512 and group_size % 2 == 0:
        group_size = group_size // 2
    logit_scale_factor = 1.0 / math.sqrt(head_depth)
    block_rows = key_blocks.shape[1]

    def one_group(operands):
        queries_group, ids_group = operands
        collected_key_blocks = key_blocks[ids_group].reshape(
            group_size, slot_count * block_rows, head_depth
        )
        gathered_v = blocked_value_rows[ids_group].reshape(
            group_size, slot_count * block_rows, head_depth
        )
        attention_logits = (
            jnp.einsum(
                "gpd,gkd->gpk",
                queries_group,
                collected_key_blocks,
                preferred_element_type=jnp.float32,
            )
            * logit_scale_factor
        )
        maxima = jnp.max(attention_logits, axis=-1)
        weights = jnp.exp(attention_logits - maxima[..., None])
        totals = jnp.sum(weights, axis=-1)
        partial_out = jnp.einsum(
            "gpk,gkd->gpd",
            weights.astype(jnp.bfloat16),
            gathered_v,
            preferred_element_type=jnp.float32,
        )
        return (partial_out, maxima, totals)

    grouped_q = query_rows.reshape(query_blocks // group_size, group_size, part_rows, head_depth)
    grouped_ids = local_ids[:, :slot_count].reshape(
        query_blocks // group_size, group_size, slot_count
    )
    partial_out, maxima, totals = lax.map(one_group, (grouped_q, grouped_ids))
    return (
        partial_out.reshape(query_blocks, part_rows, head_depth),
        maxima.reshape(query_blocks, part_rows),
        totals.reshape(query_blocks, part_rows),
    )


def arrange_heads(stacked):
    swapped = jnp.swapaxes(stacked, 0, 1)
    return swapped.reshape((-1,) + stacked.shape[2:])


def spans_by_device(queries, keys, values, kept, dense_class):
    seq_devices = lax.axis_size("seq")
    span_count = lax.axis_size("blk")
    local_rows = queries.shape[0]
    head_count = HEADS
    head_depth = HD
    local_blocks = local_rows // BLOCK
    row_parts = max(1, 2 * seq_devices // head_count)
    part_rows = BLOCK // row_parts
    item_count = head_count * row_parts
    per_device = item_count // seq_devices
    seq_place = lax.axis_index("seq")
    blk_place = lax.axis_index("blk")
    every_item = jnp.arange(item_count, dtype=jnp.int32)
    all_item_heads = every_item // row_parts
    item_heads = lax.dynamic_slice_in_dim(all_item_heads, seq_place * per_device, per_device)
    grid_q = queries.reshape(local_blocks, row_parts, part_rows, head_count, head_depth).transpose(
        1, 3, 0, 2, 4
    )
    grid_q = grid_q.reshape(row_parts, head_count, local_blocks * part_rows, head_depth)
    head_keys = keys.reshape(local_rows, head_count, head_depth).transpose(1, 0, 2)
    head_values = values.reshape(local_rows, head_count, head_depth).transpose(1, 0, 2)
    send_q = arrange_heads(grid_q)
    q_items = lax.all_to_all(send_q, "seq", split_axis=0, concat_axis=1, tiled=True)
    stride = 1
    grid_k = jnp.broadcast_to(head_keys[None], (row_parts, head_count, local_rows, head_depth))
    grid_v = jnp.broadcast_to(head_values[None], (row_parts, head_count, local_rows, head_depth))
    send_k = arrange_heads(grid_k)
    send_v = arrange_heads(grid_v)
    k_held, v_held = (
        lax.all_to_all(send_k, "seq", split_axis=0, concat_axis=1, tiled=True),
        lax.all_to_all(send_v, "seq", split_axis=0, concat_axis=1, tiled=True),
    )
    key_blocks = k_held.reshape(per_device, seq_devices * local_blocks, BLOCK, head_depth)
    blocked_value_rows = v_held.reshape(per_device, seq_devices * local_blocks, BLOCK, head_depth)
    item_slot = jnp.arange(per_device, dtype=jnp.int32) // stride
    item_class = jnp.take(dense_class, item_heads)
    item_kept = jnp.take(kept, item_heads, axis=0)
    source_index = jnp.arange(seq_devices, dtype=jnp.int32)
    block_index = jnp.arange(local_blocks, dtype=jnp.int32)
    span_index = jnp.arange(span_count, dtype=jnp.int32)
    all_ids = (
        (source_index[None, :, None] * span_count + span_index[:, None, None]) * local_blocks
        + block_index[None, None, :]
    ).reshape(-1)
    all_kept = jnp.take(item_kept, all_ids, axis=1)
    span_ids = lax.dynamic_slice_in_dim(all_kept, blk_place * KEEP, KEEP, axis=2)
    q_all = lax.all_gather(q_items, "blk", axis=1, tiled=True)
    query_rows = q_all.reshape(
        per_device, span_count * seq_devices * local_blocks, part_rows, head_depth
    )

    def one_item(operands):
        rows_item, ids_item, class_item, slot_item = operands
        keys_item = lax.dynamic_index_in_dim(key_blocks, slot_item, 0, keepdims=False)
        values_item = lax.dynamic_index_in_dim(blocked_value_rows, slot_item, 0, keepdims=False)
        return lax.cond(
            class_item == 1,
            lambda: attend_blocks(rows_item, keys_item, values_item, ids_item, KEEP),
            lambda: attend_blocks(rows_item, keys_item, values_item, ids_item, LIGHT),
        )

    partial_out, maxima, totals = lax.map(
        one_item,
        (
            query_rows,
            span_ids // (local_blocks * span_count) * local_blocks + span_ids % local_blocks,
            item_class,
            item_slot,
        ),
    )
    own_blocks = seq_devices * local_blocks
    shaped_out = partial_out.reshape(per_device, span_count, own_blocks, part_rows, head_depth)
    shaped_max = maxima.reshape(per_device, span_count, own_blocks, part_rows)
    shaped_total = totals.reshape(per_device, span_count, own_blocks, part_rows)
    got_out, got_max, got_total = (
        lax.all_to_all(shaped_out, "blk", split_axis=1, concat_axis=1, tiled=True),
        lax.all_to_all(shaped_max, "blk", split_axis=1, concat_axis=1, tiled=True),
        lax.all_to_all(shaped_total, "blk", split_axis=1, concat_axis=1, tiled=True),
    )
    attended_items = combine_spans(got_out, got_max, got_total, 1)
    attended_items = attended_items.reshape(
        per_device, seq_devices * local_blocks * part_rows, head_depth
    )
    returned = lax.all_to_all(attended_items, "seq", split_axis=1, concat_axis=0, tiled=True)
    grid_out = returned.reshape(head_count, row_parts, local_blocks, part_rows, head_depth)
    grid_out = jnp.swapaxes(grid_out, 0, 1)
    return grid_out.transpose(2, 0, 3, 1, 4).reshape(local_rows, head_count * head_depth)


def own_head(axes):
    head = 0
    for axis in axes:
        head = head * lax.axis_size(axis) + lax.axis_index(axis)
    return head


def read_kept(head, kept_hbm, kept_ref, sem):
    kept_copy = pltpu.make_async_copy(kept_hbm.at[head], kept_ref, sem)
    kept_copy.start()
    kept_copy.wait()


def each_light_block(kept_ref, block):
    return [
        kept_ref[block, span * KEEP + slot]
        for span in range(kept_ref.shape[1] // KEEP)
        for slot in range(LIGHT)
    ]


def pack_kernel(*refs):
    sources, out_ref, sems = refs[:-2], refs[-2], refs[-1]
    copies = []
    for head in range(out_ref.shape[0]):
        for place, source in enumerate(sources):
            copies.append(
                pltpu.make_async_copy(
                    source.at[:, head * HD : (head + 1) * HD],
                    out_ref.at[head, place],
                    sems.at[head, place],
                )
            )
    for copy in copies:
        copy.start()
    for copy in copies:
        copy.wait()


def pack_heads(*sources):
    count = len(sources)
    rows = sources[0].shape[0]
    return pl.pallas_call(
        pack_kernel,
        out_shape=jax.ShapeDtypeStruct((HEADS, count, rows, HD), jnp.bfloat16),
        in_specs=[pl.BlockSpec(memory_space=pl.ANY)] * count,
        out_specs=pl.BlockSpec(memory_space=pltpu.VMEM),
        scratch_shapes=[pltpu.SemaphoreType.DMA((HEADS, count))],
        compiler_params=pltpu.CompilerParams(vmem_limit_bytes=4 * 1024 * 1024),
        name="pack_heads",
    )(*sources)


def unpack_kernel(held_ref, out_ref, sems):
    copies = [
        pltpu.make_async_copy(
            held_ref.at[head], out_ref.at[:, head * HD : (head + 1) * HD], sems.at[head]
        )
        for head in range(held_ref.shape[0])
    ]
    for copy in copies:
        copy.start()
    for copy in copies:
        copy.wait()


def unpack_heads(held):
    heads, rows, depth = held.shape
    return pl.pallas_call(
        unpack_kernel,
        out_shape=jax.ShapeDtypeStruct((rows, heads * depth), jnp.bfloat16),
        in_specs=[pl.BlockSpec(memory_space=pltpu.VMEM)],
        out_specs=pl.BlockSpec(memory_space=pl.ANY),
        scratch_shapes=[pltpu.SemaphoreType.DMA((heads,))],
        compiler_params=pltpu.CompilerParams(vmem_limit_bytes=4 * 1024 * 1024),
        name="unpack_heads",
    )(held)


def weights_kernel(axes, kept_hbm, class_ref, qk_ref, weights_ref, kept_ref, k_few, sem):
    block_count = qk_ref.shape[0]
    head = own_head(axes)
    read_kept(head, kept_hbm, kept_ref, sem)
    exponent_scale = math.log2(math.e) / math.sqrt(HD)

    def weigh(query_rows, key_rows):
        logits = lax.dot_general(
            query_rows, key_rows, (((1,), (1,)), ((), ())), preferred_element_type=jnp.float32
        )
        largest = jnp.max(logits, axis=-1, keepdims=True)
        return jnp.exp2((logits - largest) * exponent_scale).astype(jnp.bfloat16)

    @pl.when(class_ref[head] == 1)
    def _():
        key_rows = qk_ref[:, 1].reshape(block_count * BLOCK, HD)
        group = 2

        def step(i, carry):
            query_rows = qk_ref[pl.ds(i * group, group), 0].reshape(group * BLOCK, HD)
            weights = weigh(query_rows, key_rows)
            weights_ref[pl.ds(i * group, group)] = weights.reshape(group, BLOCK, -1)
            return carry

        lax.fori_loop(0, block_count // group, step, 0)

    @pl.when(class_ref[head] != 1)
    def _():
        few_rows = k_few.shape[1]

        def step(i, carry):
            for lane in range(2):
                b = i * 2 + lane
                for place, block in enumerate(each_light_block(kept_ref, b)):
                    k_few[lane, place * BLOCK : (place + 1) * BLOCK, :] = qk_ref[block, 1]
                weights_ref[b, :, :few_rows] = weigh(qk_ref[b, 0], k_few[lane])
            return carry

        lax.fori_loop(0, block_count // 2, step, 0)


def values_kernel(axes, kept_hbm, class_ref, weights_ref, v_ref, out_ref, kept_ref, v_all, v_few, sem):
    block_count = v_ref.shape[0]
    head = own_head(axes)
    read_kept(head, kept_hbm, kept_ref, sem)

    def blend(weights, value_rows):
        summed = jnp.dot(weights, value_rows, preferred_element_type=jnp.float32)
        return (summed[:, :HD] / summed[:, HD:]).astype(jnp.bfloat16)

    @pl.when(class_ref[head] == 1)
    def _():
        v_all[:, :, :HD] = v_ref[...]
        v_all[:, :, HD:] = jnp.ones((block_count, BLOCK, HD), jnp.bfloat16)
        value_rows = v_all[...].reshape(block_count * BLOCK, 2 * HD)
        group = 4

        def step(i, carry):
            weights = weights_ref[pl.ds(i * group, group)].reshape(group * BLOCK, -1)
            out = blend(weights, value_rows)
            out_ref[pl.ds(i * group, group)] = out.reshape(group, BLOCK, HD)
            return carry

        lax.fori_loop(0, block_count // group, step, 0)

    @pl.when(class_ref[head] != 1)
    def _():
        few_rows = v_few.shape[1]
        v_few[:, :, HD:] = jnp.ones((2, few_rows, HD), jnp.bfloat16)

        def step(i, carry):
            for lane in range(2):
                b = i * 2 + lane
                for place, block in enumerate(each_light_block(kept_ref, b)):
                    v_few[lane, place * BLOCK : (place + 1) * BLOCK, :HD] = v_ref[block]
                out_ref[b] = blend(weights_ref[b, :, :few_rows], v_few[lane])
            return carry

        lax.fori_loop(0, block_count // 2, step, 0)


def heads_by_device(queries, keys, values, kept, dense_class):
    axes = ("seq", "blk")
    block_count = kept.shape[1]
    few = kept.shape[2] // KEEP * LIGHT
    any_space = pl.BlockSpec(memory_space=pl.ANY)
    in_smem = pl.BlockSpec(memory_space=pltpu.SMEM)
    in_vmem = pl.BlockSpec(memory_space=pltpu.VMEM)
    limit = pltpu.CompilerParams(vmem_limit_bytes=24 * 1024 * 1024)

    def exchange(send):
        return lax.all_to_all(send, axes, split_axis=0, concat_axis=0, tiled=True)

    qk_held = exchange(pack_heads(queries, keys))
    v_held = exchange(pack_heads(values))
    weights = pl.pallas_call(
        lambda *refs: weights_kernel(axes, *refs),
        out_shape=jax.ShapeDtypeStruct((block_count, BLOCK, block_count * BLOCK), jnp.bfloat16),
        in_specs=[any_space, in_smem, in_vmem],
        out_specs=in_vmem,
        scratch_shapes=[
            pltpu.SMEM(kept.shape[1:], jnp.int32),
            pltpu.VMEM((2, few * BLOCK, HD), jnp.bfloat16),
            pltpu.SemaphoreType.DMA,
        ],
        compiler_params=limit,
        cost_estimate=pl.CostEstimate(
            flops=2 * HD * (block_count * BLOCK) ** 2,
            bytes_accessed=2 * (block_count * BLOCK) ** 2,
            transcendentals=(block_count * BLOCK) ** 2,
        ),
        name="weigh_keys",
    )(kept, dense_class, qk_held)
    attended = pl.pallas_call(
        lambda *refs: values_kernel(axes, *refs),
        out_shape=jax.ShapeDtypeStruct((block_count, BLOCK, HD), jnp.bfloat16),
        in_specs=[any_space, in_smem, in_vmem, in_vmem],
        out_specs=in_vmem,
        scratch_shapes=[
            pltpu.SMEM(kept.shape[1:], jnp.int32),
            pltpu.VMEM((block_count, BLOCK, 2 * HD), jnp.bfloat16),
            pltpu.VMEM((2, few * BLOCK, 2 * HD), jnp.bfloat16),
            pltpu.SemaphoreType.DMA,
        ],
        compiler_params=limit,
        name="blend_values",
    )(kept, dense_class, weights, v_held.reshape(block_count, BLOCK, HD))
    return unpack_heads(exchange(attended))


def shards(queries, keys, values, kept, dense_class):
    devices = lax.axis_size("seq") * lax.axis_size("blk")
    one_head_each = devices == HEADS
    one_block_each = queries.shape[0] == BLOCK
    every_block_kept = kept.shape[1] == kept.shape[2]
    if one_head_each and one_block_each and every_block_kept:
        return heads_by_device(queries, keys, values, kept, dense_class)
    return spans_by_device(queries, keys, values, kept, dense_class)


def solution(mesh):
    return jax.shard_map(
        shards,
        mesh=mesh,
        in_specs=(
            P(("clip", "seq", "blk"), None),
            P(("clip", "seq", "blk"), None),
            P(("clip", "seq", "blk"), None),
            P(),
            P(),
        ),
        out_specs=P(("clip", "seq", "blk"), None),
        check_vma=False,
    )
```

```python
import math

import jax
import jax.numpy as jnp
from jax import lax
from jax.experimental import pallas as pl
from jax.experimental.pallas import tpu as pltpu
from jax.sharding import PartitionSpec as P

HEADS = 16
HD = 128
BLOCK = 128
KEEP = 4
LIGHT = 2


def combine_spans(partial_out, maxima, totals, along):
    largest = jnp.max(maxima, axis=along, keepdims=True)
    factor = jnp.exp(maxima - largest)
    numerator = jnp.sum(factor[..., None] * partial_out, axis=along)
    denominator = jnp.sum(factor * totals, axis=along)
    return (numerator / denominator[..., None]).astype(jnp.bfloat16)


def attend_blocks(query_rows, key_blocks, blocked_value_rows, local_ids, slot_count):
    query_blocks, part_rows, head_depth = query_rows.shape
    group_size = query_blocks
    while group_size * part_rows > 512 and group_size % 2 == 0:
        group_size = group_size // 2
    logit_scale_factor = 1.0 / math.sqrt(head_depth)
    block_rows = key_blocks.shape[1]

    def one_group(operands):
        queries_group, ids_group = operands
        collected_key_blocks = key_blocks[ids_group].reshape(
            group_size, slot_count * block_rows, head_depth
        )
        gathered_v = blocked_value_rows[ids_group].reshape(
            group_size, slot_count * block_rows, head_depth
        )
        attention_logits = (
            jnp.einsum(
                "gpd,gkd->gpk",
                queries_group,
                collected_key_blocks,
                preferred_element_type=jnp.float32,
            )
            * logit_scale_factor
        )
        maxima = jnp.max(attention_logits, axis=-1)
        weights = jnp.exp(attention_logits - maxima[..., None])
        totals = jnp.sum(weights, axis=-1)
        partial_out = jnp.einsum(
            "gpk,gkd->gpd",
            weights.astype(jnp.bfloat16),
            gathered_v,
            preferred_element_type=jnp.float32,
        )
        return (partial_out, maxima, totals)

    grouped_q = query_rows.reshape(query_blocks // group_size, group_size, part_rows, head_depth)
    grouped_ids = local_ids[:, :slot_count].reshape(
        query_blocks // group_size, group_size, slot_count
    )
    partial_out, maxima, totals = lax.map(one_group, (grouped_q, grouped_ids))
    return (
        partial_out.reshape(query_blocks, part_rows, head_depth),
        maxima.reshape(query_blocks, part_rows),
        totals.reshape(query_blocks, part_rows),
    )


def arrange_heads(stacked):
    swapped = jnp.swapaxes(stacked, 0, 1)
    return swapped.reshape((-1,) + stacked.shape[2:])


def spans_by_device(queries, keys, values, kept, dense_class):
    seq_devices = lax.axis_size("seq")
    span_count = lax.axis_size("blk")
    local_rows = queries.shape[0]
    head_count = HEADS
    head_depth = HD
    local_blocks = local_rows // BLOCK
    row_parts = max(1, 2 * seq_devices // head_count)
    part_rows = BLOCK // row_parts
    item_count = head_count * row_parts
    per_device = item_count // seq_devices
    seq_place = lax.axis_index("seq")
    blk_place = lax.axis_index("blk")
    every_item = jnp.arange(item_count, dtype=jnp.int32)
    all_item_heads = every_item // row_parts
    item_heads = lax.dynamic_slice_in_dim(all_item_heads, seq_place * per_device, per_device)
    grid_q = queries.reshape(local_blocks, row_parts, part_rows, head_count, head_depth).transpose(
        1, 3, 0, 2, 4
    )
    grid_q = grid_q.reshape(row_parts, head_count, local_blocks * part_rows, head_depth)
    head_keys = keys.reshape(local_rows, head_count, head_depth).transpose(1, 0, 2)
    head_values = values.reshape(local_rows, head_count, head_depth).transpose(1, 0, 2)
    send_q = arrange_heads(grid_q)
    q_items = lax.all_to_all(send_q, "seq", split_axis=0, concat_axis=1, tiled=True)
    stride = 1
    grid_k = jnp.broadcast_to(head_keys[None], (row_parts, head_count, local_rows, head_depth))
    grid_v = jnp.broadcast_to(head_values[None], (row_parts, head_count, local_rows, head_depth))
    send_k = arrange_heads(grid_k)
    send_v = arrange_heads(grid_v)
    k_held, v_held = (
        lax.all_to_all(send_k, "seq", split_axis=0, concat_axis=1, tiled=True),
        lax.all_to_all(send_v, "seq", split_axis=0, concat_axis=1, tiled=True),
    )
    key_blocks = k_held.reshape(per_device, seq_devices * local_blocks, BLOCK, head_depth)
    blocked_value_rows = v_held.reshape(per_device, seq_devices * local_blocks, BLOCK, head_depth)
    item_slot = jnp.arange(per_device, dtype=jnp.int32) // stride
    item_class = jnp.take(dense_class, item_heads)
    item_kept = jnp.take(kept, item_heads, axis=0)
    source_index = jnp.arange(seq_devices, dtype=jnp.int32)
    block_index = jnp.arange(local_blocks, dtype=jnp.int32)
    span_index = jnp.arange(span_count, dtype=jnp.int32)
    all_ids = (
        (source_index[None, :, None] * span_count + span_index[:, None, None]) * local_blocks
        + block_index[None, None, :]
    ).reshape(-1)
    all_kept = jnp.take(item_kept, all_ids, axis=1)
    span_ids = lax.dynamic_slice_in_dim(all_kept, blk_place * KEEP, KEEP, axis=2)
    q_all = lax.all_gather(q_items, "blk", axis=1, tiled=True)
    query_rows = q_all.reshape(
        per_device, span_count * seq_devices * local_blocks, part_rows, head_depth
    )

    def one_item(operands):
        rows_item, ids_item, class_item, slot_item = operands
        keys_item = lax.dynamic_index_in_dim(key_blocks, slot_item, 0, keepdims=False)
        values_item = lax.dynamic_index_in_dim(blocked_value_rows, slot_item, 0, keepdims=False)
        return lax.cond(
            class_item == 1,
            lambda: attend_blocks(rows_item, keys_item, values_item, ids_item, KEEP),
            lambda: attend_blocks(rows_item, keys_item, values_item, ids_item, LIGHT),
        )

    partial_out, maxima, totals = lax.map(
        one_item,
        (
            query_rows,
            span_ids // (local_blocks * span_count) * local_blocks + span_ids % local_blocks,
            item_class,
            item_slot,
        ),
    )
    own_blocks = seq_devices * local_blocks
    shaped_out = partial_out.reshape(per_device, span_count, own_blocks, part_rows, head_depth)
    shaped_max = maxima.reshape(per_device, span_count, own_blocks, part_rows)
    shaped_total = totals.reshape(per_device, span_count, own_blocks, part_rows)
    got_out, got_max, got_total = (
        lax.all_to_all(shaped_out, "blk", split_axis=1, concat_axis=1, tiled=True),
        lax.all_to_all(shaped_max, "blk", split_axis=1, concat_axis=1, tiled=True),
        lax.all_to_all(shaped_total, "blk", split_axis=1, concat_axis=1, tiled=True),
    )
    attended_items = combine_spans(got_out, got_max, got_total, 1)
    attended_items = attended_items.reshape(
        per_device, seq_devices * local_blocks * part_rows, head_depth
    )
    returned = lax.all_to_all(attended_items, "seq", split_axis=1, concat_axis=0, tiled=True)
    grid_out = returned.reshape(head_count, row_parts, local_blocks, part_rows, head_depth)
    grid_out = jnp.swapaxes(grid_out, 0, 1)
    return grid_out.transpose(2, 0, 3, 1, 4).reshape(local_rows, head_count * head_depth)


def own_place(axes):
    place = 0
    for axis in axes:
        place = place * lax.axis_size(axis) + lax.axis_index(axis)
    return place


def each_light_block(kept_ref, block):
    return [
        kept_ref[block, span * KEEP + slot]
        for span in range(kept_ref.shape[1] // KEEP)
        for slot in range(LIGHT)
    ]


def pack_kernel(*refs):
    sources, out_ref, sems = refs[:-2], refs[-2], refs[-1]
    copies = []
    for head in range(out_ref.shape[0]):
        for place, source in enumerate(sources):
            copies.append(
                pltpu.make_async_copy(
                    source.at[:, head * HD : (head + 1) * HD],
                    out_ref.at[head, place],
                    sems.at[head, place],
                )
            )
    for copy in copies:
        copy.start()
    for copy in copies:
        copy.wait()


def pack_heads(*sources):
    count = len(sources)
    rows = sources[0].shape[0]
    return pl.pallas_call(
        pack_kernel,
        out_shape=jax.ShapeDtypeStruct((HEADS, count, rows, HD), jnp.bfloat16),
        in_specs=[pl.BlockSpec(memory_space=pltpu.HBM)] * count,
        out_specs=pl.BlockSpec(memory_space=pltpu.VMEM),
        scratch_shapes=[pltpu.SemaphoreType.DMA((HEADS, count))],
        compiler_params=pltpu.CompilerParams(vmem_limit_bytes=4 * 1024 * 1024),
        name="pack_heads",
    )(*sources)


def unpack_kernel(axes, *refs):
    held, out_ref, sems = refs[:-2], refs[-2], refs[-1]
    me = own_place(axes)
    copies = []
    for distance, block in enumerate(held):
        column = pl.multiple_of((me ^ distance) * HD, HD)
        copies.append(
            pltpu.make_async_copy(block, out_ref.at[:, pl.ds(column, HD)], sems.at[distance])
        )
    for copy in copies:
        copy.start()
    for copy in copies:
        copy.wait()


def unpack_heads(axes, held):
    rows, depth = held[0].shape
    heads = len(held)
    return pl.pallas_call(
        lambda *refs: unpack_kernel(axes, *refs),
        out_shape=jax.ShapeDtypeStruct((rows, heads * depth), jnp.bfloat16),
        in_specs=[pl.BlockSpec(memory_space=pl.ANY)] * heads,
        out_specs=pl.BlockSpec(memory_space=pltpu.HBM),
        scratch_shapes=[pltpu.SemaphoreType.DMA((heads,))],
        compiler_params=pltpu.CompilerParams(vmem_limit_bytes=4 * 1024 * 1024),
        name="unpack_heads",
    )(*held)


def pipelined(count, score, finish):
    score(0, 0)

    def step(j, carry):
        score(2 * j + 1, 1)
        finish(2 * j, 0)
        score(2 * j + 2, 0)
        finish(2 * j + 1, 1)
        return carry

    lax.fori_loop(0, count // 2 - 1, step, 0)
    score(count - 1, 1)
    finish(count - 2, 0)
    finish(count - 1, 1)


def attend_kernel(axes, first, kept_hbm, class_ref, qkv_ref, *refs):
    (kept_ref, v_all, logits_a, logits_b, k_few, v_few, staged, sem) = refs[-8:]
    out_refs = refs[:-8]
    logits_slots = (logits_a, logits_b)
    count = len(out_refs)
    block_count = qkv_ref.shape[0]
    few_rows = v_few.shape[1]
    me = own_place(axes)
    exponent_scale = math.log2(math.e) / math.sqrt(HD)
    kept_copy = pltpu.make_async_copy(kept_hbm.at[me], kept_ref, sem)
    kept_copy.start()

    def scores(query_rows, key_rows):
        return lax.dot_general(
            query_rows, key_rows, (((1,), (1,)), ((), ())), preferred_element_type=jnp.float32
        )

    def blend(logits, value_rows):
        largest = jnp.max(logits, axis=-1, keepdims=True)
        weights = jnp.exp2((logits - largest) * exponent_scale).astype(jnp.bfloat16)
        summed = jnp.dot(weights, value_rows, preferred_element_type=jnp.float32)
        return (summed[:, :HD] / summed[:, HD:]).astype(jnp.bfloat16)

    @pl.when(class_ref[me] == 1)
    def _():
        v_all[:, :, :HD] = qkv_ref[:, 2]
        v_all[:, :, HD:] = jnp.ones((block_count, BLOCK, HD), jnp.bfloat16)
        kept_copy.wait()

        def score(i, slot):
            query_rows = jnp.concatenate(
                [qkv_ref[me ^ (first + 2 * i + half), 0] for half in range(2)], axis=0
            )
            key_rows = qkv_ref[:, 1].reshape(block_count * BLOCK, HD)
            logits_slots[slot][...] = scores(query_rows, key_rows)

        def finish(i, slot):
            value_rows = v_all[...].reshape(block_count * BLOCK, 2 * HD)
            out = blend(logits_slots[slot][...], value_rows)
            staged[pl.ds(2 * i, 2)] = out.reshape(2, BLOCK, HD)

        pipelined(count // 2, score, finish)

    @pl.when(class_ref[me] != 1)
    def _():
        v_few[:, :, HD:] = jnp.ones((2, few_rows, HD), jnp.bfloat16)
        kept_copy.wait()

        def score(i, slot):
            block = me ^ (first + i)
            for place, kept_block in enumerate(each_light_block(kept_ref, block)):
                k_few[slot, place * BLOCK : (place + 1) * BLOCK, :] = qkv_ref[kept_block, 1]
            logits_slots[slot][:BLOCK, :few_rows] = scores(qkv_ref[block, 0], k_few[slot])

        def finish(i, slot):
            block = me ^ (first + i)
            for place, kept_block in enumerate(each_light_block(kept_ref, block)):
                v_few[slot, place * BLOCK : (place + 1) * BLOCK, :HD] = qkv_ref[kept_block, 2]
            staged[i] = blend(logits_slots[slot][:BLOCK, :few_rows], v_few[slot])

        pipelined(count, score, finish)

    for place, out_ref in enumerate(out_refs):
        out_ref[...] = staged[place]


def heads_by_device(queries, keys, values, kept, dense_class):
    axes = ("seq", "blk")
    block_count = kept.shape[1]
    few = kept.shape[2] // KEEP * LIGHT
    in_vmem = pl.BlockSpec(memory_space=pltpu.VMEM)
    held = lax.all_to_all(
        pack_heads(queries, keys, values), axes, split_axis=0, concat_axis=0, tiled=True
    )

    def attend(first, count):
        return pl.pallas_call(
            lambda *refs: attend_kernel(axes, first, *refs),
            out_shape=[jax.ShapeDtypeStruct((BLOCK, HD), jnp.bfloat16)] * count,
            in_specs=[
                pl.BlockSpec(memory_space=pl.ANY),
                pl.BlockSpec(memory_space=pltpu.SMEM),
                in_vmem,
            ],
            out_specs=[in_vmem] * count,
            scratch_shapes=[
                pltpu.SMEM(kept.shape[1:], jnp.int32),
                pltpu.VMEM((block_count, BLOCK, 2 * HD), jnp.bfloat16),
                pltpu.VMEM((2 * BLOCK, block_count * BLOCK), jnp.float32),
                pltpu.VMEM((2 * BLOCK, block_count * BLOCK), jnp.float32),
                pltpu.VMEM((2, few * BLOCK, HD), jnp.bfloat16),
                pltpu.VMEM((2, few * BLOCK, 2 * HD), jnp.bfloat16),
                pltpu.VMEM((count, BLOCK, HD), jnp.bfloat16),
                pltpu.SemaphoreType.DMA,
            ],
            compiler_params=pltpu.CompilerParams(vmem_limit_bytes=32 * 1024 * 1024),
            cost_estimate=pl.CostEstimate(
                flops=4 * HD * BLOCK * count * BLOCK * block_count,
                bytes_accessed=2 * HD * BLOCK * (3 * block_count + count),
                transcendentals=BLOCK * count * BLOCK * block_count,
            ),
            name="attend_far" if first else "attend_near",
        )(kept, dense_class, held)

    half = block_count // 2
    far = attend(half, half)
    near = attend(0, half)
    returned = []
    for distance, block in enumerate(list(near) + list(far)):
        if distance > 0:
            pairs = [(i, i ^ distance) for i in range(block_count)]
            block = lax.ppermute(block, axes, pairs)
        returned.append(block)
    return unpack_heads(axes, returned)


def shards(queries, keys, values, kept, dense_class):
    devices = lax.axis_size("seq") * lax.axis_size("blk")
    one_head_each = devices == HEADS
    one_block_each = queries.shape[0] == BLOCK
    every_block_kept = kept.shape[1] == kept.shape[2]
    if one_head_each and one_block_each and every_block_kept:
        return heads_by_device(queries, keys, values, kept, dense_class)
    return spans_by_device(queries, keys, values, kept, dense_class)


def solution(mesh):
    return jax.shard_map(
        shards,
        mesh=mesh,
        in_specs=(
            P(("clip", "seq", "blk"), None),
            P(("clip", "seq", "blk"), None),
            P(("clip", "seq", "blk"), None),
            P(),
            P(),
        ),
        out_specs=P(("clip", "seq", "blk"), None),
        check_vma=False,
    )
```

```python
import math

import jax
import jax.numpy as jnp
from jax import lax
from jax.experimental import pallas as pl
from jax.experimental.pallas import tpu as pltpu
from jax.sharding import PartitionSpec as P

HEADS = 16
HD = 128
BLOCK = 128
KEEP = 4
LIGHT = 2


def combine_spans(partial_out, maxima, totals, along):
    largest = jnp.max(maxima, axis=along, keepdims=True)
    factor = jnp.exp(maxima - largest)
    numerator = jnp.sum(factor[..., None] * partial_out, axis=along)
    denominator = jnp.sum(factor * totals, axis=along)
    return (numerator / denominator[..., None]).astype(jnp.bfloat16)


def attend_blocks(query_rows, key_blocks, blocked_value_rows, local_ids, slot_count):
    query_blocks, part_rows, head_depth = query_rows.shape
    group_size = query_blocks
    while group_size * part_rows > 512 and group_size % 2 == 0:
        group_size = group_size // 2
    logit_scale_factor = 1.0 / math.sqrt(head_depth)
    block_rows = key_blocks.shape[1]

    def one_group(operands):
        queries_group, ids_group = operands
        collected_key_blocks = key_blocks[ids_group].reshape(
            group_size, slot_count * block_rows, head_depth
        )
        gathered_v = blocked_value_rows[ids_group].reshape(
            group_size, slot_count * block_rows, head_depth
        )
        attention_logits = (
            jnp.einsum(
                "gpd,gkd->gpk",
                queries_group,
                collected_key_blocks,
                preferred_element_type=jnp.float32,
            )
            * logit_scale_factor
        )
        maxima = jnp.max(attention_logits, axis=-1)
        weights = jnp.exp(attention_logits - maxima[..., None])
        totals = jnp.sum(weights, axis=-1)
        partial_out = jnp.einsum(
            "gpk,gkd->gpd",
            weights.astype(jnp.bfloat16),
            gathered_v,
            preferred_element_type=jnp.float32,
        )
        return (partial_out, maxima, totals)

    grouped_q = query_rows.reshape(query_blocks // group_size, group_size, part_rows, head_depth)
    grouped_ids = local_ids[:, :slot_count].reshape(
        query_blocks // group_size, group_size, slot_count
    )
    partial_out, maxima, totals = lax.map(one_group, (grouped_q, grouped_ids))
    return (
        partial_out.reshape(query_blocks, part_rows, head_depth),
        maxima.reshape(query_blocks, part_rows),
        totals.reshape(query_blocks, part_rows),
    )


def arrange_heads(stacked):
    swapped = jnp.swapaxes(stacked, 0, 1)
    return swapped.reshape((-1,) + stacked.shape[2:])


def spans_by_device(queries, keys, values, kept, dense_class):
    seq_devices = lax.axis_size("seq")
    span_count = lax.axis_size("blk")
    local_rows = queries.shape[0]
    head_count = HEADS
    head_depth = HD
    local_blocks = local_rows // BLOCK
    row_parts = max(1, 2 * seq_devices // head_count)
    part_rows = BLOCK // row_parts
    item_count = head_count * row_parts
    per_device = item_count // seq_devices
    seq_place = lax.axis_index("seq")
    blk_place = lax.axis_index("blk")
    every_item = jnp.arange(item_count, dtype=jnp.int32)
    all_item_heads = every_item // row_parts
    item_heads = lax.dynamic_slice_in_dim(all_item_heads, seq_place * per_device, per_device)
    grid_q = queries.reshape(local_blocks, row_parts, part_rows, head_count, head_depth).transpose(
        1, 3, 0, 2, 4
    )
    grid_q = grid_q.reshape(row_parts, head_count, local_blocks * part_rows, head_depth)
    head_keys = keys.reshape(local_rows, head_count, head_depth).transpose(1, 0, 2)
    head_values = values.reshape(local_rows, head_count, head_depth).transpose(1, 0, 2)
    send_q = arrange_heads(grid_q)
    q_items = lax.all_to_all(send_q, "seq", split_axis=0, concat_axis=1, tiled=True)
    stride = 1
    grid_k = jnp.broadcast_to(head_keys[None], (row_parts, head_count, local_rows, head_depth))
    grid_v = jnp.broadcast_to(head_values[None], (row_parts, head_count, local_rows, head_depth))
    send_k = arrange_heads(grid_k)
    send_v = arrange_heads(grid_v)
    k_held, v_held = (
        lax.all_to_all(send_k, "seq", split_axis=0, concat_axis=1, tiled=True),
        lax.all_to_all(send_v, "seq", split_axis=0, concat_axis=1, tiled=True),
    )
    key_blocks = k_held.reshape(per_device, seq_devices * local_blocks, BLOCK, head_depth)
    blocked_value_rows = v_held.reshape(per_device, seq_devices * local_blocks, BLOCK, head_depth)
    item_slot = jnp.arange(per_device, dtype=jnp.int32) // stride
    item_class = jnp.take(dense_class, item_heads)
    item_kept = jnp.take(kept, item_heads, axis=0)
    source_index = jnp.arange(seq_devices, dtype=jnp.int32)
    block_index = jnp.arange(local_blocks, dtype=jnp.int32)
    span_index = jnp.arange(span_count, dtype=jnp.int32)
    all_ids = (
        (source_index[None, :, None] * span_count + span_index[:, None, None]) * local_blocks
        + block_index[None, None, :]
    ).reshape(-1)
    all_kept = jnp.take(item_kept, all_ids, axis=1)
    span_ids = lax.dynamic_slice_in_dim(all_kept, blk_place * KEEP, KEEP, axis=2)
    q_all = lax.all_gather(q_items, "blk", axis=1, tiled=True)
    query_rows = q_all.reshape(
        per_device, span_count * seq_devices * local_blocks, part_rows, head_depth
    )

    def one_item(operands):
        rows_item, ids_item, class_item, slot_item = operands
        keys_item = lax.dynamic_index_in_dim(key_blocks, slot_item, 0, keepdims=False)
        values_item = lax.dynamic_index_in_dim(blocked_value_rows, slot_item, 0, keepdims=False)
        return lax.cond(
            class_item == 1,
            lambda: attend_blocks(rows_item, keys_item, values_item, ids_item, KEEP),
            lambda: attend_blocks(rows_item, keys_item, values_item, ids_item, LIGHT),
        )

    partial_out, maxima, totals = lax.map(
        one_item,
        (
            query_rows,
            span_ids // (local_blocks * span_count) * local_blocks + span_ids % local_blocks,
            item_class,
            item_slot,
        ),
    )
    own_blocks = seq_devices * local_blocks
    shaped_out = partial_out.reshape(per_device, span_count, own_blocks, part_rows, head_depth)
    shaped_max = maxima.reshape(per_device, span_count, own_blocks, part_rows)
    shaped_total = totals.reshape(per_device, span_count, own_blocks, part_rows)
    got_out, got_max, got_total = (
        lax.all_to_all(shaped_out, "blk", split_axis=1, concat_axis=1, tiled=True),
        lax.all_to_all(shaped_max, "blk", split_axis=1, concat_axis=1, tiled=True),
        lax.all_to_all(shaped_total, "blk", split_axis=1, concat_axis=1, tiled=True),
    )
    attended_items = combine_spans(got_out, got_max, got_total, 1)
    attended_items = attended_items.reshape(
        per_device, seq_devices * local_blocks * part_rows, head_depth
    )
    returned = lax.all_to_all(attended_items, "seq", split_axis=1, concat_axis=0, tiled=True)
    grid_out = returned.reshape(head_count, row_parts, local_blocks, part_rows, head_depth)
    grid_out = jnp.swapaxes(grid_out, 0, 1)
    return grid_out.transpose(2, 0, 3, 1, 4).reshape(local_rows, head_count * head_depth)


def own_place(axes):
    place = 0
    for axis in axes:
        place = place * lax.axis_size(axis) + lax.axis_index(axis)
    return place


def each_light_block(kept_ref, block):
    return [
        kept_ref[block, span * KEEP + slot]
        for span in range(kept_ref.shape[1] // KEEP)
        for slot in range(LIGHT)
    ]


def pack_kernel(*refs):
    sources, out_ref, sems = refs[:-2], refs[-2], refs[-1]
    copies = []
    for head in range(out_ref.shape[0]):
        for place, source in enumerate(sources):
            copies.append(
                pltpu.make_async_copy(
                    source.at[:, head * HD : (head + 1) * HD],
                    out_ref.at[head, place],
                    sems.at[head, place],
                )
            )
    for copy in copies:
        copy.start()
    for copy in copies:
        copy.wait()


def pack_heads(*sources):
    count = len(sources)
    rows = sources[0].shape[0]
    return pl.pallas_call(
        pack_kernel,
        out_shape=jax.ShapeDtypeStruct((HEADS, count, rows, HD), jnp.bfloat16),
        in_specs=[pl.BlockSpec(memory_space=pltpu.HBM)] * count,
        out_specs=pl.BlockSpec(memory_space=pl.ANY),
        scratch_shapes=[pltpu.SemaphoreType.DMA((HEADS, count))],
        compiler_params=pltpu.CompilerParams(vmem_limit_bytes=59 * 1024 * 1024),
        name="pack_heads",
    )(*sources)


def unpack_kernel(held_ref, out_ref, sems):
    copies = [
        pltpu.make_async_copy(
            held_ref.at[head], out_ref.at[:, head * HD : (head + 1) * HD], sems.at[head]
        )
        for head in range(held_ref.shape[0])
    ]
    for copy in copies:
        copy.start()
    for copy in copies:
        copy.wait()


def unpack_heads(held):
    heads, rows, depth = held.shape
    return pl.pallas_call(
        unpack_kernel,
        out_shape=jax.ShapeDtypeStruct((rows, heads * depth), jnp.bfloat16),
        in_specs=[pl.BlockSpec(memory_space=pl.ANY)],
        out_specs=pl.BlockSpec(memory_space=pltpu.HBM),
        scratch_shapes=[pltpu.SemaphoreType.DMA((heads,))],
        compiler_params=pltpu.CompilerParams(vmem_limit_bytes=4 * 1024 * 1024),
        name="unpack_heads",
    )(held)


def pipelined(count, score, finish):
    score(0, 0)

    def step(j, carry):
        score(2 * j + 1, 1)
        finish(2 * j, 0)
        score(2 * j + 2, 0)
        finish(2 * j + 1, 1)
        return carry

    lax.fori_loop(0, count // 2 - 1, step, 0)
    score(count - 1, 1)
    finish(count - 2, 0)
    finish(count - 1, 1)


def attend_kernel(axes, kept_hbm, class_ref, qkv_ref, out_ref, kept_ref, v_all, logits_a, logits_b, sem):
    logits_slots = (logits_a, logits_b)
    block_count = qkv_ref.shape[0]
    me = own_place(axes)
    exponent_scale = math.log2(math.e) / math.sqrt(HD)
    kept_copy = pltpu.make_async_copy(kept_hbm.at[me], kept_ref, sem)
    kept_copy.start()
    v_all[:, :, :HD] = qkv_ref[:, 2]
    v_all[:, :, HD:] = jnp.ones((block_count, BLOCK, HD), jnp.bfloat16)
    kept_copy.wait()

    def scores(query_rows, key_rows):
        return lax.dot_general(
            query_rows, key_rows, (((1,), (1,)), ((), ())), preferred_element_type=jnp.float32
        )

    def weigh(logits):
        largest = jnp.max(logits, axis=-1, keepdims=True)
        return jnp.exp2((logits - largest) * exponent_scale).astype(jnp.bfloat16)

    def normalized(summed):
        return (summed[:, :HD] / summed[:, HD:]).astype(jnp.bfloat16)

    @pl.when(class_ref[me] == 1)
    def _():
        group = 2

        def score(i, slot):
            query_rows = qkv_ref[pl.ds(group * i, group), 0].reshape(group * BLOCK, HD)
            key_rows = qkv_ref[:, 1].reshape(block_count * BLOCK, HD)
            logits_slots[slot][...] = scores(query_rows, key_rows)

        def finish(i, slot):
            value_rows = v_all[...].reshape(block_count * BLOCK, 2 * HD)
            weights = weigh(logits_slots[slot][...])
            out = normalized(jnp.dot(weights, value_rows, preferred_element_type=jnp.float32))
            out_ref[pl.ds(group * i, group)] = out.reshape(group, BLOCK, HD)

        pipelined(block_count // group, score, finish)

    @pl.when(class_ref[me] != 1)
    def _():
        group = 2

        def block_pairs(block):
            kept_blocks = each_light_block(kept_ref, block)
            return list(zip(kept_blocks[::2], kept_blocks[1::2]))

        def score(i, slot):
            for member in range(group):
                block = group * i + member
                rows = slice(member * BLOCK, (member + 1) * BLOCK)
                for place, (one, other) in enumerate(block_pairs(block)):
                    key_rows = jnp.concatenate([qkv_ref[one, 1], qkv_ref[other, 1]], axis=0)
                    columns = slice(place * 2 * BLOCK, (place + 1) * 2 * BLOCK)
                    logits_slots[slot][rows, columns] = scores(qkv_ref[block, 0], key_rows)

        def finish(i, slot):
            for member in range(group):
                block = group * i + member
                rows = slice(member * BLOCK, (member + 1) * BLOCK)
                pairs = block_pairs(block)
                weights = weigh(logits_slots[slot][rows, : 2 * BLOCK * len(pairs)])
                summed = jnp.zeros((BLOCK, 2 * HD), jnp.float32)
                for place, (one, other) in enumerate(pairs):
                    value_rows = jnp.concatenate([v_all[one], v_all[other]], axis=0)
                    columns = slice(place * 2 * BLOCK, (place + 1) * 2 * BLOCK)
                    summed += jnp.dot(
                        weights[:, columns], value_rows, preferred_element_type=jnp.float32
                    )
                out_ref[block] = normalized(summed)

        pipelined(block_count // group, score, finish)


def heads_by_device(queries, keys, values, kept, dense_class):
    axes = ("seq", "blk")
    block_count = kept.shape[1]
    in_vmem = pl.BlockSpec(memory_space=pltpu.VMEM)

    def exchange(send):
        return lax.all_to_all(send, axes, split_axis=0, concat_axis=0, tiled=True)

    held = exchange(pack_heads(queries, keys, values))
    attended = pl.pallas_call(
        lambda *refs: attend_kernel(axes, *refs),
        out_shape=jax.ShapeDtypeStruct((block_count, BLOCK, HD), jnp.bfloat16),
        in_specs=[
            pl.BlockSpec(memory_space=pl.ANY),
            pl.BlockSpec(memory_space=pltpu.SMEM),
            in_vmem,
        ],
        out_specs=in_vmem,
        scratch_shapes=[
            pltpu.SMEM(kept.shape[1:], jnp.int32),
            pltpu.VMEM((block_count, BLOCK, 2 * HD), jnp.bfloat16),
            pltpu.VMEM((2 * BLOCK, block_count * BLOCK), jnp.float32),
            pltpu.VMEM((2 * BLOCK, block_count * BLOCK), jnp.float32),
            pltpu.SemaphoreType.DMA,
        ],
        compiler_params=pltpu.CompilerParams(vmem_limit_bytes=32 * 1024 * 1024),
        name="attend_head",
    )(kept, dense_class, held)
    return unpack_heads(exchange(attended))


def shards(queries, keys, values, kept, dense_class):
    devices = lax.axis_size("seq") * lax.axis_size("blk")
    one_head_each = devices == HEADS
    one_block_each = queries.shape[0] == BLOCK
    every_block_kept = kept.shape[1] == kept.shape[2]
    if one_head_each and one_block_each and every_block_kept:
        return heads_by_device(queries, keys, values, kept, dense_class)
    return spans_by_device(queries, keys, values, kept, dense_class)


def solution(mesh):
    return jax.shard_map(
        shards,
        mesh=mesh,
        in_specs=(
            P(("clip", "seq", "blk"), None),
            P(("clip", "seq", "blk"), None),
            P(("clip", "seq", "blk"), None),
            P(),
            P(),
        ),
        out_specs=P(("clip", "seq", "blk"), None),
        check_vma=False,
    )
```

```python
import math

import jax
import jax.numpy as jnp
from jax import lax
from jax.experimental import pallas as pl
from jax.experimental.pallas import tpu as pltpu
from jax.sharding import PartitionSpec as P

HEADS = 16
HD = 128
BLOCK = 128
KEEP = 4
LIGHT = 2


def combine_spans(partial_out, maxima, totals, along):
    largest = jnp.max(maxima, axis=along, keepdims=True)
    factor = jnp.exp(maxima - largest)
    numerator = jnp.sum(factor[..., None] * partial_out, axis=along)
    denominator = jnp.sum(factor * totals, axis=along)
    return (numerator / denominator[..., None]).astype(jnp.bfloat16)


def attend_blocks(query_rows, key_blocks, blocked_value_rows, local_ids, slot_count):
    query_blocks, part_rows, head_depth = query_rows.shape
    group_size = query_blocks
    while group_size * part_rows > 512 and group_size % 2 == 0:
        group_size = group_size // 2
    logit_scale_factor = 1.0 / math.sqrt(head_depth)
    block_rows = key_blocks.shape[1]

    def one_group(operands):
        queries_group, ids_group = operands
        collected_key_blocks = key_blocks[ids_group].reshape(
            group_size, slot_count * block_rows, head_depth
        )
        gathered_v = blocked_value_rows[ids_group].reshape(
            group_size, slot_count * block_rows, head_depth
        )
        attention_logits = (
            jnp.einsum(
                "gpd,gkd->gpk",
                queries_group,
                collected_key_blocks,
                preferred_element_type=jnp.float32,
            )
            * logit_scale_factor
        )
        maxima = jnp.max(attention_logits, axis=-1)
        weights = jnp.exp(attention_logits - maxima[..., None])
        totals = jnp.sum(weights, axis=-1)
        partial_out = jnp.einsum(
            "gpk,gkd->gpd",
            weights.astype(jnp.bfloat16),
            gathered_v,
            preferred_element_type=jnp.float32,
        )
        return (partial_out, maxima, totals)

    grouped_q = query_rows.reshape(query_blocks // group_size, group_size, part_rows, head_depth)
    grouped_ids = local_ids[:, :slot_count].reshape(
        query_blocks // group_size, group_size, slot_count
    )
    partial_out, maxima, totals = lax.map(one_group, (grouped_q, grouped_ids))
    return (
        partial_out.reshape(query_blocks, part_rows, head_depth),
        maxima.reshape(query_blocks, part_rows),
        totals.reshape(query_blocks, part_rows),
    )


def arrange_heads(stacked):
    swapped = jnp.swapaxes(stacked, 0, 1)
    return swapped.reshape((-1,) + stacked.shape[2:])


def spans_by_device(queries, keys, values, kept, dense_class):
    seq_devices = lax.axis_size("seq")
    span_count = lax.axis_size("blk")
    local_rows = queries.shape[0]
    head_count = HEADS
    head_depth = HD
    local_blocks = local_rows // BLOCK
    row_parts = max(1, 2 * seq_devices // head_count)
    part_rows = BLOCK // row_parts
    item_count = head_count * row_parts
    per_device = item_count // seq_devices
    seq_place = lax.axis_index("seq")
    blk_place = lax.axis_index("blk")
    every_item = jnp.arange(item_count, dtype=jnp.int32)
    all_item_heads = every_item // row_parts
    item_heads = lax.dynamic_slice_in_dim(all_item_heads, seq_place * per_device, per_device)
    grid_q = queries.reshape(local_blocks, row_parts, part_rows, head_count, head_depth).transpose(
        1, 3, 0, 2, 4
    )
    grid_q = grid_q.reshape(row_parts, head_count, local_blocks * part_rows, head_depth)
    head_keys = keys.reshape(local_rows, head_count, head_depth).transpose(1, 0, 2)
    head_values = values.reshape(local_rows, head_count, head_depth).transpose(1, 0, 2)
    send_q = arrange_heads(grid_q)
    q_items = lax.all_to_all(send_q, "seq", split_axis=0, concat_axis=1, tiled=True)
    stride = 1
    grid_k = jnp.broadcast_to(head_keys[None], (row_parts, head_count, local_rows, head_depth))
    grid_v = jnp.broadcast_to(head_values[None], (row_parts, head_count, local_rows, head_depth))
    send_k = arrange_heads(grid_k)
    send_v = arrange_heads(grid_v)
    k_held, v_held = (
        lax.all_to_all(send_k, "seq", split_axis=0, concat_axis=1, tiled=True),
        lax.all_to_all(send_v, "seq", split_axis=0, concat_axis=1, tiled=True),
    )
    key_blocks = k_held.reshape(per_device, seq_devices * local_blocks, BLOCK, head_depth)
    blocked_value_rows = v_held.reshape(per_device, seq_devices * local_blocks, BLOCK, head_depth)
    item_slot = jnp.arange(per_device, dtype=jnp.int32) // stride
    item_class = jnp.take(dense_class, item_heads)
    item_kept = jnp.take(kept, item_heads, axis=0)
    source_index = jnp.arange(seq_devices, dtype=jnp.int32)
    block_index = jnp.arange(local_blocks, dtype=jnp.int32)
    span_index = jnp.arange(span_count, dtype=jnp.int32)
    all_ids = (
        (source_index[None, :, None] * span_count + span_index[:, None, None]) * local_blocks
        + block_index[None, None, :]
    ).reshape(-1)
    all_kept = jnp.take(item_kept, all_ids, axis=1)
    span_ids = lax.dynamic_slice_in_dim(all_kept, blk_place * KEEP, KEEP, axis=2)
    q_all = lax.all_gather(q_items, "blk", axis=1, tiled=True)
    query_rows = q_all.reshape(
        per_device, span_count * seq_devices * local_blocks, part_rows, head_depth
    )

    def one_item(operands):
        rows_item, ids_item, class_item, slot_item = operands
        keys_item = lax.dynamic_index_in_dim(key_blocks, slot_item, 0, keepdims=False)
        values_item = lax.dynamic_index_in_dim(blocked_value_rows, slot_item, 0, keepdims=False)
        return lax.cond(
            class_item == 1,
            lambda: attend_blocks(rows_item, keys_item, values_item, ids_item, KEEP),
            lambda: attend_blocks(rows_item, keys_item, values_item, ids_item, LIGHT),
        )

    partial_out, maxima, totals = lax.map(
        one_item,
        (
            query_rows,
            span_ids // (local_blocks * span_count) * local_blocks + span_ids % local_blocks,
            item_class,
            item_slot,
        ),
    )
    own_blocks = seq_devices * local_blocks
    shaped_out = partial_out.reshape(per_device, span_count, own_blocks, part_rows, head_depth)
    shaped_max = maxima.reshape(per_device, span_count, own_blocks, part_rows)
    shaped_total = totals.reshape(per_device, span_count, own_blocks, part_rows)
    got_out, got_max, got_total = (
        lax.all_to_all(shaped_out, "blk", split_axis=1, concat_axis=1, tiled=True),
        lax.all_to_all(shaped_max, "blk", split_axis=1, concat_axis=1, tiled=True),
        lax.all_to_all(shaped_total, "blk", split_axis=1, concat_axis=1, tiled=True),
    )
    attended_items = combine_spans(got_out, got_max, got_total, 1)
    attended_items = attended_items.reshape(
        per_device, seq_devices * local_blocks * part_rows, head_depth
    )
    returned = lax.all_to_all(attended_items, "seq", split_axis=1, concat_axis=0, tiled=True)
    grid_out = returned.reshape(head_count, row_parts, local_blocks, part_rows, head_depth)
    grid_out = jnp.swapaxes(grid_out, 0, 1)
    return grid_out.transpose(2, 0, 3, 1, 4).reshape(local_rows, head_count * head_depth)


def own_place(axes):
    place = 0
    for axis in axes:
        place = place * lax.axis_size(axis) + lax.axis_index(axis)
    return place


def each_light_place(kept_ref, place, seq_devices, span_count):
    block = place % seq_devices * span_count + place // seq_devices
    kept_blocks = [
        kept_ref[block, span * KEEP + slot] for span in range(span_count) for slot in range(LIGHT)
    ]
    return [kept % span_count * seq_devices + kept // span_count for kept in kept_blocks]


def pack_kernel(*refs):
    sources, (out_ref, staged, in_sems, out_sems) = refs[:-4], refs[-4:]
    heads, count = staged.shape[:2]
    arrivals, departures = [], []
    for head in range(heads):
        for place in range(count):
            arrivals.append(
                pltpu.make_async_copy(
                    sources[place].at[:, head * HD : (head + 1) * HD],
                    staged.at[head, place],
                    in_sems.at[head, place],
                )
            )
            departures.append(
                pltpu.make_async_copy(
                    staged.at[head, place], out_ref.at[head, place], out_sems.at[head, place]
                )
            )
    for copy in arrivals:
        copy.start()
    for arrival, departure in zip(arrivals, departures):
        arrival.wait()
        departure.start()
    for copy in departures:
        copy.wait()


def pack_heads(*sources):
    count = len(sources)
    rows = sources[0].shape[0]
    return pl.pallas_call(
        pack_kernel,
        out_shape=jax.ShapeDtypeStruct((HEADS, count, rows, HD), jnp.bfloat16),
        in_specs=[pl.BlockSpec(memory_space=pltpu.HBM)] * count,
        out_specs=pl.BlockSpec(memory_space=pl.ANY),
        scratch_shapes=[
            pltpu.VMEM((HEADS, count, rows, HD), jnp.bfloat16),
            pltpu.SemaphoreType.DMA((HEADS, count)),
            pltpu.SemaphoreType.DMA((HEADS, count)),
        ],
        compiler_params=pltpu.CompilerParams(vmem_limit_bytes=59 * 1024 * 1024),
        name="pack_heads",
    )(*sources)


def unpack_kernel(held_ref, out_ref, sems):
    copies = [
        pltpu.make_async_copy(
            held_ref.at[head], out_ref.at[:, head * HD : (head + 1) * HD], sems.at[head]
        )
        for head in range(held_ref.shape[0])
    ]
    for copy in copies:
        copy.start()
    for copy in copies:
        copy.wait()


def unpack_heads(held):
    heads, rows, depth = held.shape
    return pl.pallas_call(
        unpack_kernel,
        out_shape=jax.ShapeDtypeStruct((rows, heads * depth), jnp.bfloat16),
        in_specs=[pl.BlockSpec(memory_space=pl.ANY)],
        out_specs=pl.BlockSpec(memory_space=pltpu.HBM),
        scratch_shapes=[pltpu.SemaphoreType.DMA((heads,))],
        compiler_params=pltpu.CompilerParams(vmem_limit_bytes=4 * 1024 * 1024),
        name="unpack_heads",
    )(held)


def pipelined(count, score, finish):
    score(0, 0)

    def step(j, carry):
        score(2 * j + 1, 1)
        finish(2 * j, 0)
        score(2 * j + 2, 0)
        finish(2 * j + 1, 1)
        return carry

    lax.fori_loop(0, count // 2 - 1, step, 0)
    score(count - 1, 1)
    finish(count - 2, 0)
    finish(count - 1, 1)


def attend_kernel(axes, kept_hbm, class_ref, qkv_ref, out_ref, kept_ref, v_all, logits_a, logits_b, sem):
    logits_slots = (logits_a, logits_b)
    block_count = qkv_ref.shape[0]
    seq_devices, span_count = lax.axis_size("seq"), lax.axis_size("blk")
    me = own_place(axes)
    exponent_scale = math.log2(math.e) / math.sqrt(HD)
    kept_copy = pltpu.make_async_copy(kept_hbm.at[me], kept_ref, sem)
    kept_copy.start()
    v_all[:, :, :HD] = qkv_ref[:, 2]
    v_all[:, :, HD:] = jnp.ones((block_count, BLOCK, HD), jnp.bfloat16)
    kept_copy.wait()

    def scores(query_rows, key_rows):
        return lax.dot_general(
            query_rows, key_rows, (((1,), (1,)), ((), ())), preferred_element_type=jnp.float32
        )

    def weigh(logits):
        largest = jnp.max(logits, axis=-1, keepdims=True)
        return jnp.exp2((logits - largest) * exponent_scale).astype(jnp.bfloat16)

    def normalized(summed):
        return (summed[:, :HD] / summed[:, HD:]).astype(jnp.bfloat16)

    @pl.when(class_ref[me] == 1)
    def _():
        group = 4

        def score(i, slot):
            query_rows = qkv_ref[pl.ds(group * i, group), 0].reshape(group * BLOCK, HD)
            key_rows = qkv_ref[:, 1].reshape(block_count * BLOCK, HD)
            logits_slots[slot][...] = scores(query_rows, key_rows)

        def finish(i, slot):
            value_rows = v_all[...].reshape(block_count * BLOCK, 2 * HD)
            weights = weigh(logits_slots[slot][...])
            out = normalized(jnp.dot(weights, value_rows, preferred_element_type=jnp.float32))
            out_ref[pl.ds(group * i, group)] = out.reshape(group, BLOCK, HD)

        pipelined(block_count // group, score, finish)

    @pl.when(class_ref[me] != 1)
    def _():
        group = 2

        def block_pairs(place):
            kept_places = each_light_place(kept_ref, place, seq_devices, span_count)
            return list(zip(kept_places[::2], kept_places[1::2]))

        def score(i, slot):
            for member in range(group):
                block = group * i + member
                rows = slice(member * BLOCK, (member + 1) * BLOCK)
                for place, (one, other) in enumerate(block_pairs(block)):
                    key_rows = jnp.concatenate([qkv_ref[one, 1], qkv_ref[other, 1]], axis=0)
                    columns = slice(place * 2 * BLOCK, (place + 1) * 2 * BLOCK)
                    logits_slots[slot][rows, columns] = scores(qkv_ref[block, 0], key_rows)

        def finish(i, slot):
            for member in range(group):
                block = group * i + member
                rows = slice(member * BLOCK, (member + 1) * BLOCK)
                pairs = block_pairs(block)
                weights = weigh(logits_slots[slot][rows, : 2 * BLOCK * len(pairs)])
                summed = jnp.zeros((BLOCK, 2 * HD), jnp.float32)
                for place, (one, other) in enumerate(pairs):
                    value_rows = jnp.concatenate([v_all[one], v_all[other]], axis=0)
                    columns = slice(place * 2 * BLOCK, (place + 1) * 2 * BLOCK)
                    summed += jnp.dot(
                        weights[:, columns], value_rows, preferred_element_type=jnp.float32
                    )
                out_ref[block] = normalized(summed)

        pipelined(block_count // group, score, finish)


def heads_by_device(queries, keys, values, kept, dense_class):
    axes = ("blk", "seq")
    block_count = kept.shape[1]
    in_vmem = pl.BlockSpec(memory_space=pltpu.VMEM)

    def exchange(send):
        return lax.all_to_all(send, axes, split_axis=0, concat_axis=0, tiled=True)

    held = exchange(pack_heads(queries, keys, values))
    attended = pl.pallas_call(
        lambda *refs: attend_kernel(axes, *refs),
        out_shape=jax.ShapeDtypeStruct((block_count, BLOCK, HD), jnp.bfloat16),
        in_specs=[
            pl.BlockSpec(memory_space=pl.ANY),
            pl.BlockSpec(memory_space=pltpu.SMEM),
            in_vmem,
        ],
        out_specs=in_vmem,
        scratch_shapes=[
            pltpu.SMEM(kept.shape[1:], jnp.int32),
            pltpu.VMEM((block_count, BLOCK, 2 * HD), jnp.bfloat16),
            pltpu.VMEM((4 * BLOCK, block_count * BLOCK), jnp.float32),
            pltpu.VMEM((4 * BLOCK, block_count * BLOCK), jnp.float32),
            pltpu.SemaphoreType.DMA,
        ],
        compiler_params=pltpu.CompilerParams(vmem_limit_bytes=32 * 1024 * 1024),
        name="attend_head",
    )(kept, dense_class, held)
    return unpack_heads(exchange(attended))


def shards(queries, keys, values, kept, dense_class):
    devices = lax.axis_size("seq") * lax.axis_size("blk")
    one_head_each = devices == HEADS
    one_block_each = queries.shape[0] == BLOCK
    every_block_kept = kept.shape[1] == kept.shape[2]
    if one_head_each and one_block_each and every_block_kept:
        return heads_by_device(queries, keys, values, kept, dense_class)
    return spans_by_device(queries, keys, values, kept, dense_class)


def solution(mesh):
    return jax.shard_map(
        shards,
        mesh=mesh,
        in_specs=(
            P(("clip", "seq", "blk"), None),
            P(("clip", "seq", "blk"), None),
            P(("clip", "seq", "blk"), None),
            P(),
            P(),
        ),
        out_specs=P(("clip", "seq", "blk"), None),
        check_vma=False,
    )
```

```python
import math

import jax
import jax.numpy as jnp
from jax import lax
from jax.experimental import pallas as pl
from jax.experimental.pallas import tpu as pltpu
from jax.sharding import PartitionSpec as P

HEADS = 16
HD = 128
BLOCK = 128
KEEP = 4
LIGHT = 2


def combine_spans(partial_out, maxima, totals, along):
    largest = jnp.max(maxima, axis=along, keepdims=True)
    factor = jnp.exp(maxima - largest)
    numerator = jnp.sum(factor[..., None] * partial_out, axis=along)
    denominator = jnp.sum(factor * totals, axis=along)
    return (numerator / denominator[..., None]).astype(jnp.bfloat16)


def attend_blocks(query_rows, key_blocks, blocked_value_rows, local_ids, slot_count):
    query_blocks, part_rows, head_depth = query_rows.shape
    group_size = query_blocks
    while group_size * part_rows > 512 and group_size % 2 == 0:
        group_size = group_size // 2
    logit_scale_factor = 1.0 / math.sqrt(head_depth)
    block_rows = key_blocks.shape[1]

    def one_group(operands):
        queries_group, ids_group = operands
        collected_key_blocks = key_blocks[ids_group].reshape(
            group_size, slot_count * block_rows, head_depth
        )
        gathered_v = blocked_value_rows[ids_group].reshape(
            group_size, slot_count * block_rows, head_depth
        )
        attention_logits = (
            jnp.einsum(
                "gpd,gkd->gpk",
                queries_group,
                collected_key_blocks,
                preferred_element_type=jnp.float32,
            )
            * logit_scale_factor
        )
        maxima = jnp.max(attention_logits, axis=-1)
        weights = jnp.exp(attention_logits - maxima[..., None])
        totals = jnp.sum(weights, axis=-1)
        partial_out = jnp.einsum(
            "gpk,gkd->gpd",
            weights.astype(jnp.bfloat16),
            gathered_v,
            preferred_element_type=jnp.float32,
        )
        return (partial_out, maxima, totals)

    grouped_q = query_rows.reshape(query_blocks // group_size, group_size, part_rows, head_depth)
    grouped_ids = local_ids[:, :slot_count].reshape(
        query_blocks // group_size, group_size, slot_count
    )
    partial_out, maxima, totals = lax.map(one_group, (grouped_q, grouped_ids))
    return (
        partial_out.reshape(query_blocks, part_rows, head_depth),
        maxima.reshape(query_blocks, part_rows),
        totals.reshape(query_blocks, part_rows),
    )


def arrange_heads(stacked):
    swapped = jnp.swapaxes(stacked, 0, 1)
    return swapped.reshape((-1,) + stacked.shape[2:])


def spans_by_device(queries, keys, values, kept, dense_class):
    seq_devices = lax.axis_size("seq")
    span_count = lax.axis_size("blk")
    local_rows = queries.shape[0]
    head_count = HEADS
    head_depth = HD
    local_blocks = local_rows // BLOCK
    row_parts = max(1, 2 * seq_devices // head_count)
    part_rows = BLOCK // row_parts
    item_count = head_count * row_parts
    per_device = item_count // seq_devices
    seq_place = lax.axis_index("seq")
    blk_place = lax.axis_index("blk")
    every_item = jnp.arange(item_count, dtype=jnp.int32)
    all_item_heads = every_item // row_parts
    item_heads = lax.dynamic_slice_in_dim(all_item_heads, seq_place * per_device, per_device)
    grid_q = queries.reshape(local_blocks, row_parts, part_rows, head_count, head_depth).transpose(
        1, 3, 0, 2, 4
    )
    grid_q = grid_q.reshape(row_parts, head_count, local_blocks * part_rows, head_depth)
    head_keys = keys.reshape(local_rows, head_count, head_depth).transpose(1, 0, 2)
    head_values = values.reshape(local_rows, head_count, head_depth).transpose(1, 0, 2)
    send_q = arrange_heads(grid_q)
    q_items = lax.all_to_all(send_q, "seq", split_axis=0, concat_axis=1, tiled=True)
    stride = 1
    grid_k = jnp.broadcast_to(head_keys[None], (row_parts, head_count, local_rows, head_depth))
    grid_v = jnp.broadcast_to(head_values[None], (row_parts, head_count, local_rows, head_depth))
    send_k = arrange_heads(grid_k)
    send_v = arrange_heads(grid_v)
    k_held, v_held = (
        lax.all_to_all(send_k, "seq", split_axis=0, concat_axis=1, tiled=True),
        lax.all_to_all(send_v, "seq", split_axis=0, concat_axis=1, tiled=True),
    )
    key_blocks = k_held.reshape(per_device, seq_devices * local_blocks, BLOCK, head_depth)
    blocked_value_rows = v_held.reshape(per_device, seq_devices * local_blocks, BLOCK, head_depth)
    item_slot = jnp.arange(per_device, dtype=jnp.int32) // stride
    item_class = jnp.take(dense_class, item_heads)
    item_kept = jnp.take(kept, item_heads, axis=0)
    source_index = jnp.arange(seq_devices, dtype=jnp.int32)
    block_index = jnp.arange(local_blocks, dtype=jnp.int32)
    span_index = jnp.arange(span_count, dtype=jnp.int32)
    all_ids = (
        (source_index[None, :, None] * span_count + span_index[:, None, None]) * local_blocks
        + block_index[None, None, :]
    ).reshape(-1)
    all_kept = jnp.take(item_kept, all_ids, axis=1)
    span_ids = lax.dynamic_slice_in_dim(all_kept, blk_place * KEEP, KEEP, axis=2)
    q_all = lax.all_gather(q_items, "blk", axis=1, tiled=True)
    query_rows = q_all.reshape(
        per_device, span_count * seq_devices * local_blocks, part_rows, head_depth
    )

    def one_item(operands):
        rows_item, ids_item, class_item, slot_item = operands
        keys_item = lax.dynamic_index_in_dim(key_blocks, slot_item, 0, keepdims=False)
        values_item = lax.dynamic_index_in_dim(blocked_value_rows, slot_item, 0, keepdims=False)
        return lax.cond(
            class_item == 1,
            lambda: attend_blocks(rows_item, keys_item, values_item, ids_item, KEEP),
            lambda: attend_blocks(rows_item, keys_item, values_item, ids_item, LIGHT),
        )

    partial_out, maxima, totals = lax.map(
        one_item,
        (
            query_rows,
            span_ids // (local_blocks * span_count) * local_blocks + span_ids % local_blocks,
            item_class,
            item_slot,
        ),
    )
    own_blocks = seq_devices * local_blocks
    shaped_out = partial_out.reshape(per_device, span_count, own_blocks, part_rows, head_depth)
    shaped_max = maxima.reshape(per_device, span_count, own_blocks, part_rows)
    shaped_total = totals.reshape(per_device, span_count, own_blocks, part_rows)
    got_out, got_max, got_total = (
        lax.all_to_all(shaped_out, "blk", split_axis=1, concat_axis=1, tiled=True),
        lax.all_to_all(shaped_max, "blk", split_axis=1, concat_axis=1, tiled=True),
        lax.all_to_all(shaped_total, "blk", split_axis=1, concat_axis=1, tiled=True),
    )
    attended_items = combine_spans(got_out, got_max, got_total, 1)
    attended_items = attended_items.reshape(
        per_device, seq_devices * local_blocks * part_rows, head_depth
    )
    returned = lax.all_to_all(attended_items, "seq", split_axis=1, concat_axis=0, tiled=True)
    grid_out = returned.reshape(head_count, row_parts, local_blocks, part_rows, head_depth)
    grid_out = jnp.swapaxes(grid_out, 0, 1)
    return grid_out.transpose(2, 0, 3, 1, 4).reshape(local_rows, head_count * head_depth)


def own_place(axes):
    place = 0
    for axis in axes:
        place = place * lax.axis_size(axis) + lax.axis_index(axis)
    return place


def each_light_block(kept_ref, block):
    return [
        kept_ref[block, span * KEEP + slot]
        for span in range(kept_ref.shape[1] // KEEP)
        for slot in range(LIGHT)
    ]


def pack_kernel(*refs):
    sources, (out_ref, landed, staged, in_sems, out_sems) = refs[:-5], refs[-5:]
    heads = out_ref.shape[0]
    count, rows = landed.shape[:2]
    pieces = in_sems.shape[1]
    piece_rows = rows // pieces
    arrivals = [
        [
            pltpu.make_async_copy(
                source.at[pl.ds(piece * piece_rows, piece_rows), :],
                landed.at[place, pl.ds(piece * piece_rows, piece_rows), :],
                in_sems.at[place, piece],
            )
            for piece in range(pieces)
        ]
        for place, source in enumerate(sources)
    ]
    departures = [
        pltpu.make_async_copy(staged.at[place], out_ref.at[:, place], out_sems.at[place])
        for place in range(count)
    ]
    for copies in arrivals:
        for copy in copies:
            copy.start()
    for place in range(count):
        for copy in arrivals[place]:
            copy.wait()
        for head in range(heads):
            staged[place, head] = landed[place, :, head * HD : (head + 1) * HD]
        departures[place].start()
    for copy in departures:
        copy.wait()


def pack_heads(*sources):
    count = len(sources)
    rows = sources[0].shape[0]
    pieces = 4
    return pl.pallas_call(
        pack_kernel,
        out_shape=jax.ShapeDtypeStruct((HEADS, count, rows, HD), jnp.bfloat16),
        in_specs=[pl.BlockSpec(memory_space=pltpu.HBM)] * count,
        out_specs=pl.BlockSpec(memory_space=pl.ANY),
        scratch_shapes=[
            pltpu.VMEM((count, rows, HEADS * HD), jnp.bfloat16),
            pltpu.VMEM((count, HEADS, rows, HD), jnp.bfloat16),
            pltpu.SemaphoreType.DMA((count, pieces)),
            pltpu.SemaphoreType.DMA((count,)),
        ],
        compiler_params=pltpu.CompilerParams(vmem_limit_bytes=59 * 1024 * 1024),
        name="pack_heads",
    )(*sources)


def unpack_kernel(held_ref, out_ref, sems):
    copies = [
        pltpu.make_async_copy(
            held_ref.at[head], out_ref.at[:, head * HD : (head + 1) * HD], sems.at[head]
        )
        for head in range(held_ref.shape[0])
    ]
    for copy in copies:
        copy.start()
    for copy in copies:
        copy.wait()


def unpack_heads(held):
    heads, rows, depth = held.shape
    return pl.pallas_call(
        unpack_kernel,
        out_shape=jax.ShapeDtypeStruct((rows, heads * depth), jnp.bfloat16),
        in_specs=[pl.BlockSpec(memory_space=pl.ANY)],
        out_specs=pl.BlockSpec(memory_space=pltpu.HBM),
        scratch_shapes=[pltpu.SemaphoreType.DMA((heads,))],
        compiler_params=pltpu.CompilerParams(vmem_limit_bytes=4 * 1024 * 1024),
        name="unpack_heads",
    )(held)


def pipelined(count, score, weigh, blend):
    score(0, 0)
    weigh(0, 0)
    score(1, 1)

    def step(j, carry):
        blend(2 * j, 0)
        weigh(2 * j + 1, 1)
        score(2 * j + 2, 0)
        blend(2 * j + 1, 1)
        weigh(2 * j + 2, 0)
        score(2 * j + 3, 1)
        return carry

    lax.fori_loop(0, count // 2 - 1, step, 0)
    blend(count - 2, 0)
    weigh(count - 1, 1)
    blend(count - 1, 1)


def attend_kernel(axes, kept_hbm, class_ref, qkv_ref, out_ref, *scratch):
    kept_ref, v_all, logits_a, logits_b, weights_a, weights_b, sem = scratch
    logits_slots = (logits_a, logits_b)
    weights_slots = (weights_a, weights_b)
    block_count = qkv_ref.shape[0]
    me = own_place(axes)
    group = 2
    exponent_scale = math.log2(math.e) / math.sqrt(HD)
    kept_copy = pltpu.make_async_copy(kept_hbm.at[me], kept_ref, sem)
    kept_copy.start()
    v_all[:, :, :HD] = qkv_ref[:, 2]
    v_all[:, :, HD:] = jnp.ones((block_count, BLOCK, HD), jnp.bfloat16)

    def scores(query_rows, key_rows):
        return lax.dot_general(
            query_rows, key_rows, (((1,), (1,)), ((), ())), preferred_element_type=jnp.float32
        )

    def weigh(columns, slot):
        logits = logits_slots[slot][:, :columns]
        largest = jnp.max(logits, axis=-1, keepdims=True)
        weights = jnp.exp2((logits - largest) * exponent_scale).astype(jnp.bfloat16)
        weights_slots[slot][:, :columns] = weights

    def normalized(summed):
        return (summed[:, :HD] / summed[:, HD:]).astype(jnp.bfloat16)

    @pl.when(class_ref[me] == 1)
    def _():
        def score(i, slot):
            query_rows = qkv_ref[pl.ds(group * i, group), 0].reshape(group * BLOCK, HD)
            key_rows = qkv_ref[:, 1].reshape(block_count * BLOCK, HD)
            logits_slots[slot][...] = scores(query_rows, key_rows)

        def blend(i, slot):
            value_rows = v_all[...].reshape(block_count * BLOCK, 2 * HD)
            out = normalized(
                jnp.dot(weights_slots[slot][...], value_rows, preferred_element_type=jnp.float32)
            )
            out_ref[pl.ds(group * i, group)] = out.reshape(group, BLOCK, HD)

        all_columns = block_count * BLOCK
        pipelined(block_count // group, score, lambda i, slot: weigh(all_columns, slot), blend)
        kept_copy.wait()

    @pl.when(class_ref[me] != 1)
    def _():
        kept_copy.wait()
        few_columns = block_count // KEEP * LIGHT * BLOCK

        def block_pairs(block):
            kept_blocks = each_light_block(kept_ref, block)
            return list(zip(kept_blocks[::2], kept_blocks[1::2]))

        def score(i, slot):
            for member in range(group):
                block = group * i + member
                rows = slice(member * BLOCK, (member + 1) * BLOCK)
                for place, (one, other) in enumerate(block_pairs(block)):
                    key_rows = jnp.concatenate([qkv_ref[one, 1], qkv_ref[other, 1]], axis=0)
                    columns = slice(place * 2 * BLOCK, (place + 1) * 2 * BLOCK)
                    logits_slots[slot][rows, columns] = scores(qkv_ref[block, 0], key_rows)

        def blend(i, slot):
            for member in range(group):
                block = group * i + member
                rows = slice(member * BLOCK, (member + 1) * BLOCK)
                summed = jnp.zeros((BLOCK, 2 * HD), jnp.float32)
                for place, (one, other) in enumerate(block_pairs(block)):
                    value_rows = jnp.concatenate([v_all[one], v_all[other]], axis=0)
                    columns = slice(place * 2 * BLOCK, (place + 1) * 2 * BLOCK)
                    weights = weights_slots[slot][rows, columns]
                    summed += jnp.dot(weights, value_rows, preferred_element_type=jnp.float32)
                out_ref[block] = normalized(summed)

        pipelined(block_count // group, score, lambda i, slot: weigh(few_columns, slot), blend)


def heads_by_device(queries, keys, values, kept, dense_class):
    axes = ("seq", "blk")
    block_count = kept.shape[1]
    in_vmem = pl.BlockSpec(memory_space=pltpu.VMEM)

    def exchange(send):
        return lax.all_to_all(send, axes, split_axis=0, concat_axis=0, tiled=True)

    held = exchange(pack_heads(queries, keys, values))
    attended = pl.pallas_call(
        lambda *refs: attend_kernel(axes, *refs),
        out_shape=jax.ShapeDtypeStruct((block_count, BLOCK, HD), jnp.bfloat16),
        in_specs=[
            pl.BlockSpec(memory_space=pl.ANY),
            pl.BlockSpec(memory_space=pltpu.SMEM),
            in_vmem,
        ],
        out_specs=in_vmem,
        scratch_shapes=[
            pltpu.SMEM(kept.shape[1:], jnp.int32),
            pltpu.VMEM((block_count, BLOCK, 2 * HD), jnp.bfloat16),
            pltpu.VMEM((2 * BLOCK, block_count * BLOCK), jnp.float32),
            pltpu.VMEM((2 * BLOCK, block_count * BLOCK), jnp.float32),
            pltpu.VMEM((2 * BLOCK, block_count * BLOCK), jnp.bfloat16),
            pltpu.VMEM((2 * BLOCK, block_count * BLOCK), jnp.bfloat16),
            pltpu.SemaphoreType.DMA,
        ],
        compiler_params=pltpu.CompilerParams(vmem_limit_bytes=32 * 1024 * 1024),
        name="attend_head",
    )(kept, dense_class, held)
    return unpack_heads(exchange(attended))


def shards(queries, keys, values, kept, dense_class):
    devices = lax.axis_size("seq") * lax.axis_size("blk")
    one_head_each = devices == HEADS
    one_block_each = queries.shape[0] == BLOCK
    every_block_kept = kept.shape[1] == kept.shape[2]
    if one_head_each and one_block_each and every_block_kept:
        return heads_by_device(queries, keys, values, kept, dense_class)
    return spans_by_device(queries, keys, values, kept, dense_class)


def solution(mesh):
    return jax.shard_map(
        shards,
        mesh=mesh,
        in_specs=(
            P(("clip", "seq", "blk"), None),
            P(("clip", "seq", "blk"), None),
            P(("clip", "seq", "blk"), None),
            P(),
            P(),
        ),
        out_specs=P(("clip", "seq", "blk"), None),
        check_vma=False,
    )
```

```python
import math

import jax
import jax.numpy as jnp
from jax import lax
from jax.experimental import pallas as pl
from jax.experimental.pallas import tpu as pltpu
from jax.sharding import PartitionSpec as P

HEADS = 16
HD = 128
BLOCK = 128
KEEP = 4
LIGHT = 2


def combine_spans(partial_out, maxima, totals, along):
    largest = jnp.max(maxima, axis=along, keepdims=True)
    factor = jnp.exp(maxima - largest)
    numerator = jnp.sum(factor[..., None] * partial_out, axis=along)
    denominator = jnp.sum(factor * totals, axis=along)
    return (numerator / denominator[..., None]).astype(jnp.bfloat16)


def attend_blocks(query_rows, key_blocks, blocked_value_rows, local_ids, slot_count):
    query_blocks, part_rows, head_depth = query_rows.shape
    group_size = query_blocks
    while group_size * part_rows > 512 and group_size % 2 == 0:
        group_size = group_size // 2
    logit_scale_factor = 1.0 / math.sqrt(head_depth)
    block_rows = key_blocks.shape[1]

    def one_group(operands):
        queries_group, ids_group = operands
        collected_key_blocks = key_blocks[ids_group].reshape(
            group_size, slot_count * block_rows, head_depth
        )
        gathered_v = blocked_value_rows[ids_group].reshape(
            group_size, slot_count * block_rows, head_depth
        )
        attention_logits = (
            jnp.einsum(
                "gpd,gkd->gpk",
                queries_group,
                collected_key_blocks,
                preferred_element_type=jnp.float32,
            )
            * logit_scale_factor
        )
        maxima = jnp.max(attention_logits, axis=-1)
        weights = jnp.exp(attention_logits - maxima[..., None])
        totals = jnp.sum(weights, axis=-1)
        partial_out = jnp.einsum(
            "gpk,gkd->gpd",
            weights.astype(jnp.bfloat16),
            gathered_v,
            preferred_element_type=jnp.float32,
        )
        return (partial_out, maxima, totals)

    grouped_q = query_rows.reshape(query_blocks // group_size, group_size, part_rows, head_depth)
    grouped_ids = local_ids[:, :slot_count].reshape(
        query_blocks // group_size, group_size, slot_count
    )
    partial_out, maxima, totals = lax.map(one_group, (grouped_q, grouped_ids))
    return (
        partial_out.reshape(query_blocks, part_rows, head_depth),
        maxima.reshape(query_blocks, part_rows),
        totals.reshape(query_blocks, part_rows),
    )


def arrange_heads(stacked):
    swapped = jnp.swapaxes(stacked, 0, 1)
    return swapped.reshape((-1,) + stacked.shape[2:])


def spans_by_device(queries, keys, values, kept, dense_class):
    seq_devices = lax.axis_size("seq")
    span_count = lax.axis_size("blk")
    local_rows = queries.shape[0]
    head_count = HEADS
    head_depth = HD
    local_blocks = local_rows // BLOCK
    row_parts = max(1, 2 * seq_devices // head_count)
    part_rows = BLOCK // row_parts
    item_count = head_count * row_parts
    per_device = item_count // seq_devices
    seq_place = lax.axis_index("seq")
    blk_place = lax.axis_index("blk")
    every_item = jnp.arange(item_count, dtype=jnp.int32)
    all_item_heads = every_item // row_parts
    item_heads = lax.dynamic_slice_in_dim(all_item_heads, seq_place * per_device, per_device)
    grid_q = queries.reshape(local_blocks, row_parts, part_rows, head_count, head_depth).transpose(
        1, 3, 0, 2, 4
    )
    grid_q = grid_q.reshape(row_parts, head_count, local_blocks * part_rows, head_depth)
    head_keys = keys.reshape(local_rows, head_count, head_depth).transpose(1, 0, 2)
    head_values = values.reshape(local_rows, head_count, head_depth).transpose(1, 0, 2)
    send_q = arrange_heads(grid_q)
    q_items = lax.all_to_all(send_q, "seq", split_axis=0, concat_axis=1, tiled=True)
    stride = 1
    grid_k = jnp.broadcast_to(head_keys[None], (row_parts, head_count, local_rows, head_depth))
    grid_v = jnp.broadcast_to(head_values[None], (row_parts, head_count, local_rows, head_depth))
    send_k = arrange_heads(grid_k)
    send_v = arrange_heads(grid_v)
    k_held, v_held = (
        lax.all_to_all(send_k, "seq", split_axis=0, concat_axis=1, tiled=True),
        lax.all_to_all(send_v, "seq", split_axis=0, concat_axis=1, tiled=True),
    )
    key_blocks = k_held.reshape(per_device, seq_devices * local_blocks, BLOCK, head_depth)
    blocked_value_rows = v_held.reshape(per_device, seq_devices * local_blocks, BLOCK, head_depth)
    item_slot = jnp.arange(per_device, dtype=jnp.int32) // stride
    item_class = jnp.take(dense_class, item_heads)
    item_kept = jnp.take(kept, item_heads, axis=0)
    source_index = jnp.arange(seq_devices, dtype=jnp.int32)
    block_index = jnp.arange(local_blocks, dtype=jnp.int32)
    span_index = jnp.arange(span_count, dtype=jnp.int32)
    all_ids = (
        (source_index[None, :, None] * span_count + span_index[:, None, None]) * local_blocks
        + block_index[None, None, :]
    ).reshape(-1)
    all_kept = jnp.take(item_kept, all_ids, axis=1)
    span_ids = lax.dynamic_slice_in_dim(all_kept, blk_place * KEEP, KEEP, axis=2)
    q_all = lax.all_gather(q_items, "blk", axis=1, tiled=True)
    query_rows = q_all.reshape(
        per_device, span_count * seq_devices * local_blocks, part_rows, head_depth
    )

    def one_item(operands):
        rows_item, ids_item, class_item, slot_item = operands
        keys_item = lax.dynamic_index_in_dim(key_blocks, slot_item, 0, keepdims=False)
        values_item = lax.dynamic_index_in_dim(blocked_value_rows, slot_item, 0, keepdims=False)
        return lax.cond(
            class_item == 1,
            lambda: attend_blocks(rows_item, keys_item, values_item, ids_item, KEEP),
            lambda: attend_blocks(rows_item, keys_item, values_item, ids_item, LIGHT),
        )

    partial_out, maxima, totals = lax.map(
        one_item,
        (
            query_rows,
            span_ids // (local_blocks * span_count) * local_blocks + span_ids % local_blocks,
            item_class,
            item_slot,
        ),
    )
    own_blocks = seq_devices * local_blocks
    shaped_out = partial_out.reshape(per_device, span_count, own_blocks, part_rows, head_depth)
    shaped_max = maxima.reshape(per_device, span_count, own_blocks, part_rows)
    shaped_total = totals.reshape(per_device, span_count, own_blocks, part_rows)
    got_out, got_max, got_total = (
        lax.all_to_all(shaped_out, "blk", split_axis=1, concat_axis=1, tiled=True),
        lax.all_to_all(shaped_max, "blk", split_axis=1, concat_axis=1, tiled=True),
        lax.all_to_all(shaped_total, "blk", split_axis=1, concat_axis=1, tiled=True),
    )
    attended_items = combine_spans(got_out, got_max, got_total, 1)
    attended_items = attended_items.reshape(
        per_device, seq_devices * local_blocks * part_rows, head_depth
    )
    returned = lax.all_to_all(attended_items, "seq", split_axis=1, concat_axis=0, tiled=True)
    grid_out = returned.reshape(head_count, row_parts, local_blocks, part_rows, head_depth)
    grid_out = jnp.swapaxes(grid_out, 0, 1)
    return grid_out.transpose(2, 0, 3, 1, 4).reshape(local_rows, head_count * head_depth)


def own_place(axes):
    place = 0
    for axis in axes:
        place = place * lax.axis_size(axis) + lax.axis_index(axis)
    return place


def each_light_block(kept_ref, block):
    return [
        kept_ref[block, span * KEEP + slot]
        for span in range(kept_ref.shape[1] // KEEP)
        for slot in range(LIGHT)
    ]


def pack_kernel(*refs):
    sources, (out_ref, landed, staged, in_sems, out_sems) = refs[:-5], refs[-5:]
    heads = out_ref.shape[0]
    count, rows = landed.shape[:2]
    pieces = in_sems.shape[1]
    piece_rows = rows // pieces
    arrivals = [
        [
            pltpu.make_async_copy(
                source.at[pl.ds(piece * piece_rows, piece_rows), :],
                landed.at[place, pl.ds(piece * piece_rows, piece_rows), :],
                in_sems.at[place, piece],
            )
            for piece in range(pieces)
        ]
        for place, source in enumerate(sources)
    ]
    share = heads // pieces
    departures = [
        [
            pltpu.make_async_copy(
                staged.at[place, pl.ds(piece * share, share)],
                out_ref.at[pl.ds(piece * share, share), place],
                out_sems.at[place, piece],
            )
            for piece in range(pieces)
        ]
        for place in range(count)
    ]
    for copies in arrivals:
        for copy in copies:
            copy.start()
    for place in range(count):
        for copy in arrivals[place]:
            copy.wait()
        for piece in range(pieces):
            for head in range(piece * share, (piece + 1) * share):
                staged[place, head] = landed[place, :, head * HD : (head + 1) * HD]
            departures[place][piece].start()
    for copies in departures:
        for copy in copies:
            copy.wait()


def pack_heads(*sources):
    count = len(sources)
    rows = sources[0].shape[0]
    pieces = 4
    return pl.pallas_call(
        pack_kernel,
        out_shape=jax.ShapeDtypeStruct((HEADS, count, rows, HD), jnp.bfloat16),
        in_specs=[pl.BlockSpec(memory_space=pltpu.HBM)] * count,
        out_specs=pl.BlockSpec(memory_space=pl.ANY),
        scratch_shapes=[
            pltpu.VMEM((count, rows, HEADS * HD), jnp.bfloat16),
            pltpu.VMEM((count, HEADS, rows, HD), jnp.bfloat16),
            pltpu.SemaphoreType.DMA((count, pieces)),
            pltpu.SemaphoreType.DMA((count, pieces)),
        ],
        compiler_params=pltpu.CompilerParams(vmem_limit_bytes=59 * 1024 * 1024),
        name="pack_heads",
    )(*sources)


def unpack_kernel(held_ref, out_ref, sems):
    copies = [
        pltpu.make_async_copy(
            held_ref.at[head], out_ref.at[:, head * HD : (head + 1) * HD], sems.at[head]
        )
        for head in range(held_ref.shape[0])
    ]
    for copy in copies:
        copy.start()
    for copy in copies:
        copy.wait()


def unpack_heads(held):
    heads, rows, depth = held.shape
    return pl.pallas_call(
        unpack_kernel,
        out_shape=jax.ShapeDtypeStruct((rows, heads * depth), jnp.bfloat16),
        in_specs=[pl.BlockSpec(memory_space=pl.ANY)],
        out_specs=pl.BlockSpec(memory_space=pltpu.HBM),
        scratch_shapes=[pltpu.SemaphoreType.DMA((heads,))],
        compiler_params=pltpu.CompilerParams(vmem_limit_bytes=4 * 1024 * 1024),
        name="unpack_heads",
    )(held)


def pipelined(count, score, weigh, blend):
    score(0, 0)
    weigh(0, 0)
    score(1, 1)

    def step(j, carry):
        blend(2 * j, 0)
        weigh(2 * j + 1, 1)
        score(2 * j + 2, 0)
        blend(2 * j + 1, 1)
        weigh(2 * j + 2, 0)
        score(2 * j + 3, 1)
        return carry

    lax.fori_loop(0, count // 2 - 1, step, 0)
    blend(count - 2, 0)
    weigh(count - 1, 1)
    blend(count - 1, 1)


def attend_kernel(axes, kept_hbm, class_ref, qkv_ref, out_ref, *scratch):
    kept_ref, v_all, logits_a, logits_b, weights_a, weights_b, largest_rows, sem = scratch
    logits_slots = (logits_a, logits_b)
    weights_slots = (weights_a, weights_b)
    block_count = qkv_ref.shape[0]
    me = own_place(axes)
    exponent_scale = math.log2(math.e) / math.sqrt(HD)
    kept_copy = pltpu.make_async_copy(kept_hbm.at[me], kept_ref, sem)
    kept_copy.start()
    v_all[:, :, :HD] = qkv_ref[:, 2]
    v_all[:, :, HD:] = jnp.ones((block_count, BLOCK, HD), jnp.bfloat16)

    def scores(query_rows, key_rows):
        return lax.dot_general(
            query_rows, key_rows, (((1,), (1,)), ((), ())), preferred_element_type=jnp.float32
        )

    def weigh(rows, columns, slot):
        chunk = 16
        for row in range(0, rows, chunk):
            largest = jnp.max(logits_slots[slot][row : row + chunk, :columns], -1, keepdims=True)
            largest_rows[row : row + chunk, :] = jnp.broadcast_to(largest, (chunk, HD))
        for row in range(0, rows, chunk):
            largest = largest_rows[row : row + chunk, :]
            for column in range(0, columns, HD):
                logits = logits_slots[slot][row : row + chunk, column : column + HD]
                weights = jnp.exp2((logits - largest) * exponent_scale).astype(jnp.bfloat16)
                weights_slots[slot][row : row + chunk, column : column + HD] = weights

    def normalized(summed):
        return (summed[:, :HD] / summed[:, HD:]).astype(jnp.bfloat16)

    @pl.when(class_ref[me] == 1)
    def _():
        group = 4

        def score(i, slot):
            query_rows = qkv_ref[pl.ds(group * i, group), 0].reshape(group * BLOCK, HD)
            key_rows = qkv_ref[:, 1].reshape(block_count * BLOCK, HD)
            logits_slots[slot][...] = scores(query_rows, key_rows)

        def blend(i, slot):
            value_rows = v_all[...].reshape(block_count * BLOCK, 2 * HD)
            out = normalized(
                jnp.dot(weights_slots[slot][...], value_rows, preferred_element_type=jnp.float32)
            )
            out_ref[pl.ds(group * i, group)] = out.reshape(group, BLOCK, HD)

        def weigh_all(i, slot):
            weigh(group * BLOCK, block_count * BLOCK, slot)

        pipelined(block_count // group, score, weigh_all, blend)
        kept_copy.wait()

    @pl.when(class_ref[me] != 1)
    def _():
        kept_copy.wait()
        group = 2

        def block_pairs(block):
            kept_blocks = each_light_block(kept_ref, block)
            return list(zip(kept_blocks[::2], kept_blocks[1::2]))

        def score(i, slot):
            for member in range(group):
                block = group * i + member
                rows = slice(member * BLOCK, (member + 1) * BLOCK)
                for place, (one, other) in enumerate(block_pairs(block)):
                    key_rows = jnp.concatenate([qkv_ref[one, 1], qkv_ref[other, 1]], axis=0)
                    columns = slice(place * 2 * BLOCK, (place + 1) * 2 * BLOCK)
                    logits_slots[slot][rows, columns] = scores(qkv_ref[block, 0], key_rows)

        def blend(i, slot):
            for member in range(group):
                block = group * i + member
                rows = slice(member * BLOCK, (member + 1) * BLOCK)
                summed = jnp.zeros((BLOCK, 2 * HD), jnp.float32)
                for place, (one, other) in enumerate(block_pairs(block)):
                    value_rows = jnp.concatenate([v_all[one], v_all[other]], axis=0)
                    columns = slice(place * 2 * BLOCK, (place + 1) * 2 * BLOCK)
                    weights = weights_slots[slot][rows, columns]
                    summed += jnp.dot(weights, value_rows, preferred_element_type=jnp.float32)
                out_ref[block] = normalized(summed)

        def weigh_few(i, slot):
            weigh(group * BLOCK, block_count // KEEP * LIGHT * BLOCK, slot)

        pipelined(block_count // group, score, weigh_few, blend)


def heads_by_device(queries, keys, values, kept, dense_class):
    axes = ("seq", "blk")
    block_count = kept.shape[1]
    in_vmem = pl.BlockSpec(memory_space=pltpu.VMEM)

    def exchange(send):
        return lax.all_to_all(send, axes, split_axis=0, concat_axis=0, tiled=True)

    held = exchange(pack_heads(queries, keys, values))
    attended = pl.pallas_call(
        lambda *refs: attend_kernel(axes, *refs),
        out_shape=jax.ShapeDtypeStruct((block_count, BLOCK, HD), jnp.bfloat16),
        in_specs=[
            pl.BlockSpec(memory_space=pl.ANY),
            pl.BlockSpec(memory_space=pltpu.SMEM),
            in_vmem,
        ],
        out_specs=in_vmem,
        scratch_shapes=[
            pltpu.SMEM(kept.shape[1:], jnp.int32),
            pltpu.VMEM((block_count, BLOCK, 2 * HD), jnp.bfloat16),
            pltpu.VMEM((4 * BLOCK, block_count * BLOCK), jnp.float32),
            pltpu.VMEM((4 * BLOCK, block_count * BLOCK), jnp.float32),
            pltpu.VMEM((4 * BLOCK, block_count * BLOCK), jnp.bfloat16),
            pltpu.VMEM((4 * BLOCK, block_count * BLOCK), jnp.bfloat16),
            pltpu.VMEM((4 * BLOCK, HD), jnp.float32),
            pltpu.SemaphoreType.DMA,
        ],
        compiler_params=pltpu.CompilerParams(vmem_limit_bytes=32 * 1024 * 1024),
        name="attend_head",
    )(kept, dense_class, held)
    return unpack_heads(exchange(attended))


def shards(queries, keys, values, kept, dense_class):
    devices = lax.axis_size("seq") * lax.axis_size("blk")
    one_head_each = devices == HEADS
    one_block_each = queries.shape[0] == BLOCK
    every_block_kept = kept.shape[1] == kept.shape[2]
    if one_head_each and one_block_each and every_block_kept:
        return heads_by_device(queries, keys, values, kept, dense_class)
    return spans_by_device(queries, keys, values, kept, dense_class)


def solution(mesh):
    return jax.shard_map(
        shards,
        mesh=mesh,
        in_specs=(
            P(("clip", "seq", "blk"), None),
            P(("clip", "seq", "blk"), None),
            P(("clip", "seq", "blk"), None),
            P(),
            P(),
        ),
        out_specs=P(("clip", "seq", "blk"), None),
        check_vma=False,
    )
```

```python
import math

import jax
import jax.numpy as jnp
from jax import lax
from jax.experimental import pallas as pl
from jax.experimental.pallas import tpu as pltpu
from jax.sharding import PartitionSpec as P

HEADS = 16
HD = 128
BLOCK = 128
KEEP = 4
LIGHT = 2


def combine_spans(partial_out, maxima, totals, along):
    largest = jnp.max(maxima, axis=along, keepdims=True)
    factor = jnp.exp(maxima - largest)
    numerator = jnp.sum(factor[..., None] * partial_out, axis=along)
    denominator = jnp.sum(factor * totals, axis=along)
    return (numerator / denominator[..., None]).astype(jnp.bfloat16)


def attend_blocks(query_rows, key_blocks, blocked_value_rows, local_ids, slot_count):
    query_blocks, part_rows, head_depth = query_rows.shape
    group_size = query_blocks
    while group_size * part_rows > 512 and group_size % 2 == 0:
        group_size = group_size // 2
    logit_scale_factor = 1.0 / math.sqrt(head_depth)
    block_rows = key_blocks.shape[1]

    def one_group(operands):
        queries_group, ids_group = operands
        collected_key_blocks = key_blocks[ids_group].reshape(
            group_size, slot_count * block_rows, head_depth
        )
        gathered_v = blocked_value_rows[ids_group].reshape(
            group_size, slot_count * block_rows, head_depth
        )
        attention_logits = (
            jnp.einsum(
                "gpd,gkd->gpk",
                queries_group,
                collected_key_blocks,
                preferred_element_type=jnp.float32,
            )
            * logit_scale_factor
        )
        maxima = jnp.max(attention_logits, axis=-1)
        weights = jnp.exp(attention_logits - maxima[..., None])
        totals = jnp.sum(weights, axis=-1)
        partial_out = jnp.einsum(
            "gpk,gkd->gpd",
            weights.astype(jnp.bfloat16),
            gathered_v,
            preferred_element_type=jnp.float32,
        )
        return (partial_out, maxima, totals)

    grouped_q = query_rows.reshape(query_blocks // group_size, group_size, part_rows, head_depth)
    grouped_ids = local_ids[:, :slot_count].reshape(
        query_blocks // group_size, group_size, slot_count
    )
    partial_out, maxima, totals = lax.map(one_group, (grouped_q, grouped_ids))
    return (
        partial_out.reshape(query_blocks, part_rows, head_depth),
        maxima.reshape(query_blocks, part_rows),
        totals.reshape(query_blocks, part_rows),
    )


def arrange_heads(stacked):
    swapped = jnp.swapaxes(stacked, 0, 1)
    return swapped.reshape((-1,) + stacked.shape[2:])


def spans_by_device(queries, keys, values, kept, dense_class):
    seq_devices = lax.axis_size("seq")
    span_count = lax.axis_size("blk")
    local_rows = queries.shape[0]
    head_count = HEADS
    head_depth = HD
    local_blocks = local_rows // BLOCK
    row_parts = max(1, 2 * seq_devices // head_count)
    part_rows = BLOCK // row_parts
    item_count = head_count * row_parts
    per_device = item_count // seq_devices
    seq_place = lax.axis_index("seq")
    blk_place = lax.axis_index("blk")
    every_item = jnp.arange(item_count, dtype=jnp.int32)
    all_item_heads = every_item // row_parts
    item_heads = lax.dynamic_slice_in_dim(all_item_heads, seq_place * per_device, per_device)
    grid_q = queries.reshape(local_blocks, row_parts, part_rows, head_count, head_depth).transpose(
        1, 3, 0, 2, 4
    )
    grid_q = grid_q.reshape(row_parts, head_count, local_blocks * part_rows, head_depth)
    head_keys = keys.reshape(local_rows, head_count, head_depth).transpose(1, 0, 2)
    head_values = values.reshape(local_rows, head_count, head_depth).transpose(1, 0, 2)
    send_q = arrange_heads(grid_q)
    q_items = lax.all_to_all(send_q, "seq", split_axis=0, concat_axis=1, tiled=True)
    stride = 1
    grid_k = jnp.broadcast_to(head_keys[None], (row_parts, head_count, local_rows, head_depth))
    grid_v = jnp.broadcast_to(head_values[None], (row_parts, head_count, local_rows, head_depth))
    send_k = arrange_heads(grid_k)
    send_v = arrange_heads(grid_v)
    k_held, v_held = (
        lax.all_to_all(send_k, "seq", split_axis=0, concat_axis=1, tiled=True),
        lax.all_to_all(send_v, "seq", split_axis=0, concat_axis=1, tiled=True),
    )
    key_blocks = k_held.reshape(per_device, seq_devices * local_blocks, BLOCK, head_depth)
    blocked_value_rows = v_held.reshape(per_device, seq_devices * local_blocks, BLOCK, head_depth)
    item_slot = jnp.arange(per_device, dtype=jnp.int32) // stride
    item_class = jnp.take(dense_class, item_heads)
    item_kept = jnp.take(kept, item_heads, axis=0)
    source_index = jnp.arange(seq_devices, dtype=jnp.int32)
    block_index = jnp.arange(local_blocks, dtype=jnp.int32)
    span_index = jnp.arange(span_count, dtype=jnp.int32)
    all_ids = (
        (source_index[None, :, None] * span_count + span_index[:, None, None]) * local_blocks
        + block_index[None, None, :]
    ).reshape(-1)
    all_kept = jnp.take(item_kept, all_ids, axis=1)
    span_ids = lax.dynamic_slice_in_dim(all_kept, blk_place * KEEP, KEEP, axis=2)
    q_all = lax.all_gather(q_items, "blk", axis=1, tiled=True)
    query_rows = q_all.reshape(
        per_device, span_count * seq_devices * local_blocks, part_rows, head_depth
    )

    def one_item(operands):
        rows_item, ids_item, class_item, slot_item = operands
        keys_item = lax.dynamic_index_in_dim(key_blocks, slot_item, 0, keepdims=False)
        values_item = lax.dynamic_index_in_dim(blocked_value_rows, slot_item, 0, keepdims=False)
        return lax.cond(
            class_item == 1,
            lambda: attend_blocks(rows_item, keys_item, values_item, ids_item, KEEP),
            lambda: attend_blocks(rows_item, keys_item, values_item, ids_item, LIGHT),
        )

    partial_out, maxima, totals = lax.map(
        one_item,
        (
            query_rows,
            span_ids // (local_blocks * span_count) * local_blocks + span_ids % local_blocks,
            item_class,
            item_slot,
        ),
    )
    own_blocks = seq_devices * local_blocks
    shaped_out = partial_out.reshape(per_device, span_count, own_blocks, part_rows, head_depth)
    shaped_max = maxima.reshape(per_device, span_count, own_blocks, part_rows)
    shaped_total = totals.reshape(per_device, span_count, own_blocks, part_rows)
    got_out, got_max, got_total = (
        lax.all_to_all(shaped_out, "blk", split_axis=1, concat_axis=1, tiled=True),
        lax.all_to_all(shaped_max, "blk", split_axis=1, concat_axis=1, tiled=True),
        lax.all_to_all(shaped_total, "blk", split_axis=1, concat_axis=1, tiled=True),
    )
    attended_items = combine_spans(got_out, got_max, got_total, 1)
    attended_items = attended_items.reshape(
        per_device, seq_devices * local_blocks * part_rows, head_depth
    )
    returned = lax.all_to_all(attended_items, "seq", split_axis=1, concat_axis=0, tiled=True)
    grid_out = returned.reshape(head_count, row_parts, local_blocks, part_rows, head_depth)
    grid_out = jnp.swapaxes(grid_out, 0, 1)
    return grid_out.transpose(2, 0, 3, 1, 4).reshape(local_rows, head_count * head_depth)


def own_place(axes):
    place = 0
    for axis in axes:
        place = place * lax.axis_size(axis) + lax.axis_index(axis)
    return place


def each_light_block(kept_ref, block):
    return [
        kept_ref[block, span * KEEP + slot]
        for span in range(kept_ref.shape[1] // KEEP)
        for slot in range(LIGHT)
    ]


def pack_kernel(*refs):
    sources, out_ref, sems = refs[:-2], refs[-2], refs[-1]
    copies = []
    for head in range(out_ref.shape[0]):
        for place, source in enumerate(sources):
            copies.append(
                pltpu.make_async_copy(
                    source.at[:, head * HD : (head + 1) * HD],
                    out_ref.at[head, place],
                    sems.at[head, place],
                )
            )
    for copy in copies:
        copy.start()
    for copy in copies:
        copy.wait()


def pack_heads(*sources):
    count = len(sources)
    rows = sources[0].shape[0]
    return pl.pallas_call(
        pack_kernel,
        out_shape=jax.ShapeDtypeStruct((HEADS, count, rows, HD), jnp.bfloat16),
        in_specs=[pl.BlockSpec(memory_space=pltpu.HBM)] * count,
        out_specs=pl.BlockSpec(memory_space=pltpu.VMEM),
        scratch_shapes=[pltpu.SemaphoreType.DMA((HEADS, count))],
        compiler_params=pltpu.CompilerParams(vmem_limit_bytes=4 * 1024 * 1024),
        name="pack_heads",
    )(*[pltpu.with_memory_space_constraint(source, pltpu.HBM) for source in sources])


def unpack_kernel(held_ref, out_ref, sems):
    copies = [
        pltpu.make_async_copy(
            held_ref.at[head], out_ref.at[:, head * HD : (head + 1) * HD], sems.at[head]
        )
        for head in range(held_ref.shape[0])
    ]
    for copy in copies:
        copy.start()
    for copy in copies:
        copy.wait()


def unpack_heads(held):
    heads, rows, depth = held.shape
    return pl.pallas_call(
        unpack_kernel,
        out_shape=jax.ShapeDtypeStruct((rows, heads * depth), jnp.bfloat16),
        in_specs=[pl.BlockSpec(memory_space=pl.ANY)],
        out_specs=pl.BlockSpec(memory_space=pltpu.HBM),
        scratch_shapes=[pltpu.SemaphoreType.DMA((heads,))],
        compiler_params=pltpu.CompilerParams(vmem_limit_bytes=4 * 1024 * 1024),
        name="unpack_heads",
    )(held)


def pipelined(count, prepare, score, weigh, blend):
    score(0, 0)
    prepare()
    weigh(0, 0)
    score(1, 1)

    def step(j, carry):
        blend(2 * j, 0)
        weigh(2 * j + 1, 1)
        score(2 * j + 2, 0)
        blend(2 * j + 1, 1)
        weigh(2 * j + 2, 0)
        score(2 * j + 3, 1)
        return carry

    lax.fori_loop(0, count // 2 - 1, step, 0)
    blend(count - 2, 0)
    weigh(count - 1, 1)
    blend(count - 1, 1)


def attend_kernel(axes, kept_hbm, class_ref, qkv_ref, out_ref, *scratch):
    kept_ref, v_all, logits_a, logits_b, weights_a, weights_b, sem = scratch
    logits_slots = (logits_a, logits_b)
    weights_slots = (weights_a, weights_b)
    block_count = qkv_ref.shape[0]
    me = own_place(axes)
    exponent_scale = math.log2(math.e) / math.sqrt(HD)
    kept_copy = pltpu.make_async_copy(kept_hbm.at[me], kept_ref, sem)
    kept_copy.start()

    def set_values():
        v_all[:, :, :HD] = qkv_ref[:, 2]
        v_all[:, :, HD:] = jnp.ones((block_count, BLOCK, HD), jnp.bfloat16)

    def scores(query_rows, key_rows):
        return lax.dot_general(
            query_rows, key_rows, (((1,), (1,)), ((), ())), preferred_element_type=jnp.float32
        )

    def weigh(rows, columns, slot):
        logits = logits_slots[slot][:rows, :columns]
        largest = jnp.max(logits, axis=-1, keepdims=True)
        weights = jnp.exp2((logits - largest) * exponent_scale).astype(jnp.bfloat16)
        weights_slots[slot][:rows, :columns] = weights

    def normalized(summed):
        return (summed[:, :HD] / summed[:, HD:]).astype(jnp.bfloat16)

    @pl.when(class_ref[me] == 1)
    def _():
        group = 4

        def score(i, slot):
            query_rows = qkv_ref[pl.ds(group * i, group), 0].reshape(group * BLOCK, HD)
            key_rows = qkv_ref[:, 1].reshape(block_count * BLOCK, HD)
            logits_slots[slot][...] = scores(query_rows, key_rows)

        def blend(i, slot):
            value_rows = v_all[...].reshape(block_count * BLOCK, 2 * HD)
            out = normalized(
                jnp.dot(weights_slots[slot][...], value_rows, preferred_element_type=jnp.float32)
            )
            out_ref[pl.ds(group * i, group)] = out.reshape(group, BLOCK, HD)

        def weigh_all(i, slot):
            weigh(group * BLOCK, block_count * BLOCK, slot)

        pipelined(block_count // group, set_values, score, weigh_all, blend)
        kept_copy.wait()

    @pl.when(class_ref[me] != 1)
    def _():
        kept_copy.wait()
        group = 2

        def block_pairs(block):
            kept_blocks = each_light_block(kept_ref, block)
            return list(zip(kept_blocks[::2], kept_blocks[1::2]))

        def score(i, slot):
            for member in range(group):
                block = group * i + member
                rows = slice(member * BLOCK, (member + 1) * BLOCK)
                for place, (one, other) in enumerate(block_pairs(block)):
                    key_rows = jnp.concatenate([qkv_ref[one, 1], qkv_ref[other, 1]], axis=0)
                    columns = slice(place * 2 * BLOCK, (place + 1) * 2 * BLOCK)
                    logits_slots[slot][rows, columns] = scores(qkv_ref[block, 0], key_rows)

        def blend(i, slot):
            for member in range(group):
                block = group * i + member
                rows = slice(member * BLOCK, (member + 1) * BLOCK)
                summed = jnp.zeros((BLOCK, 2 * HD), jnp.float32)
                for place, (one, other) in enumerate(block_pairs(block)):
                    value_rows = jnp.concatenate([v_all[one], v_all[other]], axis=0)
                    columns = slice(place * 2 * BLOCK, (place + 1) * 2 * BLOCK)
                    weights = weights_slots[slot][rows, columns]
                    summed += jnp.dot(weights, value_rows, preferred_element_type=jnp.float32)
                out_ref[block] = normalized(summed)

        def weigh_few(i, slot):
            weigh(group * BLOCK, block_count // KEEP * LIGHT * BLOCK, slot)

        pipelined(block_count // group, set_values, score, weigh_few, blend)


def heads_by_device(queries, keys, values, kept, dense_class):
    axes = ("seq", "blk")
    block_count = kept.shape[1]
    in_vmem = pl.BlockSpec(memory_space=pltpu.VMEM)

    def exchange(send):
        return lax.all_to_all(send, axes, split_axis=0, concat_axis=0, tiled=True)

    held = exchange(pack_heads(queries, keys, values))
    attended = pl.pallas_call(
        lambda *refs: attend_kernel(axes, *refs),
        out_shape=jax.ShapeDtypeStruct((block_count, BLOCK, HD), jnp.bfloat16),
        in_specs=[
            pl.BlockSpec(memory_space=pl.ANY),
            pl.BlockSpec(memory_space=pltpu.SMEM),
            in_vmem,
        ],
        out_specs=in_vmem,
        scratch_shapes=[
            pltpu.SMEM(kept.shape[1:], jnp.int32),
            pltpu.VMEM((block_count, BLOCK, 2 * HD), jnp.bfloat16),
            pltpu.VMEM((4 * BLOCK, block_count * BLOCK), jnp.float32),
            pltpu.VMEM((4 * BLOCK, block_count * BLOCK), jnp.float32),
            pltpu.VMEM((4 * BLOCK, block_count * BLOCK), jnp.bfloat16),
            pltpu.VMEM((4 * BLOCK, block_count * BLOCK), jnp.bfloat16),
            pltpu.SemaphoreType.DMA,
        ],
        compiler_params=pltpu.CompilerParams(vmem_limit_bytes=32 * 1024 * 1024),
        name="attend_head",
    )(kept, dense_class, held)
    return unpack_heads(exchange(attended))


def shards(queries, keys, values, kept, dense_class):
    devices = lax.axis_size("seq") * lax.axis_size("blk")
    one_head_each = devices == HEADS
    one_block_each = queries.shape[0] == BLOCK
    every_block_kept = kept.shape[1] == kept.shape[2]
    if one_head_each and one_block_each and every_block_kept:
        return heads_by_device(queries, keys, values, kept, dense_class)
    return spans_by_device(queries, keys, values, kept, dense_class)


def solution(mesh):
    return jax.shard_map(
        shards,
        mesh=mesh,
        in_specs=(
            P(("clip", "seq", "blk"), None),
            P(("clip", "seq", "blk"), None),
            P(("clip", "seq", "blk"), None),
            P(),
            P(),
        ),
        out_specs=P(("clip", "seq", "blk"), None),
        check_vma=False,
    )
```

```python
import math

import jax
import jax.numpy as jnp
from jax import lax
from jax.experimental import pallas as pl
from jax.experimental.pallas import tpu as pltpu
from jax.sharding import PartitionSpec as P

HEADS = 16
HD = 128
BLOCK = 128
KEEP = 4
LIGHT = 2


def combine_spans(partial_out, maxima, totals, along):
    largest = jnp.max(maxima, axis=along, keepdims=True)
    factor = jnp.exp(maxima - largest)
    numerator = jnp.sum(factor[..., None] * partial_out, axis=along)
    denominator = jnp.sum(factor * totals, axis=along)
    return (numerator / denominator[..., None]).astype(jnp.bfloat16)


def attend_blocks(query_rows, key_blocks, blocked_value_rows, local_ids, slot_count):
    query_blocks, part_rows, head_depth = query_rows.shape
    group_size = query_blocks
    while group_size * part_rows > 512 and group_size % 2 == 0:
        group_size = group_size // 2
    logit_scale_factor = 1.0 / math.sqrt(head_depth)
    block_rows = key_blocks.shape[1]

    def one_group(operands):
        queries_group, ids_group = operands
        collected_key_blocks = key_blocks[ids_group].reshape(
            group_size, slot_count * block_rows, head_depth
        )
        gathered_v = blocked_value_rows[ids_group].reshape(
            group_size, slot_count * block_rows, head_depth
        )
        attention_logits = (
            jnp.einsum(
                "gpd,gkd->gpk",
                queries_group,
                collected_key_blocks,
                preferred_element_type=jnp.float32,
            )
            * logit_scale_factor
        )
        maxima = jnp.max(attention_logits, axis=-1)
        weights = jnp.exp(attention_logits - maxima[..., None])
        totals = jnp.sum(weights, axis=-1)
        partial_out = jnp.einsum(
            "gpk,gkd->gpd",
            weights.astype(jnp.bfloat16),
            gathered_v,
            preferred_element_type=jnp.float32,
        )
        return (partial_out, maxima, totals)

    grouped_q = query_rows.reshape(query_blocks // group_size, group_size, part_rows, head_depth)
    grouped_ids = local_ids[:, :slot_count].reshape(
        query_blocks // group_size, group_size, slot_count
    )
    partial_out, maxima, totals = lax.map(one_group, (grouped_q, grouped_ids))
    return (
        partial_out.reshape(query_blocks, part_rows, head_depth),
        maxima.reshape(query_blocks, part_rows),
        totals.reshape(query_blocks, part_rows),
    )


def arrange_heads(stacked):
    swapped = jnp.swapaxes(stacked, 0, 1)
    return swapped.reshape((-1,) + stacked.shape[2:])


def spans_by_device(queries, keys, values, kept, dense_class):
    seq_devices = lax.axis_size("seq")
    span_count = lax.axis_size("blk")
    local_rows = queries.shape[0]
    head_count = HEADS
    head_depth = HD
    local_blocks = local_rows // BLOCK
    row_parts = max(1, 2 * seq_devices // head_count)
    part_rows = BLOCK // row_parts
    item_count = head_count * row_parts
    per_device = item_count // seq_devices
    seq_place = lax.axis_index("seq")
    blk_place = lax.axis_index("blk")
    every_item = jnp.arange(item_count, dtype=jnp.int32)
    all_item_heads = every_item // row_parts
    item_heads = lax.dynamic_slice_in_dim(all_item_heads, seq_place * per_device, per_device)
    grid_q = queries.reshape(local_blocks, row_parts, part_rows, head_count, head_depth).transpose(
        1, 3, 0, 2, 4
    )
    grid_q = grid_q.reshape(row_parts, head_count, local_blocks * part_rows, head_depth)
    head_keys = keys.reshape(local_rows, head_count, head_depth).transpose(1, 0, 2)
    head_values = values.reshape(local_rows, head_count, head_depth).transpose(1, 0, 2)
    send_q = arrange_heads(grid_q)
    q_items = lax.all_to_all(send_q, "seq", split_axis=0, concat_axis=1, tiled=True)
    stride = 1
    grid_k = jnp.broadcast_to(head_keys[None], (row_parts, head_count, local_rows, head_depth))
    grid_v = jnp.broadcast_to(head_values[None], (row_parts, head_count, local_rows, head_depth))
    send_k = arrange_heads(grid_k)
    send_v = arrange_heads(grid_v)
    k_held, v_held = (
        lax.all_to_all(send_k, "seq", split_axis=0, concat_axis=1, tiled=True),
        lax.all_to_all(send_v, "seq", split_axis=0, concat_axis=1, tiled=True),
    )
    key_blocks = k_held.reshape(per_device, seq_devices * local_blocks, BLOCK, head_depth)
    blocked_value_rows = v_held.reshape(per_device, seq_devices * local_blocks, BLOCK, head_depth)
    item_slot = jnp.arange(per_device, dtype=jnp.int32) // stride
    item_class = jnp.take(dense_class, item_heads)
    item_kept = jnp.take(kept, item_heads, axis=0)
    source_index = jnp.arange(seq_devices, dtype=jnp.int32)
    block_index = jnp.arange(local_blocks, dtype=jnp.int32)
    span_index = jnp.arange(span_count, dtype=jnp.int32)
    all_ids = (
        (source_index[None, :, None] * span_count + span_index[:, None, None]) * local_blocks
        + block_index[None, None, :]
    ).reshape(-1)
    all_kept = jnp.take(item_kept, all_ids, axis=1)
    span_ids = lax.dynamic_slice_in_dim(all_kept, blk_place * KEEP, KEEP, axis=2)
    q_all = lax.all_gather(q_items, "blk", axis=1, tiled=True)
    query_rows = q_all.reshape(
        per_device, span_count * seq_devices * local_blocks, part_rows, head_depth
    )

    def one_item(operands):
        rows_item, ids_item, class_item, slot_item = operands
        keys_item = lax.dynamic_index_in_dim(key_blocks, slot_item, 0, keepdims=False)
        values_item = lax.dynamic_index_in_dim(blocked_value_rows, slot_item, 0, keepdims=False)
        return lax.cond(
            class_item == 1,
            lambda: attend_blocks(rows_item, keys_item, values_item, ids_item, KEEP),
            lambda: attend_blocks(rows_item, keys_item, values_item, ids_item, LIGHT),
        )

    partial_out, maxima, totals = lax.map(
        one_item,
        (
            query_rows,
            span_ids // (local_blocks * span_count) * local_blocks + span_ids % local_blocks,
            item_class,
            item_slot,
        ),
    )
    own_blocks = seq_devices * local_blocks
    shaped_out = partial_out.reshape(per_device, span_count, own_blocks, part_rows, head_depth)
    shaped_max = maxima.reshape(per_device, span_count, own_blocks, part_rows)
    shaped_total = totals.reshape(per_device, span_count, own_blocks, part_rows)
    got_out, got_max, got_total = (
        lax.all_to_all(shaped_out, "blk", split_axis=1, concat_axis=1, tiled=True),
        lax.all_to_all(shaped_max, "blk", split_axis=1, concat_axis=1, tiled=True),
        lax.all_to_all(shaped_total, "blk", split_axis=1, concat_axis=1, tiled=True),
    )
    attended_items = combine_spans(got_out, got_max, got_total, 1)
    attended_items = attended_items.reshape(
        per_device, seq_devices * local_blocks * part_rows, head_depth
    )
    returned = lax.all_to_all(attended_items, "seq", split_axis=1, concat_axis=0, tiled=True)
    grid_out = returned.reshape(head_count, row_parts, local_blocks, part_rows, head_depth)
    grid_out = jnp.swapaxes(grid_out, 0, 1)
    return grid_out.transpose(2, 0, 3, 1, 4).reshape(local_rows, head_count * head_depth)


def own_place(axes):
    place = 0
    for axis in axes:
        place = place * lax.axis_size(axis) + lax.axis_index(axis)
    return place


def each_light_block(kept_ref, block):
    return [
        kept_ref[block, span * KEEP + slot]
        for span in range(kept_ref.shape[1] // KEEP)
        for slot in range(LIGHT)
    ]


def pack_kernel(*refs):
    sources, (out_ref, landed, sems) = refs[:-3], refs[-3:]
    heads = out_ref.shape[0]
    rows = landed.shape[1]
    pieces = sems.shape[1]
    piece_rows = rows // pieces
    arrivals = [
        [
            pltpu.make_async_copy(
                source.at[pl.ds(piece * piece_rows, piece_rows), :],
                landed.at[place, pl.ds(piece * piece_rows, piece_rows), :],
                sems.at[place, piece],
            )
            for piece in range(pieces)
        ]
        for place, source in enumerate(sources)
    ]
    for copies in arrivals:
        for copy in copies:
            copy.start()
    for place, copies in enumerate(arrivals):
        for piece, copy in enumerate(copies):
            copy.wait()
            kept_rows = slice(piece * piece_rows, (piece + 1) * piece_rows)
            for head in range(heads):
                out_ref[head, place, kept_rows, :] = landed[
                    place, kept_rows, head * HD : (head + 1) * HD
                ]


def pack_heads(*sources):
    count = len(sources)
    rows = sources[0].shape[0]
    pieces = 4
    return pl.pallas_call(
        pack_kernel,
        out_shape=jax.ShapeDtypeStruct((HEADS, count, rows, HD), jnp.bfloat16),
        in_specs=[pl.BlockSpec(memory_space=pltpu.HBM)] * count,
        out_specs=pl.BlockSpec(memory_space=pltpu.VMEM),
        scratch_shapes=[
            pltpu.VMEM((count, rows, HEADS * HD), jnp.bfloat16),
            pltpu.SemaphoreType.DMA((count, pieces)),
        ],
        compiler_params=pltpu.CompilerParams(vmem_limit_bytes=8 * 1024 * 1024),
        name="pack_heads",
    )(*[pltpu.with_memory_space_constraint(source, pltpu.HBM) for source in sources])


def unpack_kernel(held_ref, out_ref, sems):
    copies = [
        pltpu.make_async_copy(
            held_ref.at[head], out_ref.at[:, head * HD : (head + 1) * HD], sems.at[head]
        )
        for head in range(held_ref.shape[0])
    ]
    for copy in copies:
        copy.start()
    for copy in copies:
        copy.wait()


def unpack_heads(held):
    heads, rows, depth = held.shape
    return pl.pallas_call(
        unpack_kernel,
        out_shape=jax.ShapeDtypeStruct((rows, heads * depth), jnp.bfloat16),
        in_specs=[pl.BlockSpec(memory_space=pl.ANY)],
        out_specs=pl.BlockSpec(memory_space=pltpu.HBM),
        scratch_shapes=[pltpu.SemaphoreType.DMA((heads,))],
        compiler_params=pltpu.CompilerParams(vmem_limit_bytes=4 * 1024 * 1024),
        name="unpack_heads",
    )(held)


def pipelined(count, prepare, score, weigh, blend):
    score(0, 0)
    prepare()
    weigh(0, 0)
    score(1, 1)

    def step(j, carry):
        blend(2 * j, 0)
        weigh(2 * j + 1, 1)
        score(2 * j + 2, 0)
        blend(2 * j + 1, 1)
        weigh(2 * j + 2, 0)
        score(2 * j + 3, 1)
        return carry

    lax.fori_loop(0, count // 2 - 1, step, 0)
    blend(count - 2, 0)
    weigh(count - 1, 1)
    blend(count - 1, 1)


def attend_kernel(axes, kept_hbm, class_ref, qkv_ref, out_ref, *scratch):
    kept_ref, k_turned, v_all, logits_a, logits_b, weights_a, weights_b, sem = scratch
    logits_slots = (logits_a, logits_b)
    weights_slots = (weights_a, weights_b)
    block_count = qkv_ref.shape[0]
    me = own_place(axes)
    exponent_scale = math.log2(math.e) / math.sqrt(HD)
    kept_copy = pltpu.make_async_copy(kept_hbm.at[me], kept_ref, sem)
    kept_copy.start()
    for block in range(block_count):
        k_turned[:, block * BLOCK : (block + 1) * BLOCK] = qkv_ref[block, 1].T

    def set_values():
        v_all[:, :, :HD] = qkv_ref[:, 2]
        v_all[:, :, HD:] = jnp.ones((block_count, BLOCK, HD), jnp.bfloat16)

    def key_columns(block):
        return k_turned[:, pl.ds(pl.multiple_of(block * BLOCK, BLOCK), BLOCK)]

    def weigh(rows, columns, slot):
        logits = logits_slots[slot][:rows, :columns]
        largest = jnp.max(logits, axis=-1, keepdims=True)
        weights = jnp.exp2((logits - largest) * exponent_scale).astype(jnp.bfloat16)
        weights_slots[slot][:rows, :columns] = weights

    def normalized(summed):
        return (summed[:, :HD] / summed[:, HD:]).astype(jnp.bfloat16)

    @pl.when(class_ref[me] == 1)
    def _():
        group = 4

        def score(i, slot):
            query_rows = qkv_ref[pl.ds(group * i, group), 0].reshape(group * BLOCK, HD)
            logits_slots[slot][...] = jnp.dot(
                query_rows, k_turned[...], preferred_element_type=jnp.float32
            )

        def blend(i, slot):
            value_rows = v_all[...].reshape(block_count * BLOCK, 2 * HD)
            out = normalized(
                jnp.dot(weights_slots[slot][...], value_rows, preferred_element_type=jnp.float32)
            )
            out_ref[pl.ds(group * i, group)] = out.reshape(group, BLOCK, HD)

        def weigh_all(i, slot):
            weigh(group * BLOCK, block_count * BLOCK, slot)

        pipelined(block_count // group, set_values, score, weigh_all, blend)
        kept_copy.wait()

    @pl.when(class_ref[me] != 1)
    def _():
        kept_copy.wait()
        group = 2

        def block_pairs(block):
            kept_blocks = each_light_block(kept_ref, block)
            return list(zip(kept_blocks[::2], kept_blocks[1::2]))

        def score(i, slot):
            for member in range(group):
                block = group * i + member
                rows = slice(member * BLOCK, (member + 1) * BLOCK)
                for place, (one, other) in enumerate(block_pairs(block)):
                    pair = jnp.concatenate([key_columns(one), key_columns(other)], axis=1)
                    columns = slice(place * 2 * BLOCK, (place + 1) * 2 * BLOCK)
                    logits_slots[slot][rows, columns] = jnp.dot(
                        qkv_ref[block, 0], pair, preferred_element_type=jnp.float32
                    )

        def blend(i, slot):
            for member in range(group):
                block = group * i + member
                rows = slice(member * BLOCK, (member + 1) * BLOCK)
                summed = jnp.zeros((BLOCK, 2 * HD), jnp.float32)
                for place, (one, other) in enumerate(block_pairs(block)):
                    value_rows = jnp.concatenate([v_all[one], v_all[other]], axis=0)
                    columns = slice(place * 2 * BLOCK, (place + 1) * 2 * BLOCK)
                    weights = weights_slots[slot][rows, columns]
                    summed += jnp.dot(weights, value_rows, preferred_element_type=jnp.float32)
                out_ref[block] = normalized(summed)

        def weigh_few(i, slot):
            weigh(group * BLOCK, block_count // KEEP * LIGHT * BLOCK, slot)

        pipelined(block_count // group, set_values, score, weigh_few, blend)


def heads_by_device(queries, keys, values, kept, dense_class):
    axes = ("seq", "blk")
    block_count = kept.shape[1]
    in_vmem = pl.BlockSpec(memory_space=pltpu.VMEM)

    def exchange(send):
        return lax.all_to_all(send, axes, split_axis=0, concat_axis=0, tiled=True)

    held = exchange(pack_heads(queries, keys, values))
    attended = pl.pallas_call(
        lambda *refs: attend_kernel(axes, *refs),
        out_shape=jax.ShapeDtypeStruct((block_count, BLOCK, HD), jnp.bfloat16),
        in_specs=[
            pl.BlockSpec(memory_space=pl.ANY),
            pl.BlockSpec(memory_space=pltpu.SMEM),
            in_vmem,
        ],
        out_specs=in_vmem,
        scratch_shapes=[
            pltpu.SMEM(kept.shape[1:], jnp.int32),
            pltpu.VMEM((HD, block_count * BLOCK), jnp.bfloat16),
            pltpu.VMEM((block_count, BLOCK, 2 * HD), jnp.bfloat16),
            pltpu.VMEM((4 * BLOCK, block_count * BLOCK), jnp.float32),
            pltpu.VMEM((4 * BLOCK, block_count * BLOCK), jnp.float32),
            pltpu.VMEM((4 * BLOCK, block_count * BLOCK), jnp.bfloat16),
            pltpu.VMEM((4 * BLOCK, block_count * BLOCK), jnp.bfloat16),
            pltpu.SemaphoreType.DMA,
        ],
        compiler_params=pltpu.CompilerParams(vmem_limit_bytes=32 * 1024 * 1024),
        name="attend_head",
    )(kept, dense_class, held)
    return unpack_heads(exchange(attended))


def shards(queries, keys, values, kept, dense_class):
    devices = lax.axis_size("seq") * lax.axis_size("blk")
    one_head_each = devices == HEADS
    one_block_each = queries.shape[0] == BLOCK
    every_block_kept = kept.shape[1] == kept.shape[2]
    if one_head_each and one_block_each and every_block_kept:
        return heads_by_device(queries, keys, values, kept, dense_class)
    return spans_by_device(queries, keys, values, kept, dense_class)


def solution(mesh):
    return jax.shard_map(
        shards,
        mesh=mesh,
        in_specs=(
            P(("clip", "seq", "blk"), None),
            P(("clip", "seq", "blk"), None),
            P(("clip", "seq", "blk"), None),
            P(),
            P(),
        ),
        out_specs=P(("clip", "seq", "blk"), None),
        check_vma=False,
    )
```

```python
import math

import jax
import jax.numpy as jnp
from jax import lax
from jax.experimental import pallas as pl
from jax.experimental.pallas import tpu as pltpu
from jax.sharding import PartitionSpec as P

HEADS = 16
HD = 128
BLOCK = 128
KEEP = 4
LIGHT = 2


def combine_spans(partial_out, maxima, totals, along):
    largest = jnp.max(maxima, axis=along, keepdims=True)
    factor = jnp.exp(maxima - largest)
    numerator = jnp.sum(factor[..., None] * partial_out, axis=along)
    denominator = jnp.sum(factor * totals, axis=along)
    return (numerator / denominator[..., None]).astype(jnp.bfloat16)


def attend_blocks(query_rows, key_blocks, blocked_value_rows, local_ids, slot_count):
    query_blocks, part_rows, head_depth = query_rows.shape
    group_size = query_blocks
    while group_size * part_rows > 512 and group_size % 2 == 0:
        group_size = group_size // 2
    logit_scale_factor = 1.0 / math.sqrt(head_depth)
    block_rows = key_blocks.shape[1]

    def one_group(operands):
        queries_group, ids_group = operands
        collected_key_blocks = key_blocks[ids_group].reshape(
            group_size, slot_count * block_rows, head_depth
        )
        gathered_v = blocked_value_rows[ids_group].reshape(
            group_size, slot_count * block_rows, head_depth
        )
        attention_logits = (
            jnp.einsum(
                "gpd,gkd->gpk",
                queries_group,
                collected_key_blocks,
                preferred_element_type=jnp.float32,
            )
            * logit_scale_factor
        )
        maxima = jnp.max(attention_logits, axis=-1)
        weights = jnp.exp(attention_logits - maxima[..., None])
        totals = jnp.sum(weights, axis=-1)
        partial_out = jnp.einsum(
            "gpk,gkd->gpd",
            weights.astype(jnp.bfloat16),
            gathered_v,
            preferred_element_type=jnp.float32,
        )
        return (partial_out, maxima, totals)

    grouped_q = query_rows.reshape(query_blocks // group_size, group_size, part_rows, head_depth)
    grouped_ids = local_ids[:, :slot_count].reshape(
        query_blocks // group_size, group_size, slot_count
    )
    partial_out, maxima, totals = lax.map(one_group, (grouped_q, grouped_ids))
    return (
        partial_out.reshape(query_blocks, part_rows, head_depth),
        maxima.reshape(query_blocks, part_rows),
        totals.reshape(query_blocks, part_rows),
    )


def arrange_heads(stacked):
    swapped = jnp.swapaxes(stacked, 0, 1)
    return swapped.reshape((-1,) + stacked.shape[2:])


def spans_by_device(queries, keys, values, kept, dense_class):
    seq_devices = lax.axis_size("seq")
    span_count = lax.axis_size("blk")
    local_rows = queries.shape[0]
    head_count = HEADS
    head_depth = HD
    local_blocks = local_rows // BLOCK
    row_parts = max(1, 2 * seq_devices // head_count)
    part_rows = BLOCK // row_parts
    item_count = head_count * row_parts
    per_device = item_count // seq_devices
    seq_place = lax.axis_index("seq")
    blk_place = lax.axis_index("blk")
    every_item = jnp.arange(item_count, dtype=jnp.int32)
    all_item_heads = every_item // row_parts
    item_heads = lax.dynamic_slice_in_dim(all_item_heads, seq_place * per_device, per_device)
    grid_q = queries.reshape(local_blocks, row_parts, part_rows, head_count, head_depth).transpose(
        1, 3, 0, 2, 4
    )
    grid_q = grid_q.reshape(row_parts, head_count, local_blocks * part_rows, head_depth)
    head_keys = keys.reshape(local_rows, head_count, head_depth).transpose(1, 0, 2)
    head_values = values.reshape(local_rows, head_count, head_depth).transpose(1, 0, 2)
    send_q = arrange_heads(grid_q)
    q_items = lax.all_to_all(send_q, "seq", split_axis=0, concat_axis=1, tiled=True)
    stride = 1
    grid_k = jnp.broadcast_to(head_keys[None], (row_parts, head_count, local_rows, head_depth))
    grid_v = jnp.broadcast_to(head_values[None], (row_parts, head_count, local_rows, head_depth))
    send_k = arrange_heads(grid_k)
    send_v = arrange_heads(grid_v)
    k_held, v_held = (
        lax.all_to_all(send_k, "seq", split_axis=0, concat_axis=1, tiled=True),
        lax.all_to_all(send_v, "seq", split_axis=0, concat_axis=1, tiled=True),
    )
    key_blocks = k_held.reshape(per_device, seq_devices * local_blocks, BLOCK, head_depth)
    blocked_value_rows = v_held.reshape(per_device, seq_devices * local_blocks, BLOCK, head_depth)
    item_slot = jnp.arange(per_device, dtype=jnp.int32) // stride
    item_class = jnp.take(dense_class, item_heads)
    item_kept = jnp.take(kept, item_heads, axis=0)
    source_index = jnp.arange(seq_devices, dtype=jnp.int32)
    block_index = jnp.arange(local_blocks, dtype=jnp.int32)
    span_index = jnp.arange(span_count, dtype=jnp.int32)
    all_ids = (
        (source_index[None, :, None] * span_count + span_index[:, None, None]) * local_blocks
        + block_index[None, None, :]
    ).reshape(-1)
    all_kept = jnp.take(item_kept, all_ids, axis=1)
    span_ids = lax.dynamic_slice_in_dim(all_kept, blk_place * KEEP, KEEP, axis=2)
    q_all = lax.all_gather(q_items, "blk", axis=1, tiled=True)
    query_rows = q_all.reshape(
        per_device, span_count * seq_devices * local_blocks, part_rows, head_depth
    )

    def one_item(operands):
        rows_item, ids_item, class_item, slot_item = operands
        keys_item = lax.dynamic_index_in_dim(key_blocks, slot_item, 0, keepdims=False)
        values_item = lax.dynamic_index_in_dim(blocked_value_rows, slot_item, 0, keepdims=False)
        return lax.cond(
            class_item == 1,
            lambda: attend_blocks(rows_item, keys_item, values_item, ids_item, KEEP),
            lambda: attend_blocks(rows_item, keys_item, values_item, ids_item, LIGHT),
        )

    partial_out, maxima, totals = lax.map(
        one_item,
        (
            query_rows,
            span_ids // (local_blocks * span_count) * local_blocks + span_ids % local_blocks,
            item_class,
            item_slot,
        ),
    )
    own_blocks = seq_devices * local_blocks
    shaped_out = partial_out.reshape(per_device, span_count, own_blocks, part_rows, head_depth)
    shaped_max = maxima.reshape(per_device, span_count, own_blocks, part_rows)
    shaped_total = totals.reshape(per_device, span_count, own_blocks, part_rows)
    got_out, got_max, got_total = (
        lax.all_to_all(shaped_out, "blk", split_axis=1, concat_axis=1, tiled=True),
        lax.all_to_all(shaped_max, "blk", split_axis=1, concat_axis=1, tiled=True),
        lax.all_to_all(shaped_total, "blk", split_axis=1, concat_axis=1, tiled=True),
    )
    attended_items = combine_spans(got_out, got_max, got_total, 1)
    attended_items = attended_items.reshape(
        per_device, seq_devices * local_blocks * part_rows, head_depth
    )
    returned = lax.all_to_all(attended_items, "seq", split_axis=1, concat_axis=0, tiled=True)
    grid_out = returned.reshape(head_count, row_parts, local_blocks, part_rows, head_depth)
    grid_out = jnp.swapaxes(grid_out, 0, 1)
    return grid_out.transpose(2, 0, 3, 1, 4).reshape(local_rows, head_count * head_depth)


def own_place(axes):
    place = 0
    for axis in axes:
        place = place * lax.axis_size(axis) + lax.axis_index(axis)
    return place


def each_light_block(kept_ref, block):
    return [
        kept_ref[block, span * KEEP + slot]
        for span in range(kept_ref.shape[1] // KEEP)
        for slot in range(LIGHT)
    ]


def pack_kernel(*refs):
    sources, (out_ref, landed, sems) = refs[:-3], refs[-3:]
    heads = out_ref.shape[0]
    rows = landed.shape[1]
    pieces = sems.shape[1]
    piece_rows = rows // pieces
    arrivals = [
        [
            pltpu.make_async_copy(
                source.at[pl.ds(piece * piece_rows, piece_rows), :],
                landed.at[place, pl.ds(piece * piece_rows, piece_rows), :],
                sems.at[place, piece],
            )
            for piece in range(pieces)
        ]
        for place, source in enumerate(sources)
    ]
    for copies in arrivals:
        for copy in copies:
            copy.start()
    for place, copies in enumerate(arrivals):
        for piece, copy in enumerate(copies):
            copy.wait()
            kept_rows = slice(piece * piece_rows, (piece + 1) * piece_rows)
            for head in range(heads):
                out_ref[head, place, kept_rows, :] = landed[
                    place, kept_rows, head * HD : (head + 1) * HD
                ]


def pack_heads(*sources):
    count = len(sources)
    rows = sources[0].shape[0]
    pieces = 4
    return pl.pallas_call(
        pack_kernel,
        out_shape=jax.ShapeDtypeStruct((HEADS, count, rows, HD), jnp.bfloat16),
        in_specs=[pl.BlockSpec(memory_space=pltpu.HBM)] * count,
        out_specs=pl.BlockSpec(memory_space=pltpu.VMEM),
        scratch_shapes=[
            pltpu.VMEM((count, rows, HEADS * HD), jnp.bfloat16),
            pltpu.SemaphoreType.DMA((count, pieces)),
        ],
        compiler_params=pltpu.CompilerParams(vmem_limit_bytes=8 * 1024 * 1024),
        name="pack_heads",
    )(*[pltpu.with_memory_space_constraint(source, pltpu.HBM) for source in sources])


def unpack_kernel(held_ref, out_ref, sems):
    copies = [
        pltpu.make_async_copy(
            held_ref.at[head], out_ref.at[:, head * HD : (head + 1) * HD], sems.at[head]
        )
        for head in range(held_ref.shape[0])
    ]
    for copy in copies:
        copy.start()
    for copy in copies:
        copy.wait()


def unpack_heads(held):
    heads, rows, depth = held.shape
    return pl.pallas_call(
        unpack_kernel,
        out_shape=jax.ShapeDtypeStruct((rows, heads * depth), jnp.bfloat16),
        in_specs=[pl.BlockSpec(memory_space=pl.ANY)],
        out_specs=pl.BlockSpec(memory_space=pltpu.HBM),
        scratch_shapes=[pltpu.SemaphoreType.DMA((heads,))],
        compiler_params=pltpu.CompilerParams(vmem_limit_bytes=4 * 1024 * 1024),
        name="unpack_heads",
    )(held)


def pipelined(count, prepare, score, weigh, blend):
    score(0, 0)
    prepare()
    weigh(0, 0)
    score(1, 1)

    def step(j, carry):
        blend(2 * j, 0)
        weigh(2 * j + 1, 1)
        score(2 * j + 2, 0)
        blend(2 * j + 1, 1)
        weigh(2 * j + 2, 0)
        score(2 * j + 3, 1)
        return carry

    lax.fori_loop(0, count // 2 - 1, step, 0)
    blend(count - 2, 0)
    weigh(count - 1, 1)
    blend(count - 1, 1)


def attend_kernel(axes, kept_hbm, class_ref, qkv_ref, out_ref, *scratch):
    kept_ref, v_all, logits_a, logits_b, weights_a, weights_b, sem = scratch
    logits_slots = (logits_a, logits_b)
    weights_slots = (weights_a, weights_b)
    block_count = qkv_ref.shape[0]
    me = own_place(axes)
    exponent_scale = math.log2(math.e) / math.sqrt(HD)
    kept_copy = pltpu.make_async_copy(kept_hbm.at[me], kept_ref, sem)
    kept_copy.start()

    def set_values():
        v_all[:, :, :HD] = qkv_ref[:, 2]
        v_all[:, :, HD:] = jnp.ones((block_count, BLOCK, HD), jnp.bfloat16)

    def scores(query_rows, key_rows):
        return lax.dot_general(
            query_rows, key_rows, (((1,), (1,)), ((), ())), preferred_element_type=jnp.float32
        )

    def weigh(rows, columns, slot):
        logits = logits_slots[slot][:rows, :columns]
        largest = jnp.max(logits, axis=-1, keepdims=True)
        weights = jnp.exp2((logits - largest) * exponent_scale).astype(jnp.bfloat16)
        weights_slots[slot][:rows, :columns] = weights

    def normalized(summed):
        return (summed[:, :HD] / summed[:, HD:]).astype(jnp.bfloat16)

    @pl.when(class_ref[me] == 1)
    def _():
        sizes = [2] + [4] * (block_count // 4 - 1) + [2]
        starts = [sum(sizes[:i]) for i in range(len(sizes))]

        def score(i):
            rows = sizes[i] * BLOCK
            query_rows = qkv_ref[starts[i] : starts[i] + sizes[i], 0].reshape(rows, HD)
            key_rows = qkv_ref[:, 1].reshape(block_count * BLOCK, HD)
            logits_slots[i % 2][:rows, :] = scores(query_rows, key_rows)

        def weigh_all(i):
            weigh(sizes[i] * BLOCK, block_count * BLOCK, i % 2)

        def blend(i):
            rows = sizes[i] * BLOCK
            value_rows = v_all[...].reshape(block_count * BLOCK, 2 * HD)
            weights = weights_slots[i % 2][:rows, :]
            out = normalized(jnp.dot(weights, value_rows, preferred_element_type=jnp.float32))
            out_ref[starts[i] : starts[i] + sizes[i]] = out.reshape(sizes[i], BLOCK, HD)

        score(0)
        set_values()
        weigh_all(0)
        score(1)
        for i in range(1, len(sizes)):
            blend(i - 1)
            weigh_all(i)
            if i + 1 < len(sizes):
                score(i + 1)
        blend(len(sizes) - 1)
        kept_copy.wait()

    @pl.when(class_ref[me] != 1)
    def _():
        kept_copy.wait()
        group = 2

        def block_pairs(block):
            kept_blocks = each_light_block(kept_ref, block)
            return list(zip(kept_blocks[::2], kept_blocks[1::2]))

        def score(i, slot):
            for member in range(group):
                block = group * i + member
                rows = slice(member * BLOCK, (member + 1) * BLOCK)
                for place, (one, other) in enumerate(block_pairs(block)):
                    key_rows = jnp.concatenate([qkv_ref[one, 1], qkv_ref[other, 1]], axis=0)
                    columns = slice(place * 2 * BLOCK, (place + 1) * 2 * BLOCK)
                    logits_slots[slot][rows, columns] = scores(qkv_ref[block, 0], key_rows)

        def blend(i, slot):
            for member in range(group):
                block = group * i + member
                rows = slice(member * BLOCK, (member + 1) * BLOCK)
                summed = jnp.zeros((BLOCK, 2 * HD), jnp.float32)
                for place, (one, other) in enumerate(block_pairs(block)):
                    value_rows = jnp.concatenate([v_all[one], v_all[other]], axis=0)
                    columns = slice(place * 2 * BLOCK, (place + 1) * 2 * BLOCK)
                    weights = weights_slots[slot][rows, columns]
                    summed += jnp.dot(weights, value_rows, preferred_element_type=jnp.float32)
                out_ref[block] = normalized(summed)

        def weigh_few(i, slot):
            weigh(group * BLOCK, block_count // KEEP * LIGHT * BLOCK, slot)

        pipelined(block_count // group, set_values, score, weigh_few, blend)


def heads_by_device(queries, keys, values, kept, dense_class):
    axes = ("seq", "blk")
    block_count = kept.shape[1]
    in_vmem = pl.BlockSpec(memory_space=pltpu.VMEM)

    def exchange(send):
        return lax.all_to_all(send, axes, split_axis=0, concat_axis=0, tiled=True)

    held = exchange(pack_heads(queries, keys, values))
    attended = pl.pallas_call(
        lambda *refs: attend_kernel(axes, *refs),
        out_shape=jax.ShapeDtypeStruct((block_count, BLOCK, HD), jnp.bfloat16),
        in_specs=[
            pl.BlockSpec(memory_space=pl.ANY),
            pl.BlockSpec(memory_space=pltpu.SMEM),
            in_vmem,
        ],
        out_specs=in_vmem,
        scratch_shapes=[
            pltpu.SMEM(kept.shape[1:], jnp.int32),
            pltpu.VMEM((block_count, BLOCK, 2 * HD), jnp.bfloat16),
            pltpu.VMEM((4 * BLOCK, block_count * BLOCK), jnp.float32),
            pltpu.VMEM((4 * BLOCK, block_count * BLOCK), jnp.float32),
            pltpu.VMEM((4 * BLOCK, block_count * BLOCK), jnp.bfloat16),
            pltpu.VMEM((4 * BLOCK, block_count * BLOCK), jnp.bfloat16),
            pltpu.SemaphoreType.DMA,
        ],
        compiler_params=pltpu.CompilerParams(vmem_limit_bytes=32 * 1024 * 1024),
        name="attend_head",
    )(kept, dense_class, held)
    return unpack_heads(exchange(attended))


def shards(queries, keys, values, kept, dense_class):
    devices = lax.axis_size("seq") * lax.axis_size("blk")
    one_head_each = devices == HEADS
    one_block_each = queries.shape[0] == BLOCK
    every_block_kept = kept.shape[1] == kept.shape[2]
    if one_head_each and one_block_each and every_block_kept:
        return heads_by_device(queries, keys, values, kept, dense_class)
    return spans_by_device(queries, keys, values, kept, dense_class)


def solution(mesh):
    return jax.shard_map(
        shards,
        mesh=mesh,
        in_specs=(
            P(("clip", "seq", "blk"), None),
            P(("clip", "seq", "blk"), None),
            P(("clip", "seq", "blk"), None),
            P(),
            P(),
        ),
        out_specs=P(("clip", "seq", "blk"), None),
        check_vma=False,
    )
```

```python
import math

import jax
import jax.numpy as jnp
from jax import lax
from jax.experimental import pallas as pl
from jax.experimental.pallas import tpu as pltpu
from jax.sharding import PartitionSpec as P

HEADS = 16
HD = 128
BLOCK = 128
KEEP = 4
LIGHT = 2


def combine_spans(partial_out, maxima, totals, along):
    largest = jnp.max(maxima, axis=along, keepdims=True)
    factor = jnp.exp(maxima - largest)
    numerator = jnp.sum(factor[..., None] * partial_out, axis=along)
    denominator = jnp.sum(factor * totals, axis=along)
    return (numerator / denominator[..., None]).astype(jnp.bfloat16)


def attend_blocks(query_rows, key_blocks, blocked_value_rows, local_ids, slot_count):
    query_blocks, part_rows, head_depth = query_rows.shape
    group_size = query_blocks
    while group_size * part_rows > 512 and group_size % 2 == 0:
        group_size = group_size // 2
    logit_scale_factor = 1.0 / math.sqrt(head_depth)
    block_rows = key_blocks.shape[1]

    def one_group(operands):
        queries_group, ids_group = operands
        collected_key_blocks = key_blocks[ids_group].reshape(
            group_size, slot_count * block_rows, head_depth
        )
        gathered_v = blocked_value_rows[ids_group].reshape(
            group_size, slot_count * block_rows, head_depth
        )
        attention_logits = (
            jnp.einsum(
                "gpd,gkd->gpk",
                queries_group,
                collected_key_blocks,
                preferred_element_type=jnp.float32,
            )
            * logit_scale_factor
        )
        maxima = jnp.max(attention_logits, axis=-1)
        weights = jnp.exp(attention_logits - maxima[..., None])
        totals = jnp.sum(weights, axis=-1)
        partial_out = jnp.einsum(
            "gpk,gkd->gpd",
            weights.astype(jnp.bfloat16),
            gathered_v,
            preferred_element_type=jnp.float32,
        )
        return (partial_out, maxima, totals)

    grouped_q = query_rows.reshape(query_blocks // group_size, group_size, part_rows, head_depth)
    grouped_ids = local_ids[:, :slot_count].reshape(
        query_blocks // group_size, group_size, slot_count
    )
    partial_out, maxima, totals = lax.map(one_group, (grouped_q, grouped_ids))
    return (
        partial_out.reshape(query_blocks, part_rows, head_depth),
        maxima.reshape(query_blocks, part_rows),
        totals.reshape(query_blocks, part_rows),
    )


def arrange_heads(stacked):
    swapped = jnp.swapaxes(stacked, 0, 1)
    return swapped.reshape((-1,) + stacked.shape[2:])


def spans_by_device(queries, keys, values, kept, dense_class):
    seq_devices = lax.axis_size("seq")
    span_count = lax.axis_size("blk")
    local_rows = queries.shape[0]
    head_count = HEADS
    head_depth = HD
    local_blocks = local_rows // BLOCK
    row_parts = max(1, 2 * seq_devices // head_count)
    part_rows = BLOCK // row_parts
    item_count = head_count * row_parts
    per_device = item_count // seq_devices
    seq_place = lax.axis_index("seq")
    blk_place = lax.axis_index("blk")
    every_item = jnp.arange(item_count, dtype=jnp.int32)
    all_item_heads = every_item // row_parts
    item_heads = lax.dynamic_slice_in_dim(all_item_heads, seq_place * per_device, per_device)
    grid_q = queries.reshape(local_blocks, row_parts, part_rows, head_count, head_depth).transpose(
        1, 3, 0, 2, 4
    )
    grid_q = grid_q.reshape(row_parts, head_count, local_blocks * part_rows, head_depth)
    head_keys = keys.reshape(local_rows, head_count, head_depth).transpose(1, 0, 2)
    head_values = values.reshape(local_rows, head_count, head_depth).transpose(1, 0, 2)
    send_q = arrange_heads(grid_q)
    q_items = lax.all_to_all(send_q, "seq", split_axis=0, concat_axis=1, tiled=True)
    stride = 1
    grid_k = jnp.broadcast_to(head_keys[None], (row_parts, head_count, local_rows, head_depth))
    grid_v = jnp.broadcast_to(head_values[None], (row_parts, head_count, local_rows, head_depth))
    send_k = arrange_heads(grid_k)
    send_v = arrange_heads(grid_v)
    k_held, v_held = (
        lax.all_to_all(send_k, "seq", split_axis=0, concat_axis=1, tiled=True),
        lax.all_to_all(send_v, "seq", split_axis=0, concat_axis=1, tiled=True),
    )
    key_blocks = k_held.reshape(per_device, seq_devices * local_blocks, BLOCK, head_depth)
    blocked_value_rows = v_held.reshape(per_device, seq_devices * local_blocks, BLOCK, head_depth)
    item_slot = jnp.arange(per_device, dtype=jnp.int32) // stride
    item_class = jnp.take(dense_class, item_heads)
    item_kept = jnp.take(kept, item_heads, axis=0)
    source_index = jnp.arange(seq_devices, dtype=jnp.int32)
    block_index = jnp.arange(local_blocks, dtype=jnp.int32)
    span_index = jnp.arange(span_count, dtype=jnp.int32)
    all_ids = (
        (source_index[None, :, None] * span_count + span_index[:, None, None]) * local_blocks
        + block_index[None, None, :]
    ).reshape(-1)
    all_kept = jnp.take(item_kept, all_ids, axis=1)
    span_ids = lax.dynamic_slice_in_dim(all_kept, blk_place * KEEP, KEEP, axis=2)
    q_all = lax.all_gather(q_items, "blk", axis=1, tiled=True)
    query_rows = q_all.reshape(
        per_device, span_count * seq_devices * local_blocks, part_rows, head_depth
    )

    def one_item(operands):
        rows_item, ids_item, class_item, slot_item = operands
        keys_item = lax.dynamic_index_in_dim(key_blocks, slot_item, 0, keepdims=False)
        values_item = lax.dynamic_index_in_dim(blocked_value_rows, slot_item, 0, keepdims=False)
        return lax.cond(
            class_item == 1,
            lambda: attend_blocks(rows_item, keys_item, values_item, ids_item, KEEP),
            lambda: attend_blocks(rows_item, keys_item, values_item, ids_item, LIGHT),
        )

    partial_out, maxima, totals = lax.map(
        one_item,
        (
            query_rows,
            span_ids // (local_blocks * span_count) * local_blocks + span_ids % local_blocks,
            item_class,
            item_slot,
        ),
    )
    own_blocks = seq_devices * local_blocks
    shaped_out = partial_out.reshape(per_device, span_count, own_blocks, part_rows, head_depth)
    shaped_max = maxima.reshape(per_device, span_count, own_blocks, part_rows)
    shaped_total = totals.reshape(per_device, span_count, own_blocks, part_rows)
    got_out, got_max, got_total = (
        lax.all_to_all(shaped_out, "blk", split_axis=1, concat_axis=1, tiled=True),
        lax.all_to_all(shaped_max, "blk", split_axis=1, concat_axis=1, tiled=True),
        lax.all_to_all(shaped_total, "blk", split_axis=1, concat_axis=1, tiled=True),
    )
    attended_items = combine_spans(got_out, got_max, got_total, 1)
    attended_items = attended_items.reshape(
        per_device, seq_devices * local_blocks * part_rows, head_depth
    )
    returned = lax.all_to_all(attended_items, "seq", split_axis=1, concat_axis=0, tiled=True)
    grid_out = returned.reshape(head_count, row_parts, local_blocks, part_rows, head_depth)
    grid_out = jnp.swapaxes(grid_out, 0, 1)
    return grid_out.transpose(2, 0, 3, 1, 4).reshape(local_rows, head_count * head_depth)


def own_place(axes):
    place = 0
    for axis in axes:
        place = place * lax.axis_size(axis) + lax.axis_index(axis)
    return place


def each_light_block(kept_ref, block):
    return [
        kept_ref[block, span * KEEP + slot]
        for span in range(kept_ref.shape[1] // KEEP)
        for slot in range(LIGHT)
    ]


def pack_kernel(*refs):
    sources, (out_ref, landed, sems) = refs[:-3], refs[-3:]
    heads = out_ref.shape[0]
    rows = landed.shape[1]
    pieces = sems.shape[1]
    piece_rows = rows // pieces
    arrivals = [
        [
            pltpu.make_async_copy(
                source.at[pl.ds(piece * piece_rows, piece_rows), :],
                landed.at[place, pl.ds(piece * piece_rows, piece_rows), :],
                sems.at[place, piece],
            )
            for piece in range(pieces)
        ]
        for place, source in enumerate(sources)
    ]
    for copies in arrivals:
        for copy in copies:
            copy.start()
    for place, copies in enumerate(arrivals):
        for piece, copy in enumerate(copies):
            copy.wait()
            kept_rows = slice(piece * piece_rows, (piece + 1) * piece_rows)
            for head in range(heads):
                out_ref[head, place, kept_rows, :] = landed[
                    place, kept_rows, head * HD : (head + 1) * HD
                ]


def pack_heads(*sources):
    count = len(sources)
    rows = sources[0].shape[0]
    pieces = 4
    return pl.pallas_call(
        pack_kernel,
        out_shape=jax.ShapeDtypeStruct((HEADS, count, rows, HD), jnp.bfloat16),
        in_specs=[pl.BlockSpec(memory_space=pltpu.HBM)] * count,
        out_specs=pl.BlockSpec(memory_space=pltpu.VMEM),
        scratch_shapes=[
            pltpu.VMEM((count, rows, HEADS * HD), jnp.bfloat16),
            pltpu.SemaphoreType.DMA((count, pieces)),
        ],
        compiler_params=pltpu.CompilerParams(vmem_limit_bytes=8 * 1024 * 1024),
        name="pack_heads",
    )(*[pltpu.with_memory_space_constraint(source, pltpu.HBM) for source in sources])


def unpack_kernel(held_ref, out_ref, turned, sems):
    heads = held_ref.shape[0]
    pieces = sems.shape[0]
    piece_rows = turned.shape[0] // pieces
    departures = []
    for piece in range(pieces):
        rows = slice(piece * piece_rows, (piece + 1) * piece_rows)
        for head in range(heads):
            turned[rows, head * HD : (head + 1) * HD] = held_ref[head, rows, :]
        departure = pltpu.make_async_copy(
            turned.at[pl.ds(piece * piece_rows, piece_rows), :],
            out_ref.at[pl.ds(piece * piece_rows, piece_rows), :],
            sems.at[piece],
        )
        departure.start()
        departures.append(departure)
    for departure in departures:
        departure.wait()


def unpack_heads(held):
    heads, rows, depth = held.shape
    return pl.pallas_call(
        unpack_kernel,
        out_shape=jax.ShapeDtypeStruct((rows, heads * depth), jnp.bfloat16),
        in_specs=[pl.BlockSpec(memory_space=pltpu.VMEM)],
        out_specs=pl.BlockSpec(memory_space=pltpu.HBM),
        scratch_shapes=[
            pltpu.VMEM((rows, heads * depth), jnp.bfloat16),
            pltpu.SemaphoreType.DMA((4,)),
        ],
        compiler_params=pltpu.CompilerParams(vmem_limit_bytes=8 * 1024 * 1024),
        name="unpack_heads",
    )(held)


def pipelined(count, score, weigh, blend):
    score(0, 0)
    weigh(0, 0)
    score(1, 1)

    def step(j, carry):
        blend(2 * j, 0)
        weigh(2 * j + 1, 1)
        score(2 * j + 2, 0)
        blend(2 * j + 1, 1)
        weigh(2 * j + 2, 0)
        score(2 * j + 3, 1)
        return carry

    lax.fori_loop(0, count // 2 - 1, step, 0)
    blend(count - 2, 0)
    weigh(count - 1, 1)
    blend(count - 1, 1)


def attend_kernel(axes, kept_hbm, class_hbm, qkv_ref, out_ref, *scratch):
    kept_ref, class_ref, v_all, logits_a, logits_b, weights_a, weights_b, kept_sem, class_sem = scratch
    logits_slots = (logits_a, logits_b)
    weights_slots = (weights_a, weights_b)
    block_count = qkv_ref.shape[0]
    me = own_place(axes)
    exponent_scale = math.log2(math.e) / math.sqrt(HD)
    kept_copy = pltpu.make_async_copy(kept_hbm.at[me], kept_ref, kept_sem)
    class_copy = pltpu.make_async_copy(class_hbm, class_ref, class_sem)
    class_copy.start()
    kept_copy.start()
    v_all[:, :, :HD] = qkv_ref[:, 2]
    v_all[:, :, HD:] = jnp.ones((block_count, BLOCK, HD), jnp.bfloat16)
    class_copy.wait()

    def scores(query_rows, key_rows):
        return lax.dot_general(
            query_rows, key_rows, (((1,), (1,)), ((), ())), preferred_element_type=jnp.float32
        )

    def weigh(rows, columns, slot):
        logits = logits_slots[slot][:rows, :columns]
        largest = jnp.max(logits, axis=-1, keepdims=True)
        weights = jnp.exp2((logits - largest) * exponent_scale).astype(jnp.bfloat16)
        weights_slots[slot][:rows, :columns] = weights

    def normalized(summed):
        return (summed[:, :HD] / summed[:, HD:]).astype(jnp.bfloat16)

    @pl.when(class_ref[me] == 1)
    def _():
        sizes = [2, block_count // 2 - 2, block_count // 2 - 2, 2]
        starts = [sum(sizes[:i]) for i in range(len(sizes))]

        def score(i):
            rows = sizes[i] * BLOCK
            query_rows = qkv_ref[starts[i] : starts[i] + sizes[i], 0].reshape(rows, HD)
            key_rows = qkv_ref[:, 1].reshape(block_count * BLOCK, HD)
            logits_slots[i % 2][:rows, :] = scores(query_rows, key_rows)

        def weigh_all(i):
            weigh(sizes[i] * BLOCK, block_count * BLOCK, i % 2)

        def blend(i):
            rows = sizes[i] * BLOCK
            value_rows = v_all[...].reshape(block_count * BLOCK, 2 * HD)
            weights = weights_slots[i % 2][:rows, :]
            out = normalized(jnp.dot(weights, value_rows, preferred_element_type=jnp.float32))
            out_ref[starts[i] : starts[i] + sizes[i]] = out.reshape(sizes[i], BLOCK, HD)

        score(0)
        weigh_all(0)
        score(1)
        for i in range(1, len(sizes)):
            blend(i - 1)
            weigh_all(i)
            if i + 1 < len(sizes):
                score(i + 1)
        blend(len(sizes) - 1)
        kept_copy.wait()

    @pl.when(class_ref[me] != 1)
    def _():
        kept_copy.wait()
        group = 2

        def block_pairs(block):
            kept_blocks = each_light_block(kept_ref, block)
            return list(zip(kept_blocks[::2], kept_blocks[1::2]))

        def score(i, slot):
            for member in range(group):
                block = group * i + member
                rows = slice(member * BLOCK, (member + 1) * BLOCK)
                for place, (one, other) in enumerate(block_pairs(block)):
                    key_rows = jnp.concatenate([qkv_ref[one, 1], qkv_ref[other, 1]], axis=0)
                    columns = slice(place * 2 * BLOCK, (place + 1) * 2 * BLOCK)
                    logits_slots[slot][rows, columns] = scores(qkv_ref[block, 0], key_rows)

        def blend(i, slot):
            for member in range(group):
                block = group * i + member
                rows = slice(member * BLOCK, (member + 1) * BLOCK)
                summed = jnp.zeros((BLOCK, 2 * HD), jnp.float32)
                for place, (one, other) in enumerate(block_pairs(block)):
                    value_rows = jnp.concatenate([v_all[one], v_all[other]], axis=0)
                    columns = slice(place * 2 * BLOCK, (place + 1) * 2 * BLOCK)
                    weights = weights_slots[slot][rows, columns]
                    summed += jnp.dot(weights, value_rows, preferred_element_type=jnp.float32)
                out_ref[block] = normalized(summed)

        def weigh_few(i, slot):
            weigh(group * BLOCK, block_count // KEEP * LIGHT * BLOCK, slot)

        pipelined(block_count // group, score, weigh_few, blend)


def heads_by_device(queries, keys, values, kept, dense_class):
    axes = ("seq", "blk")
    block_count = kept.shape[1]
    in_vmem = pl.BlockSpec(memory_space=pltpu.VMEM)

    def exchange(send):
        return lax.all_to_all(send, axes, split_axis=0, concat_axis=0, tiled=True)

    held = exchange(pack_heads(queries, keys, values))
    stage_rows = (block_count // 2 - 2) * BLOCK
    attended = pl.pallas_call(
        lambda *refs: attend_kernel(axes, *refs),
        out_shape=jax.ShapeDtypeStruct((block_count, BLOCK, HD), jnp.bfloat16),
        in_specs=[
            pl.BlockSpec(memory_space=pl.ANY),
            pl.BlockSpec(memory_space=pl.ANY),
            in_vmem,
        ],
        out_specs=in_vmem,
        scratch_shapes=[
            pltpu.SMEM(kept.shape[1:], jnp.int32),
            pltpu.SMEM(dense_class.shape, jnp.int32),
            pltpu.VMEM((block_count, BLOCK, 2 * HD), jnp.bfloat16),
            pltpu.VMEM((stage_rows, block_count * BLOCK), jnp.float32),
            pltpu.VMEM((stage_rows, block_count * BLOCK), jnp.float32),
            pltpu.VMEM((stage_rows, block_count * BLOCK), jnp.bfloat16),
            pltpu.VMEM((stage_rows, block_count * BLOCK), jnp.bfloat16),
            pltpu.SemaphoreType.DMA,
            pltpu.SemaphoreType.DMA,
        ],
        compiler_params=pltpu.CompilerParams(vmem_limit_bytes=40 * 1024 * 1024),
        name="attend_head",
    )(kept, dense_class, held)
    return unpack_heads(exchange(attended))


def shards(queries, keys, values, kept, dense_class):
    devices = lax.axis_size("seq") * lax.axis_size("blk")
    one_head_each = devices == HEADS
    one_block_each = queries.shape[0] == BLOCK
    every_block_kept = kept.shape[1] == kept.shape[2]
    if one_head_each and one_block_each and every_block_kept:
        return heads_by_device(queries, keys, values, kept, dense_class)
    return spans_by_device(queries, keys, values, kept, dense_class)


def solution(mesh):
    return jax.shard_map(
        shards,
        mesh=mesh,
        in_specs=(
            P(("clip", "seq", "blk"), None),
            P(("clip", "seq", "blk"), None),
            P(("clip", "seq", "blk"), None),
            P(),
            P(),
        ),
        out_specs=P(("clip", "seq", "blk"), None),
        check_vma=False,
    )
```

```python
import math

import jax
import jax.numpy as jnp
from jax import lax
from jax.experimental import pallas as pl
from jax.experimental.pallas import tpu as pltpu
from jax.sharding import PartitionSpec as P

HEADS = 16
HD = 128
BLOCK = 128
KEEP = 4
LIGHT = 2


def combine_spans(partial_out, maxima, totals, along):
    largest = jnp.max(maxima, axis=along, keepdims=True)
    factor = jnp.exp(maxima - largest)
    numerator = jnp.sum(factor[..., None] * partial_out, axis=along)
    denominator = jnp.sum(factor * totals, axis=along)
    return (numerator / denominator[..., None]).astype(jnp.bfloat16)


def attend_blocks(query_rows, key_blocks, blocked_value_rows, local_ids, slot_count):
    query_blocks, part_rows, head_depth = query_rows.shape
    group_size = query_blocks
    while group_size * part_rows > 512 and group_size % 2 == 0:
        group_size = group_size // 2
    logit_scale_factor = 1.0 / math.sqrt(head_depth)
    block_rows = key_blocks.shape[1]

    def one_group(operands):
        queries_group, ids_group = operands
        collected_key_blocks = key_blocks[ids_group].reshape(
            group_size, slot_count * block_rows, head_depth
        )
        gathered_v = blocked_value_rows[ids_group].reshape(
            group_size, slot_count * block_rows, head_depth
        )
        attention_logits = (
            jnp.einsum(
                "gpd,gkd->gpk",
                queries_group,
                collected_key_blocks,
                preferred_element_type=jnp.float32,
            )
            * logit_scale_factor
        )
        maxima = jnp.max(attention_logits, axis=-1)
        weights = jnp.exp(attention_logits - maxima[..., None])
        totals = jnp.sum(weights, axis=-1)
        partial_out = jnp.einsum(
            "gpk,gkd->gpd",
            weights.astype(jnp.bfloat16),
            gathered_v,
            preferred_element_type=jnp.float32,
        )
        return (partial_out, maxima, totals)

    grouped_q = query_rows.reshape(query_blocks // group_size, group_size, part_rows, head_depth)
    grouped_ids = local_ids[:, :slot_count].reshape(
        query_blocks // group_size, group_size, slot_count
    )
    partial_out, maxima, totals = lax.map(one_group, (grouped_q, grouped_ids))
    return (
        partial_out.reshape(query_blocks, part_rows, head_depth),
        maxima.reshape(query_blocks, part_rows),
        totals.reshape(query_blocks, part_rows),
    )


def arrange_heads(stacked):
    swapped = jnp.swapaxes(stacked, 0, 1)
    return swapped.reshape((-1,) + stacked.shape[2:])


def spans_by_device(queries, keys, values, kept, dense_class):
    seq_devices = lax.axis_size("seq")
    span_count = lax.axis_size("blk")
    local_rows = queries.shape[0]
    head_count = HEADS
    head_depth = HD
    local_blocks = local_rows // BLOCK
    row_parts = max(1, 2 * seq_devices // head_count)
    part_rows = BLOCK // row_parts
    item_count = head_count * row_parts
    per_device = item_count // seq_devices
    seq_place = lax.axis_index("seq")
    blk_place = lax.axis_index("blk")
    every_item = jnp.arange(item_count, dtype=jnp.int32)
    all_item_heads = every_item // row_parts
    item_heads = lax.dynamic_slice_in_dim(all_item_heads, seq_place * per_device, per_device)
    grid_q = queries.reshape(local_blocks, row_parts, part_rows, head_count, head_depth).transpose(
        1, 3, 0, 2, 4
    )
    grid_q = grid_q.reshape(row_parts, head_count, local_blocks * part_rows, head_depth)
    head_keys = keys.reshape(local_rows, head_count, head_depth).transpose(1, 0, 2)
    head_values = values.reshape(local_rows, head_count, head_depth).transpose(1, 0, 2)
    send_q = arrange_heads(grid_q)
    q_items = lax.all_to_all(send_q, "seq", split_axis=0, concat_axis=1, tiled=True)
    stride = 1
    grid_k = jnp.broadcast_to(head_keys[None], (row_parts, head_count, local_rows, head_depth))
    grid_v = jnp.broadcast_to(head_values[None], (row_parts, head_count, local_rows, head_depth))
    send_k = arrange_heads(grid_k)
    send_v = arrange_heads(grid_v)
    k_held, v_held = (
        lax.all_to_all(send_k, "seq", split_axis=0, concat_axis=1, tiled=True),
        lax.all_to_all(send_v, "seq", split_axis=0, concat_axis=1, tiled=True),
    )
    key_blocks = k_held.reshape(per_device, seq_devices * local_blocks, BLOCK, head_depth)
    blocked_value_rows = v_held.reshape(per_device, seq_devices * local_blocks, BLOCK, head_depth)
    item_slot = jnp.arange(per_device, dtype=jnp.int32) // stride
    item_class = jnp.take(dense_class, item_heads)
    item_kept = jnp.take(kept, item_heads, axis=0)
    source_index = jnp.arange(seq_devices, dtype=jnp.int32)
    block_index = jnp.arange(local_blocks, dtype=jnp.int32)
    span_index = jnp.arange(span_count, dtype=jnp.int32)
    all_ids = (
        (source_index[None, :, None] * span_count + span_index[:, None, None]) * local_blocks
        + block_index[None, None, :]
    ).reshape(-1)
    all_kept = jnp.take(item_kept, all_ids, axis=1)
    span_ids = lax.dynamic_slice_in_dim(all_kept, blk_place * KEEP, KEEP, axis=2)
    q_all = lax.all_gather(q_items, "blk", axis=1, tiled=True)
    query_rows = q_all.reshape(
        per_device, span_count * seq_devices * local_blocks, part_rows, head_depth
    )

    def one_item(operands):
        rows_item, ids_item, class_item, slot_item = operands
        keys_item = lax.dynamic_index_in_dim(key_blocks, slot_item, 0, keepdims=False)
        values_item = lax.dynamic_index_in_dim(blocked_value_rows, slot_item, 0, keepdims=False)
        return lax.cond(
            class_item == 1,
            lambda: attend_blocks(rows_item, keys_item, values_item, ids_item, KEEP),
            lambda: attend_blocks(rows_item, keys_item, values_item, ids_item, LIGHT),
        )

    partial_out, maxima, totals = lax.map(
        one_item,
        (
            query_rows,
            span_ids // (local_blocks * span_count) * local_blocks + span_ids % local_blocks,
            item_class,
            item_slot,
        ),
    )
    own_blocks = seq_devices * local_blocks
    shaped_out = partial_out.reshape(per_device, span_count, own_blocks, part_rows, head_depth)
    shaped_max = maxima.reshape(per_device, span_count, own_blocks, part_rows)
    shaped_total = totals.reshape(per_device, span_count, own_blocks, part_rows)
    got_out, got_max, got_total = (
        lax.all_to_all(shaped_out, "blk", split_axis=1, concat_axis=1, tiled=True),
        lax.all_to_all(shaped_max, "blk", split_axis=1, concat_axis=1, tiled=True),
        lax.all_to_all(shaped_total, "blk", split_axis=1, concat_axis=1, tiled=True),
    )
    attended_items = combine_spans(got_out, got_max, got_total, 1)
    attended_items = attended_items.reshape(
        per_device, seq_devices * local_blocks * part_rows, head_depth
    )
    returned = lax.all_to_all(attended_items, "seq", split_axis=1, concat_axis=0, tiled=True)
    grid_out = returned.reshape(head_count, row_parts, local_blocks, part_rows, head_depth)
    grid_out = jnp.swapaxes(grid_out, 0, 1)
    return grid_out.transpose(2, 0, 3, 1, 4).reshape(local_rows, head_count * head_depth)


def own_place(axes):
    place = 0
    for axis in axes:
        place = place * lax.axis_size(axis) + lax.axis_index(axis)
    return place


def each_light_block(kept_ref, block):
    return [
        kept_ref[block, span * KEEP + slot]
        for span in range(kept_ref.shape[1] // KEEP)
        for slot in range(LIGHT)
    ]


def pack_kernel(*refs):
    sources, (out_ref, landed, sems) = refs[:-3], refs[-3:]
    heads = out_ref.shape[0]
    rows = landed.shape[1]
    pieces = sems.shape[1]
    piece_rows = rows // pieces
    arrivals = [
        [
            pltpu.make_async_copy(
                source.at[pl.ds(piece * piece_rows, piece_rows), :],
                landed.at[place, pl.ds(piece * piece_rows, piece_rows), :],
                sems.at[place, piece],
            )
            for piece in range(pieces)
        ]
        for place, source in enumerate(sources)
    ]
    for copies in arrivals:
        for copy in copies:
            copy.start()
    for place, copies in enumerate(arrivals):
        for piece, copy in enumerate(copies):
            copy.wait()
            kept_rows = slice(piece * piece_rows, (piece + 1) * piece_rows)
            for head in range(heads):
                out_ref[head, place, kept_rows, :] = landed[
                    place, kept_rows, head * HD : (head + 1) * HD
                ]


def pack_heads(*sources):
    count = len(sources)
    rows = sources[0].shape[0]
    pieces = 4
    return pl.pallas_call(
        pack_kernel,
        out_shape=jax.ShapeDtypeStruct((HEADS, count, rows, HD), jnp.bfloat16),
        in_specs=[pl.BlockSpec(memory_space=pltpu.HBM)] * count,
        out_specs=pl.BlockSpec(memory_space=pltpu.VMEM),
        scratch_shapes=[
            pltpu.VMEM((count, rows, HEADS * HD), jnp.bfloat16),
            pltpu.SemaphoreType.DMA((count, pieces)),
        ],
        compiler_params=pltpu.CompilerParams(vmem_limit_bytes=8 * 1024 * 1024),
        name="pack_heads",
    )(*[pltpu.with_memory_space_constraint(source, pltpu.HBM) for source in sources])


def unpack_kernel(held_ref, out_ref, turned, sems):
    heads = held_ref.shape[0]
    pieces = sems.shape[0]
    piece_rows = turned.shape[0] // pieces
    departures = []
    for piece in range(pieces):
        rows = slice(piece * piece_rows, (piece + 1) * piece_rows)
        for head in range(heads):
            turned[rows, head * HD : (head + 1) * HD] = held_ref[head, rows, :]
        departure = pltpu.make_async_copy(
            turned.at[pl.ds(piece * piece_rows, piece_rows), :],
            out_ref.at[pl.ds(piece * piece_rows, piece_rows), :],
            sems.at[piece],
        )
        departure.start()
        departures.append(departure)
    for departure in departures:
        departure.wait()


def unpack_heads(held):
    heads, rows, depth = held.shape
    return pl.pallas_call(
        unpack_kernel,
        out_shape=jax.ShapeDtypeStruct((rows, heads * depth), jnp.bfloat16),
        in_specs=[pl.BlockSpec(memory_space=pltpu.VMEM)],
        out_specs=pl.BlockSpec(memory_space=pltpu.HBM),
        scratch_shapes=[
            pltpu.VMEM((rows, heads * depth), jnp.bfloat16),
            pltpu.SemaphoreType.DMA((4,)),
        ],
        compiler_params=pltpu.CompilerParams(vmem_limit_bytes=8 * 1024 * 1024),
        name="unpack_heads",
    )(held)


def pipelined(count, score, weigh, blend):
    score(0, 0)
    weigh(0, 0)
    score(1, 1)

    def step(j, carry):
        blend(2 * j, 0)
        weigh(2 * j + 1, 1)
        score(2 * j + 2, 0)
        blend(2 * j + 1, 1)
        weigh(2 * j + 2, 0)
        score(2 * j + 3, 1)
        return carry

    lax.fori_loop(0, count // 2 - 1, step, 0)
    blend(count - 2, 0)
    weigh(count - 1, 1)
    blend(count - 1, 1)


def attend_kernel(axes, kept_hbm, class_hbm, qkv_ref, out_ref, *scratch):
    kept_ref, class_ref, v_all, logits_a, logits_b, weights_a, weights_b, kept_sem, class_sem = scratch
    logits_slots = (logits_a, logits_b)
    weights_slots = (weights_a, weights_b)
    block_count = qkv_ref.shape[0]
    me = own_place(axes)
    exponent_scale = math.log2(math.e) / math.sqrt(HD)
    kept_copy = pltpu.make_async_copy(kept_hbm, kept_ref, kept_sem)
    class_copy = pltpu.make_async_copy(class_hbm, class_ref, class_sem)
    class_copy.start()
    kept_copy.start()
    v_all[:, :, :HD] = qkv_ref[:, 2]
    v_all[:, :, HD:] = jnp.ones((block_count, BLOCK, HD), jnp.bfloat16)
    class_copy.wait()

    def scores(query_rows, key_rows):
        return lax.dot_general(
            query_rows, key_rows, (((1,), (1,)), ((), ())), preferred_element_type=jnp.float32
        )

    def weigh(rows, columns, slot):
        logits = logits_slots[slot][:rows, :columns]
        largest = jnp.max(logits, axis=-1, keepdims=True)
        weights = jnp.exp2((logits - largest) * exponent_scale).astype(jnp.bfloat16)
        weights_slots[slot][:rows, :columns] = weights

    def normalized(summed):
        return (summed[:, :HD] / summed[:, HD:]).astype(jnp.bfloat16)

    @pl.when(class_ref[me] == 1)
    def _():
        sizes = [2] + [4] * (block_count // 4 - 1) + [2]
        starts = [sum(sizes[:i]) for i in range(len(sizes))]

        def score(i):
            rows = sizes[i] * BLOCK
            query_rows = qkv_ref[starts[i] : starts[i] + sizes[i], 0].reshape(rows, HD)
            key_rows = qkv_ref[:, 1].reshape(block_count * BLOCK, HD)
            logits_slots[i % 2][:rows, :] = scores(query_rows, key_rows)

        def weigh_all(i):
            weigh(sizes[i] * BLOCK, block_count * BLOCK, i % 2)

        def blend(i):
            rows = sizes[i] * BLOCK
            value_rows = v_all[...].reshape(block_count * BLOCK, 2 * HD)
            weights = weights_slots[i % 2][:rows, :]
            out = normalized(jnp.dot(weights, value_rows, preferred_element_type=jnp.float32))
            out_ref[starts[i] : starts[i] + sizes[i]] = out.reshape(sizes[i], BLOCK, HD)

        score(0)
        weigh_all(0)
        score(1)
        for i in range(1, len(sizes)):
            blend(i - 1)
            weigh_all(i)
            if i + 1 < len(sizes):
                score(i + 1)
        blend(len(sizes) - 1)
        kept_copy.wait()

    @pl.when(class_ref[me] != 1)
    def _():
        kept_copy.wait()
        group = 2

        def block_pairs(block):
            kept_blocks = each_light_block(kept_ref, block)
            return list(zip(kept_blocks[::2], kept_blocks[1::2]))

        def score(i, slot):
            for member in range(group):
                block = group * i + member
                rows = slice(member * BLOCK, (member + 1) * BLOCK)
                for place, (one, other) in enumerate(block_pairs(block)):
                    key_rows = jnp.concatenate([qkv_ref[one, 1], qkv_ref[other, 1]], axis=0)
                    columns = slice(place * 2 * BLOCK, (place + 1) * 2 * BLOCK)
                    logits_slots[slot][rows, columns] = scores(qkv_ref[block, 0], key_rows)

        def blend(i, slot):
            for member in range(group):
                block = group * i + member
                rows = slice(member * BLOCK, (member + 1) * BLOCK)
                summed = jnp.zeros((BLOCK, 2 * HD), jnp.float32)
                for place, (one, other) in enumerate(block_pairs(block)):
                    value_rows = jnp.concatenate([v_all[one], v_all[other]], axis=0)
                    columns = slice(place * 2 * BLOCK, (place + 1) * 2 * BLOCK)
                    weights = weights_slots[slot][rows, columns]
                    summed += jnp.dot(weights, value_rows, preferred_element_type=jnp.float32)
                out_ref[block] = normalized(summed)

        def weigh_few(i, slot):
            weigh(group * BLOCK, block_count // KEEP * LIGHT * BLOCK, slot)

        pipelined(block_count // group, score, weigh_few, blend)


def heads_by_device(queries, keys, values, kept, dense_class):
    axes = ("seq", "blk")
    block_count = kept.shape[1]
    in_vmem = pl.BlockSpec(memory_space=pltpu.VMEM)

    def exchange(send):
        return lax.all_to_all(send, axes, split_axis=0, concat_axis=0, tiled=True)

    held = exchange(pack_heads(queries, keys, values))
    own_kept = lax.dynamic_index_in_dim(kept, own_place(axes), 0, keepdims=False)
    stage_rows = 4 * BLOCK
    attended = pl.pallas_call(
        lambda *refs: attend_kernel(axes, *refs),
        out_shape=jax.ShapeDtypeStruct((block_count, BLOCK, HD), jnp.bfloat16),
        in_specs=[
            pl.BlockSpec(memory_space=pl.ANY),
            pl.BlockSpec(memory_space=pl.ANY),
            in_vmem,
        ],
        out_specs=in_vmem,
        scratch_shapes=[
            pltpu.SMEM(kept.shape[1:], jnp.int32),
            pltpu.SMEM(dense_class.shape, jnp.int32),
            pltpu.VMEM((block_count, BLOCK, 2 * HD), jnp.bfloat16),
            pltpu.VMEM((stage_rows, block_count * BLOCK), jnp.float32),
            pltpu.VMEM((stage_rows, block_count * BLOCK), jnp.float32),
            pltpu.VMEM((stage_rows, block_count * BLOCK), jnp.bfloat16),
            pltpu.VMEM((stage_rows, block_count * BLOCK), jnp.bfloat16),
            pltpu.SemaphoreType.DMA,
            pltpu.SemaphoreType.DMA,
        ],
        compiler_params=pltpu.CompilerParams(vmem_limit_bytes=40 * 1024 * 1024),
        name="attend_head",
    )(own_kept, dense_class, held)
    return unpack_heads(exchange(attended))


def shards(queries, keys, values, kept, dense_class):
    devices = lax.axis_size("seq") * lax.axis_size("blk")
    one_head_each = devices == HEADS
    one_block_each = queries.shape[0] == BLOCK
    every_block_kept = kept.shape[1] == kept.shape[2]
    if one_head_each and one_block_each and every_block_kept:
        return heads_by_device(queries, keys, values, kept, dense_class)
    return spans_by_device(queries, keys, values, kept, dense_class)


def solution(mesh):
    return jax.shard_map(
        shards,
        mesh=mesh,
        in_specs=(
            P(("clip", "seq", "blk"), None),
            P(("clip", "seq", "blk"), None),
            P(("clip", "seq", "blk"), None),
            P(),
            P(),
        ),
        out_specs=P(("clip", "seq", "blk"), None),
        check_vma=False,
    )
```

```python
import math

import jax
import jax.numpy as jnp
from jax import lax
from jax.experimental import pallas as pl
from jax.experimental.pallas import tpu as pltpu
from jax.sharding import PartitionSpec as P

HEADS = 16
HD = 128
BLOCK = 128
KEEP = 4
LIGHT = 2


def combine_spans(partial_out, maxima, totals, along):
    largest = jnp.max(maxima, axis=along, keepdims=True)
    factor = jnp.exp(maxima - largest)
    numerator = jnp.sum(factor[..., None] * partial_out, axis=along)
    denominator = jnp.sum(factor * totals, axis=along)
    return (numerator / denominator[..., None]).astype(jnp.bfloat16)


def attend_blocks(query_rows, key_blocks, blocked_value_rows, local_ids, slot_count):
    query_blocks, part_rows, head_depth = query_rows.shape
    group_size = query_blocks
    while group_size * part_rows > 512 and group_size % 2 == 0:
        group_size = group_size // 2
    logit_scale_factor = 1.0 / math.sqrt(head_depth)
    block_rows = key_blocks.shape[1]

    def one_group(operands):
        queries_group, ids_group = operands
        collected_key_blocks = key_blocks[ids_group].reshape(
            group_size, slot_count * block_rows, head_depth
        )
        gathered_v = blocked_value_rows[ids_group].reshape(
            group_size, slot_count * block_rows, head_depth
        )
        attention_logits = (
            jnp.einsum(
                "gpd,gkd->gpk",
                queries_group,
                collected_key_blocks,
                preferred_element_type=jnp.float32,
            )
            * logit_scale_factor
        )
        maxima = jnp.max(attention_logits, axis=-1)
        weights = jnp.exp(attention_logits - maxima[..., None])
        totals = jnp.sum(weights, axis=-1)
        partial_out = jnp.einsum(
            "gpk,gkd->gpd",
            weights.astype(jnp.bfloat16),
            gathered_v,
            preferred_element_type=jnp.float32,
        )
        return (partial_out, maxima, totals)

    grouped_q = query_rows.reshape(query_blocks // group_size, group_size, part_rows, head_depth)
    grouped_ids = local_ids[:, :slot_count].reshape(
        query_blocks // group_size, group_size, slot_count
    )
    partial_out, maxima, totals = lax.map(one_group, (grouped_q, grouped_ids))
    return (
        partial_out.reshape(query_blocks, part_rows, head_depth),
        maxima.reshape(query_blocks, part_rows),
        totals.reshape(query_blocks, part_rows),
    )


def arrange_heads(stacked):
    swapped = jnp.swapaxes(stacked, 0, 1)
    return swapped.reshape((-1,) + stacked.shape[2:])


def spans_by_device(queries, keys, values, kept, dense_class):
    seq_devices = lax.axis_size("seq")
    span_count = lax.axis_size("blk")
    local_rows = queries.shape[0]
    head_count = HEADS
    head_depth = HD
    local_blocks = local_rows // BLOCK
    row_parts = max(1, 2 * seq_devices // head_count)
    part_rows = BLOCK // row_parts
    item_count = head_count * row_parts
    per_device = item_count // seq_devices
    seq_place = lax.axis_index("seq")
    blk_place = lax.axis_index("blk")
    every_item = jnp.arange(item_count, dtype=jnp.int32)
    all_item_heads = every_item // row_parts
    item_heads = lax.dynamic_slice_in_dim(all_item_heads, seq_place * per_device, per_device)
    grid_q = queries.reshape(local_blocks, row_parts, part_rows, head_count, head_depth).transpose(
        1, 3, 0, 2, 4
    )
    grid_q = grid_q.reshape(row_parts, head_count, local_blocks * part_rows, head_depth)
    head_keys = keys.reshape(local_rows, head_count, head_depth).transpose(1, 0, 2)
    head_values = values.reshape(local_rows, head_count, head_depth).transpose(1, 0, 2)
    send_q = arrange_heads(grid_q)
    q_items = lax.all_to_all(send_q, "seq", split_axis=0, concat_axis=1, tiled=True)
    stride = 1
    grid_k = jnp.broadcast_to(head_keys[None], (row_parts, head_count, local_rows, head_depth))
    grid_v = jnp.broadcast_to(head_values[None], (row_parts, head_count, local_rows, head_depth))
    send_k = arrange_heads(grid_k)
    send_v = arrange_heads(grid_v)
    k_held, v_held = (
        lax.all_to_all(send_k, "seq", split_axis=0, concat_axis=1, tiled=True),
        lax.all_to_all(send_v, "seq", split_axis=0, concat_axis=1, tiled=True),
    )
    key_blocks = k_held.reshape(per_device, seq_devices * local_blocks, BLOCK, head_depth)
    blocked_value_rows = v_held.reshape(per_device, seq_devices * local_blocks, BLOCK, head_depth)
    item_slot = jnp.arange(per_device, dtype=jnp.int32) // stride
    item_class = jnp.take(dense_class, item_heads)
    item_kept = jnp.take(kept, item_heads, axis=0)
    source_index = jnp.arange(seq_devices, dtype=jnp.int32)
    block_index = jnp.arange(local_blocks, dtype=jnp.int32)
    span_index = jnp.arange(span_count, dtype=jnp.int32)
    all_ids = (
        (source_index[None, :, None] * span_count + span_index[:, None, None]) * local_blocks
        + block_index[None, None, :]
    ).reshape(-1)
    all_kept = jnp.take(item_kept, all_ids, axis=1)
    span_ids = lax.dynamic_slice_in_dim(all_kept, blk_place * KEEP, KEEP, axis=2)
    q_all = lax.all_gather(q_items, "blk", axis=1, tiled=True)
    query_rows = q_all.reshape(
        per_device, span_count * seq_devices * local_blocks, part_rows, head_depth
    )

    def one_item(operands):
        rows_item, ids_item, class_item, slot_item = operands
        keys_item = lax.dynamic_index_in_dim(key_blocks, slot_item, 0, keepdims=False)
        values_item = lax.dynamic_index_in_dim(blocked_value_rows, slot_item, 0, keepdims=False)
        return lax.cond(
            class_item == 1,
            lambda: attend_blocks(rows_item, keys_item, values_item, ids_item, KEEP),
            lambda: attend_blocks(rows_item, keys_item, values_item, ids_item, LIGHT),
        )

    partial_out, maxima, totals = lax.map(
        one_item,
        (
            query_rows,
            span_ids // (local_blocks * span_count) * local_blocks + span_ids % local_blocks,
            item_class,
            item_slot,
        ),
    )
    own_blocks = seq_devices * local_blocks
    shaped_out = partial_out.reshape(per_device, span_count, own_blocks, part_rows, head_depth)
    shaped_max = maxima.reshape(per_device, span_count, own_blocks, part_rows)
    shaped_total = totals.reshape(per_device, span_count, own_blocks, part_rows)
    got_out, got_max, got_total = (
        lax.all_to_all(shaped_out, "blk", split_axis=1, concat_axis=1, tiled=True),
        lax.all_to_all(shaped_max, "blk", split_axis=1, concat_axis=1, tiled=True),
        lax.all_to_all(shaped_total, "blk", split_axis=1, concat_axis=1, tiled=True),
    )
    attended_items = combine_spans(got_out, got_max, got_total, 1)
    attended_items = attended_items.reshape(
        per_device, seq_devices * local_blocks * part_rows, head_depth
    )
    returned = lax.all_to_all(attended_items, "seq", split_axis=1, concat_axis=0, tiled=True)
    grid_out = returned.reshape(head_count, row_parts, local_blocks, part_rows, head_depth)
    grid_out = jnp.swapaxes(grid_out, 0, 1)
    return grid_out.transpose(2, 0, 3, 1, 4).reshape(local_rows, head_count * head_depth)


def own_place(axes):
    place = 0
    for axis in axes:
        place = place * lax.axis_size(axis) + lax.axis_index(axis)
    return place


def each_light_block(kept_ref, block):
    return [
        kept_ref[block, span * KEEP + slot]
        for span in range(kept_ref.shape[1] // KEEP)
        for slot in range(LIGHT)
    ]


def pack_kernel(*refs):
    sources, (out_ref, landed, sems) = refs[:-3], refs[-3:]
    heads = out_ref.shape[0]
    rows = landed.shape[1]
    pieces = sems.shape[1]
    piece_rows = rows // pieces
    arrivals = [
        [
            pltpu.make_async_copy(
                source.at[pl.ds(piece * piece_rows, piece_rows), :],
                landed.at[place, pl.ds(piece * piece_rows, piece_rows), :],
                sems.at[place, piece],
            )
            for piece in range(pieces)
        ]
        for place, source in enumerate(sources)
    ]
    for copies in arrivals:
        for copy in copies:
            copy.start()
    for place, copies in enumerate(arrivals):
        for piece, copy in enumerate(copies):
            copy.wait()
            kept_rows = slice(piece * piece_rows, (piece + 1) * piece_rows)
            for head in range(heads):
                out_ref[head, place, kept_rows, :] = landed[
                    place, kept_rows, head * HD : (head + 1) * HD
                ]


def pack_heads(*sources):
    count = len(sources)
    rows = sources[0].shape[0]
    pieces = 4
    return pl.pallas_call(
        pack_kernel,
        out_shape=jax.ShapeDtypeStruct((HEADS, count, rows, HD), jnp.bfloat16),
        in_specs=[pl.BlockSpec(memory_space=pltpu.HBM)] * count,
        out_specs=pl.BlockSpec(memory_space=pltpu.VMEM),
        scratch_shapes=[
            pltpu.VMEM((count, rows, HEADS * HD), jnp.bfloat16),
            pltpu.SemaphoreType.DMA((count, pieces)),
        ],
        compiler_params=pltpu.CompilerParams(vmem_limit_bytes=8 * 1024 * 1024),
        name="pack_heads",
    )(*[pltpu.with_memory_space_constraint(source, pltpu.HBM) for source in sources])


def unpack_kernel(held_ref, out_ref, turned, sems):
    heads = held_ref.shape[0]
    pieces = sems.shape[0]
    piece_rows = turned.shape[0] // pieces
    departures = []
    for piece in range(pieces):
        rows = slice(piece * piece_rows, (piece + 1) * piece_rows)
        for head in range(heads):
            turned[rows, head * HD : (head + 1) * HD] = held_ref[head, rows, :]
        departure = pltpu.make_async_copy(
            turned.at[pl.ds(piece * piece_rows, piece_rows), :],
            out_ref.at[pl.ds(piece * piece_rows, piece_rows), :],
            sems.at[piece],
        )
        departure.start()
        departures.append(departure)
    for departure in departures:
        departure.wait()


def unpack_heads(held):
    heads, rows, depth = held.shape
    return pl.pallas_call(
        unpack_kernel,
        out_shape=jax.ShapeDtypeStruct((rows, heads * depth), jnp.bfloat16),
        in_specs=[pl.BlockSpec(memory_space=pltpu.VMEM)],
        out_specs=pl.BlockSpec(memory_space=pltpu.HBM),
        scratch_shapes=[
            pltpu.VMEM((rows, heads * depth), jnp.bfloat16),
            pltpu.SemaphoreType.DMA((4,)),
        ],
        compiler_params=pltpu.CompilerParams(vmem_limit_bytes=8 * 1024 * 1024),
        name="unpack_heads",
    )(held)


def pipelined(count, score, weigh, blend):
    score(0, 0)
    weigh(0, 0)
    score(1, 1)

    def step(j, carry):
        blend(2 * j, 0)
        weigh(2 * j + 1, 1)
        score(2 * j + 2, 0)
        blend(2 * j + 1, 1)
        weigh(2 * j + 2, 0)
        score(2 * j + 3, 1)
        return carry

    lax.fori_loop(0, count // 2 - 1, step, 0)
    blend(count - 2, 0)
    weigh(count - 1, 1)
    blend(count - 1, 1)


def attend_kernel(axes, kept_hbm, class_hbm, qkv_ref, out_ref, *scratch):
    kept_ref, class_ref, v_all, logits_a, logits_b, weights_a, weights_b, kept_sem, class_sem = scratch
    logits_slots = (logits_a, logits_b)
    weights_slots = (weights_a, weights_b)
    block_count = qkv_ref.shape[0]
    me = own_place(axes)
    exponent_scale = math.log2(math.e) / math.sqrt(HD)
    kept_copy = pltpu.make_async_copy(kept_hbm.at[me], kept_ref, kept_sem)
    class_copy = pltpu.make_async_copy(class_hbm, class_ref, class_sem)
    class_copy.start()
    kept_copy.start()
    v_all[:, :, :HD] = qkv_ref[:, 2]
    v_all[:, :, HD:] = jnp.ones((block_count, BLOCK, HD), jnp.bfloat16)
    class_copy.wait()

    def scores(query_rows, key_rows):
        return lax.dot_general(
            query_rows, key_rows, (((1,), (1,)), ((), ())), preferred_element_type=jnp.float32
        )

    def weigh(rows, columns, slot):
        logits = logits_slots[slot][:rows, :columns]
        largest = jnp.max(logits, axis=-1, keepdims=True)
        weights = jnp.exp2((logits - largest) * exponent_scale).astype(jnp.bfloat16)
        weights_slots[slot][:rows, :columns] = weights

    def normalized(summed):
        return (summed[:, :HD] / summed[:, HD:]).astype(jnp.bfloat16)

    @pl.when(class_ref[me] == 1)
    def _():
        sizes = [2] + [4] * (block_count // 4 - 1) + [2]
        starts = [sum(sizes[:i]) for i in range(len(sizes))]

        def score(i):
            rows = sizes[i] * BLOCK
            query_rows = qkv_ref[starts[i] : starts[i] + sizes[i], 0].reshape(rows, HD)
            key_rows = qkv_ref[:, 1].reshape(block_count * BLOCK, HD)
            logits_slots[i % 2][:rows, :] = scores(query_rows, key_rows)

        def weigh_all(i):
            weigh(sizes[i] * BLOCK, block_count * BLOCK, i % 2)

        def blend(i):
            rows = sizes[i] * BLOCK
            value_rows = v_all[...].reshape(block_count * BLOCK, 2 * HD)
            weights = weights_slots[i % 2][:rows, :]
            out = normalized(jnp.dot(weights, value_rows, preferred_element_type=jnp.float32))
            out_ref[starts[i] : starts[i] + sizes[i]] = out.reshape(sizes[i], BLOCK, HD)

        score(0)
        weigh_all(0)
        score(1)
        for i in range(1, len(sizes)):
            blend(i - 1)
            weigh_all(i)
            if i + 1 < len(sizes):
                score(i + 1)
        blend(len(sizes) - 1)
        kept_copy.wait()

    @pl.when(class_ref[me] != 1)
    def _():
        kept_copy.wait()
        group = 2

        def block_pairs(block):
            kept_blocks = each_light_block(kept_ref, block)
            return list(zip(kept_blocks[::2], kept_blocks[1::2]))

        def score(i, slot):
            for member in range(group):
                block = group * i + member
                rows = slice(member * BLOCK, (member + 1) * BLOCK)
                for place, (one, other) in enumerate(block_pairs(block)):
                    key_rows = jnp.concatenate([qkv_ref[one, 1], qkv_ref[other, 1]], axis=0)
                    columns = slice(place * 2 * BLOCK, (place + 1) * 2 * BLOCK)
                    logits_slots[slot][rows, columns] = scores(qkv_ref[block, 0], key_rows)

        def blend(i, slot):
            for member in range(group):
                block = group * i + member
                rows = slice(member * BLOCK, (member + 1) * BLOCK)
                summed = jnp.zeros((BLOCK, 2 * HD), jnp.float32)
                for place, (one, other) in enumerate(block_pairs(block)):
                    value_rows = jnp.concatenate([v_all[one], v_all[other]], axis=0)
                    columns = slice(place * 2 * BLOCK, (place + 1) * 2 * BLOCK)
                    weights = weights_slots[slot][rows, columns]
                    summed += jnp.dot(weights, value_rows, preferred_element_type=jnp.float32)
                out_ref[block] = normalized(summed)

        def weigh_few(i, slot):
            weigh(group * BLOCK, block_count // KEEP * LIGHT * BLOCK, slot)

        pipelined(block_count // group, score, weigh_few, blend)


def heads_by_device(queries, keys, values, kept, dense_class):
    axes = ("seq", "blk")
    block_count = kept.shape[1]
    in_vmem = pl.BlockSpec(memory_space=pltpu.VMEM)

    def exchange(send):
        return lax.all_to_all(send, axes, split_axis=0, concat_axis=0, tiled=True)

    held = exchange(pack_heads(queries, keys, values))
    stage_rows = 4 * BLOCK
    attended = pl.pallas_call(
        lambda *refs: attend_kernel(axes, *refs),
        out_shape=jax.ShapeDtypeStruct((block_count, BLOCK, HD), jnp.bfloat16),
        in_specs=[
            pl.BlockSpec(memory_space=pl.ANY),
            pl.BlockSpec(memory_space=pl.ANY),
            in_vmem,
        ],
        out_specs=in_vmem,
        scratch_shapes=[
            pltpu.SMEM(kept.shape[1:], jnp.int32),
            pltpu.SMEM(dense_class.shape, jnp.int32),
            pltpu.VMEM((block_count, BLOCK, 2 * HD), jnp.bfloat16),
            pltpu.VMEM((stage_rows, block_count * BLOCK), jnp.float32),
            pltpu.VMEM((stage_rows, block_count * BLOCK), jnp.float32),
            pltpu.VMEM((stage_rows, block_count * BLOCK), jnp.bfloat16),
            pltpu.VMEM((stage_rows, block_count * BLOCK), jnp.bfloat16),
            pltpu.SemaphoreType.DMA,
            pltpu.SemaphoreType.DMA,
        ],
        compiler_params=pltpu.CompilerParams(vmem_limit_bytes=40 * 1024 * 1024),
        name="attend_head",
    )(kept, dense_class, held)
    return unpack_heads(exchange(attended))


def shards(queries, keys, values, kept, dense_class):
    devices = lax.axis_size("seq") * lax.axis_size("blk")
    one_head_each = devices == HEADS
    one_block_each = queries.shape[0] == BLOCK
    every_block_kept = kept.shape[1] == kept.shape[2]
    if one_head_each and one_block_each and every_block_kept:
        return heads_by_device(queries, keys, values, kept, dense_class)
    return spans_by_device(queries, keys, values, kept, dense_class)


def solution(mesh):
    return jax.shard_map(
        shards,
        mesh=mesh,
        in_specs=(
            P(("clip", "seq", "blk"), None),
            P(("clip", "seq", "blk"), None),
            P(("clip", "seq", "blk"), None),
            P(),
            P(),
        ),
        out_specs=P(("clip", "seq", "blk"), None),
        check_vma=False,
    )
```

```python
import math

import jax
import jax.numpy as jnp
from jax import lax
from jax.experimental import pallas as pl
from jax.experimental.pallas import tpu as pltpu
from jax.sharding import PartitionSpec as P

HEADS = 16
HD = 128
BLOCK = 128
KEEP = 4
LIGHT = 2


def combine_spans(partial_out, maxima, totals, along):
    largest = jnp.max(maxima, axis=along, keepdims=True)
    factor = jnp.exp(maxima - largest)
    numerator = jnp.sum(factor[..., None] * partial_out, axis=along)
    denominator = jnp.sum(factor * totals, axis=along)
    return (numerator / denominator[..., None]).astype(jnp.bfloat16)


def attend_blocks(query_rows, key_blocks, blocked_value_rows, local_ids, slot_count):
    query_blocks, part_rows, head_depth = query_rows.shape
    group_size = query_blocks
    while group_size * part_rows > 512 and group_size % 2 == 0:
        group_size = group_size // 2
    logit_scale_factor = 1.0 / math.sqrt(head_depth)
    block_rows = key_blocks.shape[1]

    def one_group(operands):
        queries_group, ids_group = operands
        collected_key_blocks = key_blocks[ids_group].reshape(
            group_size, slot_count * block_rows, head_depth
        )
        gathered_v = blocked_value_rows[ids_group].reshape(
            group_size, slot_count * block_rows, head_depth
        )
        attention_logits = (
            jnp.einsum(
                "gpd,gkd->gpk",
                queries_group,
                collected_key_blocks,
                preferred_element_type=jnp.float32,
            )
            * logit_scale_factor
        )
        maxima = jnp.max(attention_logits, axis=-1)
        weights = jnp.exp(attention_logits - maxima[..., None])
        totals = jnp.sum(weights, axis=-1)
        partial_out = jnp.einsum(
            "gpk,gkd->gpd",
            weights.astype(jnp.bfloat16),
            gathered_v,
            preferred_element_type=jnp.float32,
        )
        return (partial_out, maxima, totals)

    grouped_q = query_rows.reshape(query_blocks // group_size, group_size, part_rows, head_depth)
    grouped_ids = local_ids[:, :slot_count].reshape(
        query_blocks // group_size, group_size, slot_count
    )
    partial_out, maxima, totals = lax.map(one_group, (grouped_q, grouped_ids))
    return (
        partial_out.reshape(query_blocks, part_rows, head_depth),
        maxima.reshape(query_blocks, part_rows),
        totals.reshape(query_blocks, part_rows),
    )


def arrange_heads(stacked):
    swapped = jnp.swapaxes(stacked, 0, 1)
    return swapped.reshape((-1,) + stacked.shape[2:])


def spans_by_device(queries, keys, values, kept, dense_class):
    seq_devices = lax.axis_size("seq")
    span_count = lax.axis_size("blk")
    local_rows = queries.shape[0]
    head_count = HEADS
    head_depth = HD
    local_blocks = local_rows // BLOCK
    row_parts = max(1, 2 * seq_devices // head_count)
    part_rows = BLOCK // row_parts
    item_count = head_count * row_parts
    per_device = item_count // seq_devices
    seq_place = lax.axis_index("seq")
    blk_place = lax.axis_index("blk")
    every_item = jnp.arange(item_count, dtype=jnp.int32)
    all_item_heads = every_item // row_parts
    item_heads = lax.dynamic_slice_in_dim(all_item_heads, seq_place * per_device, per_device)
    grid_q = queries.reshape(local_blocks, row_parts, part_rows, head_count, head_depth).transpose(
        1, 3, 0, 2, 4
    )
    grid_q = grid_q.reshape(row_parts, head_count, local_blocks * part_rows, head_depth)
    head_keys = keys.reshape(local_rows, head_count, head_depth).transpose(1, 0, 2)
    head_values = values.reshape(local_rows, head_count, head_depth).transpose(1, 0, 2)
    send_q = arrange_heads(grid_q)
    q_items = lax.all_to_all(send_q, "seq", split_axis=0, concat_axis=1, tiled=True)
    stride = 1
    grid_k = jnp.broadcast_to(head_keys[None], (row_parts, head_count, local_rows, head_depth))
    grid_v = jnp.broadcast_to(head_values[None], (row_parts, head_count, local_rows, head_depth))
    send_k = arrange_heads(grid_k)
    send_v = arrange_heads(grid_v)
    k_held, v_held = (
        lax.all_to_all(send_k, "seq", split_axis=0, concat_axis=1, tiled=True),
        lax.all_to_all(send_v, "seq", split_axis=0, concat_axis=1, tiled=True),
    )
    key_blocks = k_held.reshape(per_device, seq_devices * local_blocks, BLOCK, head_depth)
    blocked_value_rows = v_held.reshape(per_device, seq_devices * local_blocks, BLOCK, head_depth)
    item_slot = jnp.arange(per_device, dtype=jnp.int32) // stride
    item_class = jnp.take(dense_class, item_heads)
    item_kept = jnp.take(kept, item_heads, axis=0)
    source_index = jnp.arange(seq_devices, dtype=jnp.int32)
    block_index = jnp.arange(local_blocks, dtype=jnp.int32)
    span_index = jnp.arange(span_count, dtype=jnp.int32)
    all_ids = (
        (source_index[None, :, None] * span_count + span_index[:, None, None]) * local_blocks
        + block_index[None, None, :]
    ).reshape(-1)
    all_kept = jnp.take(item_kept, all_ids, axis=1)
    span_ids = lax.dynamic_slice_in_dim(all_kept, blk_place * KEEP, KEEP, axis=2)
    q_all = lax.all_gather(q_items, "blk", axis=1, tiled=True)
    query_rows = q_all.reshape(
        per_device, span_count * seq_devices * local_blocks, part_rows, head_depth
    )

    def one_item(operands):
        rows_item, ids_item, class_item, slot_item = operands
        keys_item = lax.dynamic_index_in_dim(key_blocks, slot_item, 0, keepdims=False)
        values_item = lax.dynamic_index_in_dim(blocked_value_rows, slot_item, 0, keepdims=False)
        return lax.cond(
            class_item == 1,
            lambda: attend_blocks(rows_item, keys_item, values_item, ids_item, KEEP),
            lambda: attend_blocks(rows_item, keys_item, values_item, ids_item, LIGHT),
        )

    partial_out, maxima, totals = lax.map(
        one_item,
        (
            query_rows,
            span_ids // (local_blocks * span_count) * local_blocks + span_ids % local_blocks,
            item_class,
            item_slot,
        ),
    )
    own_blocks = seq_devices * local_blocks
    shaped_out = partial_out.reshape(per_device, span_count, own_blocks, part_rows, head_depth)
    shaped_max = maxima.reshape(per_device, span_count, own_blocks, part_rows)
    shaped_total = totals.reshape(per_device, span_count, own_blocks, part_rows)
    got_out, got_max, got_total = (
        lax.all_to_all(shaped_out, "blk", split_axis=1, concat_axis=1, tiled=True),
        lax.all_to_all(shaped_max, "blk", split_axis=1, concat_axis=1, tiled=True),
        lax.all_to_all(shaped_total, "blk", split_axis=1, concat_axis=1, tiled=True),
    )
    attended_items = combine_spans(got_out, got_max, got_total, 1)
    attended_items = attended_items.reshape(
        per_device, seq_devices * local_blocks * part_rows, head_depth
    )
    returned = lax.all_to_all(attended_items, "seq", split_axis=1, concat_axis=0, tiled=True)
    grid_out = returned.reshape(head_count, row_parts, local_blocks, part_rows, head_depth)
    grid_out = jnp.swapaxes(grid_out, 0, 1)
    return grid_out.transpose(2, 0, 3, 1, 4).reshape(local_rows, head_count * head_depth)


def own_place(axes):
    place = 0
    for axis in axes:
        place = place * lax.axis_size(axis) + lax.axis_index(axis)
    return place


def each_light_block(kept_ref, block):
    return [
        kept_ref[block, span * KEEP + slot]
        for span in range(kept_ref.shape[1] // KEEP)
        for slot in range(LIGHT)
    ]


def pack_kernel(*refs):
    sources, (out_ref, landed, sems) = refs[:-3], refs[-3:]
    heads = out_ref.shape[0]
    rows = landed.shape[1]
    pieces = sems.shape[1]
    piece_rows = rows // pieces
    arrivals = [
        [
            pltpu.make_async_copy(
                source.at[pl.ds(piece * piece_rows, piece_rows), :],
                landed.at[place, pl.ds(piece * piece_rows, piece_rows), :],
                sems.at[place, piece],
            )
            for piece in range(pieces)
        ]
        for place, source in enumerate(sources)
    ]
    for copies in arrivals:
        for copy in copies:
            copy.start()
    for place, copies in enumerate(arrivals):
        for piece, copy in enumerate(copies):
            copy.wait()
            kept_rows = slice(piece * piece_rows, (piece + 1) * piece_rows)
            for head in range(heads):
                out_ref[head, place, kept_rows, :] = landed[
                    place, kept_rows, head * HD : (head + 1) * HD
                ]


def pack_heads(*sources):
    count = len(sources)
    rows = sources[0].shape[0]
    pieces = 4
    return pl.pallas_call(
        pack_kernel,
        out_shape=jax.ShapeDtypeStruct((HEADS, count, rows, HD), jnp.bfloat16),
        in_specs=[pl.BlockSpec(memory_space=pltpu.HBM)] * count,
        out_specs=pl.BlockSpec(memory_space=pltpu.VMEM),
        scratch_shapes=[
            pltpu.VMEM((count, rows, HEADS * HD), jnp.bfloat16),
            pltpu.SemaphoreType.DMA((count, pieces)),
        ],
        compiler_params=pltpu.CompilerParams(vmem_limit_bytes=8 * 1024 * 1024),
        name="pack_heads",
    )(*[pltpu.with_memory_space_constraint(source, pltpu.HBM) for source in sources])


def unpack_kernel(held_ref, out_ref, turned, sems):
    heads = held_ref.shape[0]
    pieces = sems.shape[0]
    piece_rows = turned.shape[0] // pieces
    departures = []
    for piece in range(pieces):
        rows = slice(piece * piece_rows, (piece + 1) * piece_rows)
        for head in range(heads):
            turned[rows, head * HD : (head + 1) * HD] = held_ref[head, rows, :]
        departure = pltpu.make_async_copy(
            turned.at[pl.ds(piece * piece_rows, piece_rows), :],
            out_ref.at[pl.ds(piece * piece_rows, piece_rows), :],
            sems.at[piece],
        )
        departure.start()
        departures.append(departure)
    for departure in departures:
        departure.wait()


def unpack_heads(held):
    heads, rows, depth = held.shape
    return pl.pallas_call(
        unpack_kernel,
        out_shape=jax.ShapeDtypeStruct((rows, heads * depth), jnp.bfloat16),
        in_specs=[pl.BlockSpec(memory_space=pltpu.VMEM)],
        out_specs=pl.BlockSpec(memory_space=pltpu.HBM),
        scratch_shapes=[
            pltpu.VMEM((rows, heads * depth), jnp.bfloat16),
            pltpu.SemaphoreType.DMA((4,)),
        ],
        compiler_params=pltpu.CompilerParams(vmem_limit_bytes=8 * 1024 * 1024),
        name="unpack_heads",
    )(held)


def pipelined(count, score, weigh, blend):
    score(0, 0)
    weigh(0, 0)
    score(1, 1)

    def step(j, carry):
        blend(2 * j, 0)
        weigh(2 * j + 1, 1)
        score(2 * j + 2, 0)
        blend(2 * j + 1, 1)
        weigh(2 * j + 2, 0)
        score(2 * j + 3, 1)
        return carry

    lax.fori_loop(0, count // 2 - 1, step, 0)
    blend(count - 2, 0)
    weigh(count - 1, 1)
    blend(count - 1, 1)


def attend_kernel(axes, kept_hbm, class_hbm, qkv_ref, out_ref, *scratch):
    kept_ref, class_ref, v_all, logits_a, logits_b, weights_a, weights_b, kept_sem, class_sem = scratch
    logits_slots = (logits_a, logits_b)
    weights_slots = (weights_a, weights_b)
    block_count = qkv_ref.shape[0]
    me = own_place(axes)
    exponent_scale = math.log2(math.e) / math.sqrt(HD)
    kept_copy = pltpu.make_async_copy(kept_hbm.at[me], kept_ref, kept_sem)
    class_copy = pltpu.make_async_copy(class_hbm, class_ref, class_sem)
    class_copy.start()
    kept_copy.start()
    v_all[:, :, :HD] = qkv_ref[:, 2]
    v_all[:, :, HD:] = jnp.ones((block_count, BLOCK, HD), jnp.bfloat16)
    class_copy.wait()

    def scores(query_rows, key_rows):
        return lax.dot_general(
            query_rows, key_rows, (((1,), (1,)), ((), ())), preferred_element_type=jnp.float32
        )

    def weigh(first, rows, columns, slot):
        chosen = slice(first, first + rows)
        logits = logits_slots[slot][chosen, :columns]
        largest = jnp.max(logits, axis=-1, keepdims=True)
        weights = jnp.exp2((logits - largest) * exponent_scale).astype(jnp.bfloat16)
        weights_slots[slot][chosen, :columns] = weights

    def normalized(summed):
        return (summed[:, :HD] / summed[:, HD:]).astype(jnp.bfloat16)

    @pl.when(class_ref[me] == 1)
    def _():
        sizes = [2] + [4] * (block_count // 4 - 1) + [2]
        starts = [sum(sizes[:i]) for i in range(len(sizes))]

        parts = 4
        part_blocks = block_count // parts

        def score(i, part):
            rows = sizes[i] * BLOCK
            query_rows = qkv_ref[starts[i] : starts[i] + sizes[i], 0].reshape(rows, HD)
            blocks = slice(part * part_blocks, (part + 1) * part_blocks)
            key_rows = qkv_ref[blocks, 1].reshape(part_blocks * BLOCK, HD)
            columns = slice(part * part_blocks * BLOCK, (part + 1) * part_blocks * BLOCK)
            logits_slots[i % 2][:rows, columns] = scores(query_rows, key_rows)

        def weigh_all(i, part):
            rows = sizes[i] * BLOCK // parts
            weigh(part * rows, rows, block_count * BLOCK, i % 2)

        def blend(i):
            rows = sizes[i] * BLOCK
            value_rows = v_all[...].reshape(block_count * BLOCK, 2 * HD)
            weights = weights_slots[i % 2][:rows, :]
            out = normalized(jnp.dot(weights, value_rows, preferred_element_type=jnp.float32))
            out_ref[starts[i] : starts[i] + sizes[i]] = out.reshape(sizes[i], BLOCK, HD)

        for part in range(parts):
            score(0, part)
        for i in range(len(sizes)):
            if i > 0:
                blend(i - 1)
            for part in range(parts):
                weigh_all(i, part)
                if i + 1 < len(sizes):
                    score(i + 1, part)
        blend(len(sizes) - 1)
        kept_copy.wait()

    @pl.when(class_ref[me] != 1)
    def _():
        kept_copy.wait()
        group = 2

        def block_pairs(block):
            kept_blocks = each_light_block(kept_ref, block)
            return list(zip(kept_blocks[::2], kept_blocks[1::2]))

        def score(i, slot):
            for member in range(group):
                block = group * i + member
                rows = slice(member * BLOCK, (member + 1) * BLOCK)
                for place, (one, other) in enumerate(block_pairs(block)):
                    key_rows = jnp.concatenate([qkv_ref[one, 1], qkv_ref[other, 1]], axis=0)
                    columns = slice(place * 2 * BLOCK, (place + 1) * 2 * BLOCK)
                    logits_slots[slot][rows, columns] = scores(qkv_ref[block, 0], key_rows)

        def blend(i, slot):
            for member in range(group):
                block = group * i + member
                rows = slice(member * BLOCK, (member + 1) * BLOCK)
                summed = jnp.zeros((BLOCK, 2 * HD), jnp.float32)
                for place, (one, other) in enumerate(block_pairs(block)):
                    value_rows = jnp.concatenate([v_all[one], v_all[other]], axis=0)
                    columns = slice(place * 2 * BLOCK, (place + 1) * 2 * BLOCK)
                    weights = weights_slots[slot][rows, columns]
                    summed += jnp.dot(weights, value_rows, preferred_element_type=jnp.float32)
                out_ref[block] = normalized(summed)

        def weigh_few(i, slot):
            weigh(0, group * BLOCK, block_count // KEEP * LIGHT * BLOCK, slot)

        pipelined(block_count // group, score, weigh_few, blend)


def heads_by_device(queries, keys, values, kept, dense_class):
    axes = ("seq", "blk")
    block_count = kept.shape[1]
    in_vmem = pl.BlockSpec(memory_space=pltpu.VMEM)

    def exchange(send):
        return lax.all_to_all(send, axes, split_axis=0, concat_axis=0, tiled=True)

    held = exchange(pack_heads(queries, keys, values))
    stage_rows = 4 * BLOCK
    attended = pl.pallas_call(
        lambda *refs: attend_kernel(axes, *refs),
        out_shape=jax.ShapeDtypeStruct((block_count, BLOCK, HD), jnp.bfloat16),
        in_specs=[
            pl.BlockSpec(memory_space=pl.ANY),
            pl.BlockSpec(memory_space=pl.ANY),
            in_vmem,
        ],
        out_specs=in_vmem,
        scratch_shapes=[
            pltpu.SMEM(kept.shape[1:], jnp.int32),
            pltpu.SMEM(dense_class.shape, jnp.int32),
            pltpu.VMEM((block_count, BLOCK, 2 * HD), jnp.bfloat16),
            pltpu.VMEM((stage_rows, block_count * BLOCK), jnp.float32),
            pltpu.VMEM((stage_rows, block_count * BLOCK), jnp.float32),
            pltpu.VMEM((stage_rows, block_count * BLOCK), jnp.bfloat16),
            pltpu.VMEM((stage_rows, block_count * BLOCK), jnp.bfloat16),
            pltpu.SemaphoreType.DMA,
            pltpu.SemaphoreType.DMA,
        ],
        compiler_params=pltpu.CompilerParams(vmem_limit_bytes=40 * 1024 * 1024),
        name="attend_head",
    )(kept, dense_class, held)
    return unpack_heads(exchange(attended))


def shards(queries, keys, values, kept, dense_class):
    devices = lax.axis_size("seq") * lax.axis_size("blk")
    one_head_each = devices == HEADS
    one_block_each = queries.shape[0] == BLOCK
    every_block_kept = kept.shape[1] == kept.shape[2]
    if one_head_each and one_block_each and every_block_kept:
        return heads_by_device(queries, keys, values, kept, dense_class)
    return spans_by_device(queries, keys, values, kept, dense_class)


def solution(mesh):
    return jax.shard_map(
        shards,
        mesh=mesh,
        in_specs=(
            P(("clip", "seq", "blk"), None),
            P(("clip", "seq", "blk"), None),
            P(("clip", "seq", "blk"), None),
            P(),
            P(),
        ),
        out_specs=P(("clip", "seq", "blk"), None),
        check_vma=False,
    )
```

```python
import math

import jax
import jax.numpy as jnp
from jax import lax
from jax.experimental import pallas as pl
from jax.experimental.pallas import tpu as pltpu
from jax.sharding import PartitionSpec as P

HEADS = 16
HD = 128
BLOCK = 128
KEEP = 4
LIGHT = 2


def combine_spans(partial_out, maxima, totals, along):
    largest = jnp.max(maxima, axis=along, keepdims=True)
    factor = jnp.exp(maxima - largest)
    numerator = jnp.sum(factor[..., None] * partial_out, axis=along)
    denominator = jnp.sum(factor * totals, axis=along)
    return (numerator / denominator[..., None]).astype(jnp.bfloat16)


def attend_blocks(query_rows, key_blocks, blocked_value_rows, local_ids, slot_count):
    query_blocks, part_rows, head_depth = query_rows.shape
    group_size = query_blocks
    while group_size * part_rows > 512 and group_size % 2 == 0:
        group_size = group_size // 2
    logit_scale_factor = 1.0 / math.sqrt(head_depth)
    block_rows = key_blocks.shape[1]

    def one_group(operands):
        queries_group, ids_group = operands
        collected_key_blocks = key_blocks[ids_group].reshape(
            group_size, slot_count * block_rows, head_depth
        )
        gathered_v = blocked_value_rows[ids_group].reshape(
            group_size, slot_count * block_rows, head_depth
        )
        attention_logits = (
            jnp.einsum(
                "gpd,gkd->gpk",
                queries_group,
                collected_key_blocks,
                preferred_element_type=jnp.float32,
            )
            * logit_scale_factor
        )
        maxima = jnp.max(attention_logits, axis=-1)
        weights = jnp.exp(attention_logits - maxima[..., None])
        totals = jnp.sum(weights, axis=-1)
        partial_out = jnp.einsum(
            "gpk,gkd->gpd",
            weights.astype(jnp.bfloat16),
            gathered_v,
            preferred_element_type=jnp.float32,
        )
        return (partial_out, maxima, totals)

    grouped_q = query_rows.reshape(query_blocks // group_size, group_size, part_rows, head_depth)
    grouped_ids = local_ids[:, :slot_count].reshape(
        query_blocks // group_size, group_size, slot_count
    )
    partial_out, maxima, totals = lax.map(one_group, (grouped_q, grouped_ids))
    return (
        partial_out.reshape(query_blocks, part_rows, head_depth),
        maxima.reshape(query_blocks, part_rows),
        totals.reshape(query_blocks, part_rows),
    )


def arrange_heads(stacked):
    swapped = jnp.swapaxes(stacked, 0, 1)
    return swapped.reshape((-1,) + stacked.shape[2:])


def spans_by_device(queries, keys, values, kept, dense_class):
    seq_devices = lax.axis_size("seq")
    span_count = lax.axis_size("blk")
    local_rows = queries.shape[0]
    head_count = HEADS
    head_depth = HD
    local_blocks = local_rows // BLOCK
    row_parts = max(1, 2 * seq_devices // head_count)
    part_rows = BLOCK // row_parts
    item_count = head_count * row_parts
    per_device = item_count // seq_devices
    seq_place = lax.axis_index("seq")
    blk_place = lax.axis_index("blk")
    every_item = jnp.arange(item_count, dtype=jnp.int32)
    all_item_heads = every_item // row_parts
    item_heads = lax.dynamic_slice_in_dim(all_item_heads, seq_place * per_device, per_device)
    grid_q = queries.reshape(local_blocks, row_parts, part_rows, head_count, head_depth).transpose(
        1, 3, 0, 2, 4
    )
    grid_q = grid_q.reshape(row_parts, head_count, local_blocks * part_rows, head_depth)
    head_keys = keys.reshape(local_rows, head_count, head_depth).transpose(1, 0, 2)
    head_values = values.reshape(local_rows, head_count, head_depth).transpose(1, 0, 2)
    send_q = arrange_heads(grid_q)
    q_items = lax.all_to_all(send_q, "seq", split_axis=0, concat_axis=1, tiled=True)
    stride = 1
    grid_k = jnp.broadcast_to(head_keys[None], (row_parts, head_count, local_rows, head_depth))
    grid_v = jnp.broadcast_to(head_values[None], (row_parts, head_count, local_rows, head_depth))
    send_k = arrange_heads(grid_k)
    send_v = arrange_heads(grid_v)
    k_held, v_held = (
        lax.all_to_all(send_k, "seq", split_axis=0, concat_axis=1, tiled=True),
        lax.all_to_all(send_v, "seq", split_axis=0, concat_axis=1, tiled=True),
    )
    key_blocks = k_held.reshape(per_device, seq_devices * local_blocks, BLOCK, head_depth)
    blocked_value_rows = v_held.reshape(per_device, seq_devices * local_blocks, BLOCK, head_depth)
    item_slot = jnp.arange(per_device, dtype=jnp.int32) // stride
    item_class = jnp.take(dense_class, item_heads)
    item_kept = jnp.take(kept, item_heads, axis=0)
    source_index = jnp.arange(seq_devices, dtype=jnp.int32)
    block_index = jnp.arange(local_blocks, dtype=jnp.int32)
    span_index = jnp.arange(span_count, dtype=jnp.int32)
    all_ids = (
        (source_index[None, :, None] * span_count + span_index[:, None, None]) * local_blocks
        + block_index[None, None, :]
    ).reshape(-1)
    all_kept = jnp.take(item_kept, all_ids, axis=1)
    span_ids = lax.dynamic_slice_in_dim(all_kept, blk_place * KEEP, KEEP, axis=2)
    q_all = lax.all_gather(q_items, "blk", axis=1, tiled=True)
    query_rows = q_all.reshape(
        per_device, span_count * seq_devices * local_blocks, part_rows, head_depth
    )

    def one_item(operands):
        rows_item, ids_item, class_item, slot_item = operands
        keys_item = lax.dynamic_index_in_dim(key_blocks, slot_item, 0, keepdims=False)
        values_item = lax.dynamic_index_in_dim(blocked_value_rows, slot_item, 0, keepdims=False)
        return lax.cond(
            class_item == 1,
            lambda: attend_blocks(rows_item, keys_item, values_item, ids_item, KEEP),
            lambda: attend_blocks(rows_item, keys_item, values_item, ids_item, LIGHT),
        )

    partial_out, maxima, totals = lax.map(
        one_item,
        (
            query_rows,
            span_ids // (local_blocks * span_count) * local_blocks + span_ids % local_blocks,
            item_class,
            item_slot,
        ),
    )
    own_blocks = seq_devices * local_blocks
    shaped_out = partial_out.reshape(per_device, span_count, own_blocks, part_rows, head_depth)
    shaped_max = maxima.reshape(per_device, span_count, own_blocks, part_rows)
    shaped_total = totals.reshape(per_device, span_count, own_blocks, part_rows)
    got_out, got_max, got_total = (
        lax.all_to_all(shaped_out, "blk", split_axis=1, concat_axis=1, tiled=True),
        lax.all_to_all(shaped_max, "blk", split_axis=1, concat_axis=1, tiled=True),
        lax.all_to_all(shaped_total, "blk", split_axis=1, concat_axis=1, tiled=True),
    )
    attended_items = combine_spans(got_out, got_max, got_total, 1)
    attended_items = attended_items.reshape(
        per_device, seq_devices * local_blocks * part_rows, head_depth
    )
    returned = lax.all_to_all(attended_items, "seq", split_axis=1, concat_axis=0, tiled=True)
    grid_out = returned.reshape(head_count, row_parts, local_blocks, part_rows, head_depth)
    grid_out = jnp.swapaxes(grid_out, 0, 1)
    return grid_out.transpose(2, 0, 3, 1, 4).reshape(local_rows, head_count * head_depth)


def own_place(axes):
    place = 0
    for axis in axes:
        place = place * lax.axis_size(axis) + lax.axis_index(axis)
    return place


def each_light_block(kept_ref, block):
    return [
        kept_ref[block, span * KEEP + slot]
        for span in range(kept_ref.shape[1] // KEEP)
        for slot in range(LIGHT)
    ]


def pack_kernel(*refs):
    sources, (out_ref, landed, sems) = refs[:-3], refs[-3:]
    heads = out_ref.shape[0]
    rows = landed.shape[1]
    pieces = sems.shape[1]
    piece_rows = rows // pieces
    arrivals = [
        [
            pltpu.make_async_copy(
                source.at[pl.ds(piece * piece_rows, piece_rows), :],
                landed.at[place, pl.ds(piece * piece_rows, piece_rows), :],
                sems.at[place, piece],
            )
            for piece in range(pieces)
        ]
        for place, source in enumerate(sources)
    ]
    for copies in arrivals:
        for copy in copies:
            copy.start()
    for place, copies in enumerate(arrivals):
        for piece, copy in enumerate(copies):
            copy.wait()
            kept_rows = slice(piece * piece_rows, (piece + 1) * piece_rows)
            for head in range(heads):
                out_ref[head, place, kept_rows, :] = landed[
                    place, kept_rows, head * HD : (head + 1) * HD
                ]


def pack_heads(*sources):
    count = len(sources)
    rows = sources[0].shape[0]
    pieces = 4
    return pl.pallas_call(
        pack_kernel,
        out_shape=jax.ShapeDtypeStruct((HEADS, count, rows, HD), jnp.bfloat16),
        in_specs=[pl.BlockSpec(memory_space=pltpu.HBM)] * count,
        out_specs=pl.BlockSpec(memory_space=pltpu.VMEM),
        scratch_shapes=[
            pltpu.VMEM((count, rows, HEADS * HD), jnp.bfloat16),
            pltpu.SemaphoreType.DMA((count, pieces)),
        ],
        compiler_params=pltpu.CompilerParams(vmem_limit_bytes=8 * 1024 * 1024),
        name="pack_heads",
    )(*[pltpu.with_memory_space_constraint(source, pltpu.HBM) for source in sources])


def unpack_kernel(held_ref, out_ref, turned, sems):
    heads = held_ref.shape[0]
    pieces = sems.shape[0]
    piece_rows = turned.shape[0] // pieces
    departures = []
    for piece in range(pieces):
        rows = slice(piece * piece_rows, (piece + 1) * piece_rows)
        for head in range(heads):
            turned[rows, head * HD : (head + 1) * HD] = held_ref[head, rows, :]
        departure = pltpu.make_async_copy(
            turned.at[pl.ds(piece * piece_rows, piece_rows), :],
            out_ref.at[pl.ds(piece * piece_rows, piece_rows), :],
            sems.at[piece],
        )
        departure.start()
        departures.append(departure)
    for departure in departures:
        departure.wait()


def unpack_heads(held):
    heads, rows, depth = held.shape
    return pl.pallas_call(
        unpack_kernel,
        out_shape=jax.ShapeDtypeStruct((rows, heads * depth), jnp.bfloat16),
        in_specs=[pl.BlockSpec(memory_space=pltpu.VMEM)],
        out_specs=pl.BlockSpec(memory_space=pltpu.HBM),
        scratch_shapes=[
            pltpu.VMEM((rows, heads * depth), jnp.bfloat16),
            pltpu.SemaphoreType.DMA((4,)),
        ],
        compiler_params=pltpu.CompilerParams(vmem_limit_bytes=8 * 1024 * 1024),
        name="unpack_heads",
    )(held)


def pipelined(count, score, weigh, blend):
    score(0, 0)
    weigh(0, 0)
    score(1, 1)

    def step(j, carry):
        blend(2 * j, 0)
        weigh(2 * j + 1, 1)
        score(2 * j + 2, 0)
        blend(2 * j + 1, 1)
        weigh(2 * j + 2, 0)
        score(2 * j + 3, 1)
        return carry

    lax.fori_loop(0, count // 2 - 1, step, 0)
    blend(count - 2, 0)
    weigh(count - 1, 1)
    blend(count - 1, 1)


def attend_kernel(axes, kept_hbm, class_hbm, qkv_ref, out_ref, *scratch):
    kept_ref, class_ref, logits_a, logits_b, weights_a, weights_b, totals_a, totals_b, kept_sem, class_sem = scratch
    logits_slots = (logits_a, logits_b)
    weights_slots = (weights_a, weights_b)
    totals_slots = (totals_a, totals_b)
    block_count = qkv_ref.shape[0]
    me = own_place(axes)
    exponent_scale = math.log2(math.e) / math.sqrt(HD)
    kept_copy = pltpu.make_async_copy(kept_hbm.at[me], kept_ref, kept_sem)
    class_copy = pltpu.make_async_copy(class_hbm, class_ref, class_sem)
    class_copy.start()
    kept_copy.start()
    class_copy.wait()

    def scores(query_rows, key_rows):
        return lax.dot_general(
            query_rows, key_rows, (((1,), (1,)), ((), ())), preferred_element_type=jnp.float32
        )

    def weigh(rows, columns, slot):
        logits = logits_slots[slot][:rows, :columns]
        largest = jnp.max(logits, axis=-1, keepdims=True)
        weights = jnp.exp2((logits - largest) * exponent_scale)
        totals = jnp.sum(weights, axis=-1, keepdims=True)
        totals_slots[slot][:rows, :] = jnp.broadcast_to(totals, (rows, HD))
        weights_slots[slot][:rows, :columns] = weights.astype(jnp.bfloat16)

    def normalized(summed, totals):
        return (summed / totals).astype(jnp.bfloat16)

    @pl.when(class_ref[me] == 1)
    def _():
        sizes = [2] + [4] * (block_count // 4 - 1) + [2]
        starts = [sum(sizes[:i]) for i in range(len(sizes))]

        def score(i):
            rows = sizes[i] * BLOCK
            query_rows = qkv_ref[starts[i] : starts[i] + sizes[i], 0].reshape(rows, HD)
            key_rows = qkv_ref[:, 1].reshape(block_count * BLOCK, HD)
            logits_slots[i % 2][:rows, :] = scores(query_rows, key_rows)

        def weigh_all(i):
            weigh(sizes[i] * BLOCK, block_count * BLOCK, i % 2)

        def blend(i):
            rows = sizes[i] * BLOCK
            value_rows = qkv_ref[:, 2].reshape(block_count * BLOCK, HD)
            weights = weights_slots[i % 2][:rows, :]
            summed = jnp.dot(weights, value_rows, preferred_element_type=jnp.float32)
            out = normalized(summed, totals_slots[i % 2][:rows, :])
            out_ref[starts[i] : starts[i] + sizes[i]] = out.reshape(sizes[i], BLOCK, HD)

        score(0)
        weigh_all(0)
        score(1)
        for i in range(1, len(sizes)):
            blend(i - 1)
            weigh_all(i)
            if i + 1 < len(sizes):
                score(i + 1)
        blend(len(sizes) - 1)
        kept_copy.wait()

    @pl.when(class_ref[me] != 1)
    def _():
        kept_copy.wait()
        group = 2

        def block_pairs(block):
            kept_blocks = each_light_block(kept_ref, block)
            return list(zip(kept_blocks[::2], kept_blocks[1::2]))

        def score(i, slot):
            for member in range(group):
                block = group * i + member
                rows = slice(member * BLOCK, (member + 1) * BLOCK)
                for place, (one, other) in enumerate(block_pairs(block)):
                    key_rows = jnp.concatenate([qkv_ref[one, 1], qkv_ref[other, 1]], axis=0)
                    columns = slice(place * 2 * BLOCK, (place + 1) * 2 * BLOCK)
                    logits_slots[slot][rows, columns] = scores(qkv_ref[block, 0], key_rows)

        def blend(i, slot):
            for member in range(group):
                block = group * i + member
                rows = slice(member * BLOCK, (member + 1) * BLOCK)
                summed = jnp.zeros((BLOCK, HD), jnp.float32)
                for place, (one, other) in enumerate(block_pairs(block)):
                    value_rows = jnp.concatenate([qkv_ref[one, 2], qkv_ref[other, 2]], axis=0)
                    columns = slice(place * 2 * BLOCK, (place + 1) * 2 * BLOCK)
                    weights = weights_slots[slot][rows, columns]
                    summed += jnp.dot(weights, value_rows, preferred_element_type=jnp.float32)
                out_ref[block] = normalized(summed, totals_slots[slot][rows, :])

        def weigh_few(i, slot):
            weigh(group * BLOCK, block_count // KEEP * LIGHT * BLOCK, slot)

        pipelined(block_count // group, score, weigh_few, blend)


def heads_by_device(queries, keys, values, kept, dense_class):
    axes = ("seq", "blk")
    block_count = kept.shape[1]
    in_vmem = pl.BlockSpec(memory_space=pltpu.VMEM)

    def exchange(send):
        return lax.all_to_all(send, axes, split_axis=0, concat_axis=0, tiled=True)

    held = exchange(pack_heads(queries, keys, values))
    stage_rows = 4 * BLOCK
    attended = pl.pallas_call(
        lambda *refs: attend_kernel(axes, *refs),
        out_shape=jax.ShapeDtypeStruct((block_count, BLOCK, HD), jnp.bfloat16),
        in_specs=[
            pl.BlockSpec(memory_space=pl.ANY),
            pl.BlockSpec(memory_space=pl.ANY),
            in_vmem,
        ],
        out_specs=in_vmem,
        scratch_shapes=[
            pltpu.SMEM(kept.shape[1:], jnp.int32),
            pltpu.SMEM(dense_class.shape, jnp.int32),
            pltpu.VMEM((stage_rows, block_count * BLOCK), jnp.float32),
            pltpu.VMEM((stage_rows, block_count * BLOCK), jnp.float32),
            pltpu.VMEM((stage_rows, block_count * BLOCK), jnp.bfloat16),
            pltpu.VMEM((stage_rows, block_count * BLOCK), jnp.bfloat16),
            pltpu.VMEM((stage_rows, HD), jnp.float32),
            pltpu.VMEM((stage_rows, HD), jnp.float32),
            pltpu.SemaphoreType.DMA,
            pltpu.SemaphoreType.DMA,
        ],
        compiler_params=pltpu.CompilerParams(vmem_limit_bytes=40 * 1024 * 1024),
        name="attend_head",
    )(kept, dense_class, held)
    return unpack_heads(exchange(attended))


def shards(queries, keys, values, kept, dense_class):
    devices = lax.axis_size("seq") * lax.axis_size("blk")
    one_head_each = devices == HEADS
    one_block_each = queries.shape[0] == BLOCK
    every_block_kept = kept.shape[1] == kept.shape[2]
    if one_head_each and one_block_each and every_block_kept:
        return heads_by_device(queries, keys, values, kept, dense_class)
    return spans_by_device(queries, keys, values, kept, dense_class)


def solution(mesh):
    return jax.shard_map(
        shards,
        mesh=mesh,
        in_specs=(
            P(("clip", "seq", "blk"), None),
            P(("clip", "seq", "blk"), None),
            P(("clip", "seq", "blk"), None),
            P(),
            P(),
        ),
        out_specs=P(("clip", "seq", "blk"), None),
        check_vma=False,
    )
```

```python
import math

import jax
import jax.numpy as jnp
from jax import lax
from jax.experimental import pallas as pl
from jax.experimental.pallas import tpu as pltpu
from jax.sharding import PartitionSpec as P

HEADS = 16
HD = 128
BLOCK = 128
KEEP = 4
LIGHT = 2


def combine_spans(partial_out, maxima, totals, along):
    largest = jnp.max(maxima, axis=along, keepdims=True)
    factor = jnp.exp(maxima - largest)
    numerator = jnp.sum(factor[..., None] * partial_out, axis=along)
    denominator = jnp.sum(factor * totals, axis=along)
    return (numerator / denominator[..., None]).astype(jnp.bfloat16)


def attend_blocks(query_rows, key_blocks, blocked_value_rows, local_ids, slot_count):
    query_blocks, part_rows, head_depth = query_rows.shape
    group_size = query_blocks
    while group_size * part_rows > 512 and group_size % 2 == 0:
        group_size = group_size // 2
    logit_scale_factor = 1.0 / math.sqrt(head_depth)
    block_rows = key_blocks.shape[1]

    def one_group(operands):
        queries_group, ids_group = operands
        collected_key_blocks = key_blocks[ids_group].reshape(
            group_size, slot_count * block_rows, head_depth
        )
        gathered_v = blocked_value_rows[ids_group].reshape(
            group_size, slot_count * block_rows, head_depth
        )
        attention_logits = (
            jnp.einsum(
                "gpd,gkd->gpk",
                queries_group,
                collected_key_blocks,
                preferred_element_type=jnp.float32,
            )
            * logit_scale_factor
        )
        maxima = jnp.max(attention_logits, axis=-1)
        weights = jnp.exp(attention_logits - maxima[..., None])
        totals = jnp.sum(weights, axis=-1)
        partial_out = jnp.einsum(
            "gpk,gkd->gpd",
            weights.astype(jnp.bfloat16),
            gathered_v,
            preferred_element_type=jnp.float32,
        )
        return (partial_out, maxima, totals)

    grouped_q = query_rows.reshape(query_blocks // group_size, group_size, part_rows, head_depth)
    grouped_ids = local_ids[:, :slot_count].reshape(
        query_blocks // group_size, group_size, slot_count
    )
    partial_out, maxima, totals = lax.map(one_group, (grouped_q, grouped_ids))
    return (
        partial_out.reshape(query_blocks, part_rows, head_depth),
        maxima.reshape(query_blocks, part_rows),
        totals.reshape(query_blocks, part_rows),
    )


def arrange_heads(stacked):
    swapped = jnp.swapaxes(stacked, 0, 1)
    return swapped.reshape((-1,) + stacked.shape[2:])


def spans_by_device(queries, keys, values, kept, dense_class):
    seq_devices = lax.axis_size("seq")
    span_count = lax.axis_size("blk")
    local_rows = queries.shape[0]
    head_count = HEADS
    head_depth = HD
    local_blocks = local_rows // BLOCK
    row_parts = max(1, 2 * seq_devices // head_count)
    part_rows = BLOCK // row_parts
    item_count = head_count * row_parts
    per_device = item_count // seq_devices
    seq_place = lax.axis_index("seq")
    blk_place = lax.axis_index("blk")
    every_item = jnp.arange(item_count, dtype=jnp.int32)
    all_item_heads = every_item // row_parts
    item_heads = lax.dynamic_slice_in_dim(all_item_heads, seq_place * per_device, per_device)
    grid_q = queries.reshape(local_blocks, row_parts, part_rows, head_count, head_depth).transpose(
        1, 3, 0, 2, 4
    )
    grid_q = grid_q.reshape(row_parts, head_count, local_blocks * part_rows, head_depth)
    head_keys = keys.reshape(local_rows, head_count, head_depth).transpose(1, 0, 2)
    head_values = values.reshape(local_rows, head_count, head_depth).transpose(1, 0, 2)
    send_q = arrange_heads(grid_q)
    q_items = lax.all_to_all(send_q, "seq", split_axis=0, concat_axis=1, tiled=True)
    stride = 1
    grid_k = jnp.broadcast_to(head_keys[None], (row_parts, head_count, local_rows, head_depth))
    grid_v = jnp.broadcast_to(head_values[None], (row_parts, head_count, local_rows, head_depth))
    send_k = arrange_heads(grid_k)
    send_v = arrange_heads(grid_v)
    k_held, v_held = (
        lax.all_to_all(send_k, "seq", split_axis=0, concat_axis=1, tiled=True),
        lax.all_to_all(send_v, "seq", split_axis=0, concat_axis=1, tiled=True),
    )
    key_blocks = k_held.reshape(per_device, seq_devices * local_blocks, BLOCK, head_depth)
    blocked_value_rows = v_held.reshape(per_device, seq_devices * local_blocks, BLOCK, head_depth)
    item_slot = jnp.arange(per_device, dtype=jnp.int32) // stride
    item_class = jnp.take(dense_class, item_heads)
    item_kept = jnp.take(kept, item_heads, axis=0)
    source_index = jnp.arange(seq_devices, dtype=jnp.int32)
    block_index = jnp.arange(local_blocks, dtype=jnp.int32)
    span_index = jnp.arange(span_count, dtype=jnp.int32)
    all_ids = (
        (source_index[None, :, None] * span_count + span_index[:, None, None]) * local_blocks
        + block_index[None, None, :]
    ).reshape(-1)
    all_kept = jnp.take(item_kept, all_ids, axis=1)
    span_ids = lax.dynamic_slice_in_dim(all_kept, blk_place * KEEP, KEEP, axis=2)
    q_all = lax.all_gather(q_items, "blk", axis=1, tiled=True)
    query_rows = q_all.reshape(
        per_device, span_count * seq_devices * local_blocks, part_rows, head_depth
    )

    def one_item(operands):
        rows_item, ids_item, class_item, slot_item = operands
        keys_item = lax.dynamic_index_in_dim(key_blocks, slot_item, 0, keepdims=False)
        values_item = lax.dynamic_index_in_dim(blocked_value_rows, slot_item, 0, keepdims=False)
        return lax.cond(
            class_item == 1,
            lambda: attend_blocks(rows_item, keys_item, values_item, ids_item, KEEP),
            lambda: attend_blocks(rows_item, keys_item, values_item, ids_item, LIGHT),
        )

    partial_out, maxima, totals = lax.map(
        one_item,
        (
            query_rows,
            span_ids // (local_blocks * span_count) * local_blocks + span_ids % local_blocks,
            item_class,
            item_slot,
        ),
    )
    own_blocks = seq_devices * local_blocks
    shaped_out = partial_out.reshape(per_device, span_count, own_blocks, part_rows, head_depth)
    shaped_max = maxima.reshape(per_device, span_count, own_blocks, part_rows)
    shaped_total = totals.reshape(per_device, span_count, own_blocks, part_rows)
    got_out, got_max, got_total = (
        lax.all_to_all(shaped_out, "blk", split_axis=1, concat_axis=1, tiled=True),
        lax.all_to_all(shaped_max, "blk", split_axis=1, concat_axis=1, tiled=True),
        lax.all_to_all(shaped_total, "blk", split_axis=1, concat_axis=1, tiled=True),
    )
    attended_items = combine_spans(got_out, got_max, got_total, 1)
    attended_items = attended_items.reshape(
        per_device, seq_devices * local_blocks * part_rows, head_depth
    )
    returned = lax.all_to_all(attended_items, "seq", split_axis=1, concat_axis=0, tiled=True)
    grid_out = returned.reshape(head_count, row_parts, local_blocks, part_rows, head_depth)
    grid_out = jnp.swapaxes(grid_out, 0, 1)
    return grid_out.transpose(2, 0, 3, 1, 4).reshape(local_rows, head_count * head_depth)


def own_place(axes):
    place = 0
    for axis in axes:
        place = place * lax.axis_size(axis) + lax.axis_index(axis)
    return place


def each_light_block(kept_ref, block):
    return [
        kept_ref[block, span * KEEP + slot]
        for span in range(kept_ref.shape[1] // KEEP)
        for slot in range(LIGHT)
    ]


def pack_kernel(*refs):
    sources, (out_ref, landed, sems) = refs[:-3], refs[-3:]
    heads = out_ref.shape[0]
    rows = landed.shape[1]
    pieces = sems.shape[1]
    piece_rows = rows // pieces
    arrivals = [
        [
            pltpu.make_async_copy(
                source.at[pl.ds(piece * piece_rows, piece_rows), :],
                landed.at[place, pl.ds(piece * piece_rows, piece_rows), :],
                sems.at[place, piece],
            )
            for piece in range(pieces)
        ]
        for place, source in enumerate(sources)
    ]
    for copies in arrivals:
        for copy in copies:
            copy.start()
    for place, copies in enumerate(arrivals):
        for piece, copy in enumerate(copies):
            copy.wait()
            kept_rows = slice(piece * piece_rows, (piece + 1) * piece_rows)
            for head in range(heads):
                out_ref[head, place, kept_rows, :] = landed[
                    place, kept_rows, head * HD : (head + 1) * HD
                ]


def pack_heads(*sources):
    count = len(sources)
    rows = sources[0].shape[0]
    pieces = 4
    return pl.pallas_call(
        pack_kernel,
        out_shape=jax.ShapeDtypeStruct((HEADS, count, rows, HD), jnp.bfloat16),
        in_specs=[pl.BlockSpec(memory_space=pltpu.HBM)] * count,
        out_specs=pl.BlockSpec(memory_space=pltpu.VMEM),
        scratch_shapes=[
            pltpu.VMEM((count, rows, HEADS * HD), jnp.bfloat16),
            pltpu.SemaphoreType.DMA((count, pieces)),
        ],
        compiler_params=pltpu.CompilerParams(vmem_limit_bytes=8 * 1024 * 1024),
        name="pack_heads",
    )(*[pltpu.with_memory_space_constraint(source, pltpu.HBM) for source in sources])


def unpack_kernel(held_ref, out_ref, turned, sems):
    heads = held_ref.shape[0]
    pieces = sems.shape[0]
    piece_rows = turned.shape[0] // pieces
    departures = []
    for piece in range(pieces):
        rows = slice(piece * piece_rows, (piece + 1) * piece_rows)
        for head in range(heads):
            turned[rows, head * HD : (head + 1) * HD] = held_ref[head, rows, :]
        departure = pltpu.make_async_copy(
            turned.at[pl.ds(piece * piece_rows, piece_rows), :],
            out_ref.at[pl.ds(piece * piece_rows, piece_rows), :],
            sems.at[piece],
        )
        departure.start()
        departures.append(departure)
    for departure in departures:
        departure.wait()


def unpack_heads(held):
    heads, rows, depth = held.shape
    return pl.pallas_call(
        unpack_kernel,
        out_shape=jax.ShapeDtypeStruct((rows, heads * depth), jnp.bfloat16),
        in_specs=[pl.BlockSpec(memory_space=pltpu.VMEM)],
        out_specs=pl.BlockSpec(memory_space=pltpu.HBM),
        scratch_shapes=[
            pltpu.VMEM((rows, heads * depth), jnp.bfloat16),
            pltpu.SemaphoreType.DMA((4,)),
        ],
        compiler_params=pltpu.CompilerParams(vmem_limit_bytes=8 * 1024 * 1024),
        name="unpack_heads",
    )(held)


def pipelined(count, score, weigh, blend):
    score(0, 0)
    weigh(0, 0)
    score(1, 1)

    def step(j, carry):
        blend(2 * j, 0)
        weigh(2 * j + 1, 1)
        score(2 * j + 2, 0)
        blend(2 * j + 1, 1)
        weigh(2 * j + 2, 0)
        score(2 * j + 3, 1)
        return carry

    lax.fori_loop(0, count // 2 - 1, step, 0)
    blend(count - 2, 0)
    weigh(count - 1, 1)
    blend(count - 1, 1)


def attend_kernel(axes, kept_hbm, class_hbm, qkv_ref, out_ref, *scratch):
    kept_ref, class_ref, q_parts, k_twice, v_all, logits_a, logits_b, weights_a, weights_b, kept_sem, class_sem = scratch
    logits_slots = (logits_a, logits_b)
    weights_slots = (weights_a, weights_b)
    block_count = qkv_ref.shape[0]
    me = own_place(axes)
    exponent_scale = math.log2(math.e) / math.sqrt(HD)
    kept_copy = pltpu.make_async_copy(kept_hbm.at[me], kept_ref, kept_sem)
    class_copy = pltpu.make_async_copy(class_hbm, class_ref, class_sem)
    class_copy.start()
    kept_copy.start()
    v_all[:, :, :HD] = qkv_ref[:, 2]
    v_all[:, :, HD:] = jnp.ones((block_count, BLOCK, HD), jnp.bfloat16)
    for block in range(block_count):
        scaled = qkv_ref[block, 0].astype(jnp.float32) * exponent_scale
        high = scaled.astype(jnp.bfloat16)
        q_parts[block, :, :HD] = high
        q_parts[block, :, HD:] = (scaled - high.astype(jnp.float32)).astype(jnp.bfloat16)
        k_twice[block, :, :HD] = qkv_ref[block, 1]
        k_twice[block, :, HD:] = qkv_ref[block, 1]
    class_copy.wait()

    def scores(query_rows, key_rows):
        return lax.dot_general(
            query_rows, key_rows, (((1,), (1,)), ((), ())), preferred_element_type=jnp.float32
        )

    def weigh(rows, columns, slot):
        logits = logits_slots[slot][:rows, :columns]
        largest = jnp.max(logits, axis=-1, keepdims=True)
        weights = jnp.exp2(logits - largest).astype(jnp.bfloat16)
        weights_slots[slot][:rows, :columns] = weights

    def normalized(summed):
        return (summed[:, :HD] / summed[:, HD:]).astype(jnp.bfloat16)

    @pl.when(class_ref[me] == 1)
    def _():
        sizes = [2] + [4] * (block_count // 4 - 1) + [2]
        starts = [sum(sizes[:i]) for i in range(len(sizes))]

        def score(i):
            rows = sizes[i] * BLOCK
            query_rows = q_parts[starts[i] : starts[i] + sizes[i]].reshape(rows, 2 * HD)
            key_rows = k_twice[...].reshape(block_count * BLOCK, 2 * HD)
            logits_slots[i % 2][:rows, :] = scores(query_rows, key_rows)

        def weigh_all(i):
            weigh(sizes[i] * BLOCK, block_count * BLOCK, i % 2)

        def blend(i):
            rows = sizes[i] * BLOCK
            value_rows = v_all[...].reshape(block_count * BLOCK, 2 * HD)
            weights = weights_slots[i % 2][:rows, :]
            out = normalized(jnp.dot(weights, value_rows, preferred_element_type=jnp.float32))
            out_ref[starts[i] : starts[i] + sizes[i]] = out.reshape(sizes[i], BLOCK, HD)

        score(0)
        weigh_all(0)
        score(1)
        for i in range(1, len(sizes)):
            blend(i - 1)
            weigh_all(i)
            if i + 1 < len(sizes):
                score(i + 1)
        blend(len(sizes) - 1)
        kept_copy.wait()

    @pl.when(class_ref[me] != 1)
    def _():
        kept_copy.wait()
        group = 2

        def block_pairs(block):
            kept_blocks = each_light_block(kept_ref, block)
            return list(zip(kept_blocks[::2], kept_blocks[1::2]))

        def score(i, slot):
            for member in range(group):
                block = group * i + member
                rows = slice(member * BLOCK, (member + 1) * BLOCK)
                for place, (one, other) in enumerate(block_pairs(block)):
                    key_rows = jnp.concatenate([k_twice[one], k_twice[other]], axis=0)
                    columns = slice(place * 2 * BLOCK, (place + 1) * 2 * BLOCK)
                    logits_slots[slot][rows, columns] = scores(q_parts[block], key_rows)

        def blend(i, slot):
            for member in range(group):
                block = group * i + member
                rows = slice(member * BLOCK, (member + 1) * BLOCK)
                summed = jnp.zeros((BLOCK, 2 * HD), jnp.float32)
                for place, (one, other) in enumerate(block_pairs(block)):
                    value_rows = jnp.concatenate([v_all[one], v_all[other]], axis=0)
                    columns = slice(place * 2 * BLOCK, (place + 1) * 2 * BLOCK)
                    weights = weights_slots[slot][rows, columns]
                    summed += jnp.dot(weights, value_rows, preferred_element_type=jnp.float32)
                out_ref[block] = normalized(summed)

        def weigh_few(i, slot):
            weigh(group * BLOCK, block_count // KEEP * LIGHT * BLOCK, slot)

        pipelined(block_count // group, score, weigh_few, blend)


def heads_by_device(queries, keys, values, kept, dense_class):
    axes = ("seq", "blk")
    block_count = kept.shape[1]
    in_vmem = pl.BlockSpec(memory_space=pltpu.VMEM)

    def exchange(send):
        return lax.all_to_all(send, axes, split_axis=0, concat_axis=0, tiled=True)

    held = exchange(pack_heads(queries, keys, values))
    stage_rows = 4 * BLOCK
    attended = pl.pallas_call(
        lambda *refs: attend_kernel(axes, *refs),
        out_shape=jax.ShapeDtypeStruct((block_count, BLOCK, HD), jnp.bfloat16),
        in_specs=[
            pl.BlockSpec(memory_space=pl.ANY),
            pl.BlockSpec(memory_space=pl.ANY),
            in_vmem,
        ],
        out_specs=in_vmem,
        scratch_shapes=[
            pltpu.SMEM(kept.shape[1:], jnp.int32),
            pltpu.SMEM(dense_class.shape, jnp.int32),
            pltpu.VMEM((block_count, BLOCK, 2 * HD), jnp.bfloat16),
            pltpu.VMEM((block_count, BLOCK, 2 * HD), jnp.bfloat16),
            pltpu.VMEM((block_count, BLOCK, 2 * HD), jnp.bfloat16),
            pltpu.VMEM((stage_rows, block_count * BLOCK), jnp.float32),
            pltpu.VMEM((stage_rows, block_count * BLOCK), jnp.float32),
            pltpu.VMEM((stage_rows, block_count * BLOCK), jnp.bfloat16),
            pltpu.VMEM((stage_rows, block_count * BLOCK), jnp.bfloat16),
            pltpu.SemaphoreType.DMA,
            pltpu.SemaphoreType.DMA,
        ],
        compiler_params=pltpu.CompilerParams(vmem_limit_bytes=40 * 1024 * 1024),
        name="attend_head",
    )(kept, dense_class, held)
    return unpack_heads(exchange(attended))


def shards(queries, keys, values, kept, dense_class):
    devices = lax.axis_size("seq") * lax.axis_size("blk")
    one_head_each = devices == HEADS
    one_block_each = queries.shape[0] == BLOCK
    every_block_kept = kept.shape[1] == kept.shape[2]
    if one_head_each and one_block_each and every_block_kept:
        return heads_by_device(queries, keys, values, kept, dense_class)
    return spans_by_device(queries, keys, values, kept, dense_class)


def solution(mesh):
    return jax.shard_map(
        shards,
        mesh=mesh,
        in_specs=(
            P(("clip", "seq", "blk"), None),
            P(("clip", "seq", "blk"), None),
            P(("clip", "seq", "blk"), None),
            P(),
            P(),
        ),
        out_specs=P(("clip", "seq", "blk"), None),
        check_vma=False,
    )
```

```python
import math

import jax
import jax.numpy as jnp
from jax import lax
from jax.experimental import pallas as pl
from jax.experimental.pallas import tpu as pltpu
from jax.sharding import PartitionSpec as P

HEADS = 16
HD = 128
BLOCK = 128
KEEP = 4
LIGHT = 2


def combine_spans(partial_out, maxima, totals, along):
    largest = jnp.max(maxima, axis=along, keepdims=True)
    factor = jnp.exp(maxima - largest)
    numerator = jnp.sum(factor[..., None] * partial_out, axis=along)
    denominator = jnp.sum(factor * totals, axis=along)
    return (numerator / denominator[..., None]).astype(jnp.bfloat16)


def attend_blocks(query_rows, key_blocks, blocked_value_rows, local_ids, slot_count):
    query_blocks, part_rows, head_depth = query_rows.shape
    group_size = query_blocks
    while group_size * part_rows > 512 and group_size % 2 == 0:
        group_size = group_size // 2
    logit_scale_factor = 1.0 / math.sqrt(head_depth)
    block_rows = key_blocks.shape[1]

    def one_group(operands):
        queries_group, ids_group = operands
        collected_key_blocks = key_blocks[ids_group].reshape(
            group_size, slot_count * block_rows, head_depth
        )
        gathered_v = blocked_value_rows[ids_group].reshape(
            group_size, slot_count * block_rows, head_depth
        )
        attention_logits = (
            jnp.einsum(
                "gpd,gkd->gpk",
                queries_group,
                collected_key_blocks,
                preferred_element_type=jnp.float32,
            )
            * logit_scale_factor
        )
        maxima = jnp.max(attention_logits, axis=-1)
        weights = jnp.exp(attention_logits - maxima[..., None])
        totals = jnp.sum(weights, axis=-1)
        partial_out = jnp.einsum(
            "gpk,gkd->gpd",
            weights.astype(jnp.bfloat16),
            gathered_v,
            preferred_element_type=jnp.float32,
        )
        return (partial_out, maxima, totals)

    grouped_q = query_rows.reshape(query_blocks // group_size, group_size, part_rows, head_depth)
    grouped_ids = local_ids[:, :slot_count].reshape(
        query_blocks // group_size, group_size, slot_count
    )
    partial_out, maxima, totals = lax.map(one_group, (grouped_q, grouped_ids))
    return (
        partial_out.reshape(query_blocks, part_rows, head_depth),
        maxima.reshape(query_blocks, part_rows),
        totals.reshape(query_blocks, part_rows),
    )


def arrange_heads(stacked):
    swapped = jnp.swapaxes(stacked, 0, 1)
    return swapped.reshape((-1,) + stacked.shape[2:])


def spans_by_device(queries, keys, values, kept, dense_class):
    seq_devices = lax.axis_size("seq")
    span_count = lax.axis_size("blk")
    local_rows = queries.shape[0]
    head_count = HEADS
    head_depth = HD
    local_blocks = local_rows // BLOCK
    row_parts = max(1, 2 * seq_devices // head_count)
    part_rows = BLOCK // row_parts
    item_count = head_count * row_parts
    per_device = item_count // seq_devices
    seq_place = lax.axis_index("seq")
    blk_place = lax.axis_index("blk")
    every_item = jnp.arange(item_count, dtype=jnp.int32)
    all_item_heads = every_item // row_parts
    item_heads = lax.dynamic_slice_in_dim(all_item_heads, seq_place * per_device, per_device)
    grid_q = queries.reshape(local_blocks, row_parts, part_rows, head_count, head_depth).transpose(
        1, 3, 0, 2, 4
    )
    grid_q = grid_q.reshape(row_parts, head_count, local_blocks * part_rows, head_depth)
    head_keys = keys.reshape(local_rows, head_count, head_depth).transpose(1, 0, 2)
    head_values = values.reshape(local_rows, head_count, head_depth).transpose(1, 0, 2)
    send_q = arrange_heads(grid_q)
    q_items = lax.all_to_all(send_q, "seq", split_axis=0, concat_axis=1, tiled=True)
    stride = 1
    grid_k = jnp.broadcast_to(head_keys[None], (row_parts, head_count, local_rows, head_depth))
    grid_v = jnp.broadcast_to(head_values[None], (row_parts, head_count, local_rows, head_depth))
    send_k = arrange_heads(grid_k)
    send_v = arrange_heads(grid_v)
    k_held, v_held = (
        lax.all_to_all(send_k, "seq", split_axis=0, concat_axis=1, tiled=True),
        lax.all_to_all(send_v, "seq", split_axis=0, concat_axis=1, tiled=True),
    )
    key_blocks = k_held.reshape(per_device, seq_devices * local_blocks, BLOCK, head_depth)
    blocked_value_rows = v_held.reshape(per_device, seq_devices * local_blocks, BLOCK, head_depth)
    item_slot = jnp.arange(per_device, dtype=jnp.int32) // stride
    item_class = jnp.take(dense_class, item_heads)
    item_kept = jnp.take(kept, item_heads, axis=0)
    source_index = jnp.arange(seq_devices, dtype=jnp.int32)
    block_index = jnp.arange(local_blocks, dtype=jnp.int32)
    span_index = jnp.arange(span_count, dtype=jnp.int32)
    all_ids = (
        (source_index[None, :, None] * span_count + span_index[:, None, None]) * local_blocks
        + block_index[None, None, :]
    ).reshape(-1)
    all_kept = jnp.take(item_kept, all_ids, axis=1)
    span_ids = lax.dynamic_slice_in_dim(all_kept, blk_place * KEEP, KEEP, axis=2)
    q_all = lax.all_gather(q_items, "blk", axis=1, tiled=True)
    query_rows = q_all.reshape(
        per_device, span_count * seq_devices * local_blocks, part_rows, head_depth
    )

    def one_item(operands):
        rows_item, ids_item, class_item, slot_item = operands
        keys_item = lax.dynamic_index_in_dim(key_blocks, slot_item, 0, keepdims=False)
        values_item = lax.dynamic_index_in_dim(blocked_value_rows, slot_item, 0, keepdims=False)
        return lax.cond(
            class_item == 1,
            lambda: attend_blocks(rows_item, keys_item, values_item, ids_item, KEEP),
            lambda: attend_blocks(rows_item, keys_item, values_item, ids_item, LIGHT),
        )

    partial_out, maxima, totals = lax.map(
        one_item,
        (
            query_rows,
            span_ids // (local_blocks * span_count) * local_blocks + span_ids % local_blocks,
            item_class,
            item_slot,
        ),
    )
    own_blocks = seq_devices * local_blocks
    shaped_out = partial_out.reshape(per_device, span_count, own_blocks, part_rows, head_depth)
    shaped_max = maxima.reshape(per_device, span_count, own_blocks, part_rows)
    shaped_total = totals.reshape(per_device, span_count, own_blocks, part_rows)
    got_out, got_max, got_total = (
        lax.all_to_all(shaped_out, "blk", split_axis=1, concat_axis=1, tiled=True),
        lax.all_to_all(shaped_max, "blk", split_axis=1, concat_axis=1, tiled=True),
        lax.all_to_all(shaped_total, "blk", split_axis=1, concat_axis=1, tiled=True),
    )
    attended_items = combine_spans(got_out, got_max, got_total, 1)
    attended_items = attended_items.reshape(
        per_device, seq_devices * local_blocks * part_rows, head_depth
    )
    returned = lax.all_to_all(attended_items, "seq", split_axis=1, concat_axis=0, tiled=True)
    grid_out = returned.reshape(head_count, row_parts, local_blocks, part_rows, head_depth)
    grid_out = jnp.swapaxes(grid_out, 0, 1)
    return grid_out.transpose(2, 0, 3, 1, 4).reshape(local_rows, head_count * head_depth)


def own_place(axes):
    place = 0
    for axis in axes:
        place = place * lax.axis_size(axis) + lax.axis_index(axis)
    return place


def each_light_block(kept_ref, block):
    return [
        kept_ref[block, span * KEEP + slot]
        for span in range(kept_ref.shape[1] // KEEP)
        for slot in range(LIGHT)
    ]


def pack_kernel(*refs):
    sources, (out_ref, landed, sems) = refs[:-3], refs[-3:]
    heads = out_ref.shape[0]
    rows = landed.shape[1]
    pieces = sems.shape[1]
    piece_rows = rows // pieces
    arrivals = [
        [
            pltpu.make_async_copy(
                source.at[pl.ds(piece * piece_rows, piece_rows), :],
                landed.at[place, pl.ds(piece * piece_rows, piece_rows), :],
                sems.at[place, piece],
            )
            for piece in range(pieces)
        ]
        for place, source in enumerate(sources)
    ]
    for copies in arrivals:
        for copy in copies:
            copy.start()
    for place, copies in enumerate(arrivals):
        for piece, copy in enumerate(copies):
            copy.wait()
            kept_rows = slice(piece * piece_rows, (piece + 1) * piece_rows)
            for head in range(heads):
                out_ref[head, place, kept_rows, :] = landed[
                    place, kept_rows, head * HD : (head + 1) * HD
                ]


def pack_heads(*sources):
    count = len(sources)
    rows = sources[0].shape[0]
    pieces = 4
    return pl.pallas_call(
        pack_kernel,
        out_shape=jax.ShapeDtypeStruct((HEADS, count, rows, HD), jnp.bfloat16),
        in_specs=[pl.BlockSpec(memory_space=pltpu.HBM)] * count,
        out_specs=pl.BlockSpec(memory_space=pltpu.VMEM),
        scratch_shapes=[
            pltpu.VMEM((count, rows, HEADS * HD), jnp.bfloat16),
            pltpu.SemaphoreType.DMA((count, pieces)),
        ],
        compiler_params=pltpu.CompilerParams(vmem_limit_bytes=8 * 1024 * 1024),
        name="pack_heads",
    )(*[pltpu.with_memory_space_constraint(source, pltpu.HBM) for source in sources])


def unpack_kernel(held_ref, out_ref, turned, sems):
    heads = held_ref.shape[0]
    pieces = sems.shape[0]
    piece_rows = turned.shape[0] // pieces
    departures = []
    for piece in range(pieces):
        rows = slice(piece * piece_rows, (piece + 1) * piece_rows)
        for head in range(heads):
            turned[rows, head * HD : (head + 1) * HD] = held_ref[head, rows, :]
        departure = pltpu.make_async_copy(
            turned.at[pl.ds(piece * piece_rows, piece_rows), :],
            out_ref.at[pl.ds(piece * piece_rows, piece_rows), :],
            sems.at[piece],
        )
        departure.start()
        departures.append(departure)
    for departure in departures:
        departure.wait()


def unpack_heads(held):
    heads, rows, depth = held.shape
    return pl.pallas_call(
        unpack_kernel,
        out_shape=jax.ShapeDtypeStruct((rows, heads * depth), jnp.bfloat16),
        in_specs=[pl.BlockSpec(memory_space=pltpu.VMEM)],
        out_specs=pl.BlockSpec(memory_space=pltpu.HBM),
        scratch_shapes=[
            pltpu.VMEM((rows, heads * depth), jnp.bfloat16),
            pltpu.SemaphoreType.DMA((4,)),
        ],
        compiler_params=pltpu.CompilerParams(vmem_limit_bytes=8 * 1024 * 1024),
        name="unpack_heads",
    )(held)


def pipelined(count, score, weigh, blend):
    score(0, 0)
    weigh(0, 0)
    score(1, 1)

    def step(j, carry):
        blend(2 * j, 0)
        weigh(2 * j + 1, 1)
        score(2 * j + 2, 0)
        blend(2 * j + 1, 1)
        weigh(2 * j + 2, 0)
        score(2 * j + 3, 1)
        return carry

    lax.fori_loop(0, count // 2 - 1, step, 0)
    blend(count - 2, 0)
    weigh(count - 1, 1)
    blend(count - 1, 1)


def attend_kernel(axes, kept_hbm, class_hbm, qkv_ref, out_ref, *scratch):
    kept_ref, class_ref, v_all, logits_a, logits_b, weights_a, weights_b, kept_sem, class_sem = scratch
    logits_slots = (logits_a, logits_b)
    weights_slots = (weights_a, weights_b)
    block_count = qkv_ref.shape[0]
    me = own_place(axes)
    exponent_scale = math.log2(math.e) / math.sqrt(HD)
    kept_copy = pltpu.make_async_copy(kept_hbm.at[me], kept_ref, kept_sem)
    class_copy = pltpu.make_async_copy(class_hbm, class_ref, class_sem)
    class_copy.start()
    kept_copy.start()
    v_all[:, :, :HD] = qkv_ref[:, 2]
    v_all[:, :, HD:] = jnp.ones((block_count, BLOCK, HD), jnp.bfloat16)
    class_copy.wait()

    def scores(query_rows, key_rows):
        return lax.dot_general(
            query_rows, key_rows, (((1,), (1,)), ((), ())), preferred_element_type=jnp.float32
        )

    def weigh(rows, columns, slot, scale=None):
        logits = logits_slots[slot][:rows, :columns]
        largest = jnp.max(logits, axis=-1, keepdims=True)
        below = logits - largest
        if scale is not None:
            below = below * scale
        weights_slots[slot][:rows, :columns] = jnp.exp2(below).astype(jnp.bfloat16)

    def normalized(summed):
        return (summed[:, :HD] / summed[:, HD:]).astype(jnp.bfloat16)

    @pl.when(class_ref[me] == 1)
    def _():
        sizes = [2] + [4] * (block_count // 4 - 1) + [2]
        starts = [sum(sizes[:i]) for i in range(len(sizes))]

        def score(i):
            rows = sizes[i] * BLOCK
            query_rows = qkv_ref[starts[i] : starts[i] + sizes[i], 0].reshape(rows, HD)
            scaled = query_rows.astype(jnp.float32) * exponent_scale
            high = scaled.astype(jnp.bfloat16)
            low = (scaled - high.astype(jnp.float32)).astype(jnp.bfloat16)
            key_rows = qkv_ref[:, 1].reshape(block_count * BLOCK, HD)
            logits_slots[i % 2][:rows, :] = scores(
                jnp.concatenate([high, low], axis=1), jnp.concatenate([key_rows, key_rows], axis=1)
            )

        def weigh_all(i):
            weigh(sizes[i] * BLOCK, block_count * BLOCK, i % 2)

        def blend(i):
            rows = sizes[i] * BLOCK
            value_rows = v_all[...].reshape(block_count * BLOCK, 2 * HD)
            weights = weights_slots[i % 2][:rows, :]
            out = normalized(jnp.dot(weights, value_rows, preferred_element_type=jnp.float32))
            out_ref[starts[i] : starts[i] + sizes[i]] = out.reshape(sizes[i], BLOCK, HD)

        score(0)
        weigh_all(0)
        score(1)
        for i in range(1, len(sizes)):
            blend(i - 1)
            weigh_all(i)
            if i + 1 < len(sizes):
                score(i + 1)
        blend(len(sizes) - 1)
        kept_copy.wait()

    @pl.when(class_ref[me] != 1)
    def _():
        kept_copy.wait()
        group = 2

        def block_pairs(block):
            kept_blocks = each_light_block(kept_ref, block)
            return list(zip(kept_blocks[::2], kept_blocks[1::2]))

        def score(i, slot):
            for member in range(group):
                block = group * i + member
                rows = slice(member * BLOCK, (member + 1) * BLOCK)
                for place, (one, other) in enumerate(block_pairs(block)):
                    key_rows = jnp.concatenate([qkv_ref[one, 1], qkv_ref[other, 1]], axis=0)
                    columns = slice(place * 2 * BLOCK, (place + 1) * 2 * BLOCK)
                    logits_slots[slot][rows, columns] = scores(qkv_ref[block, 0], key_rows)

        def blend(i, slot):
            for member in range(group):
                block = group * i + member
                rows = slice(member * BLOCK, (member + 1) * BLOCK)
                summed = jnp.zeros((BLOCK, 2 * HD), jnp.float32)
                for place, (one, other) in enumerate(block_pairs(block)):
                    value_rows = jnp.concatenate([v_all[one], v_all[other]], axis=0)
                    columns = slice(place * 2 * BLOCK, (place + 1) * 2 * BLOCK)
                    weights = weights_slots[slot][rows, columns]
                    summed += jnp.dot(weights, value_rows, preferred_element_type=jnp.float32)
                out_ref[block] = normalized(summed)

        def weigh_few(i, slot):
            weigh(group * BLOCK, block_count // KEEP * LIGHT * BLOCK, slot, exponent_scale)

        pipelined(block_count // group, score, weigh_few, blend)


def heads_by_device(queries, keys, values, kept, dense_class):
    axes = ("seq", "blk")
    block_count = kept.shape[1]
    in_vmem = pl.BlockSpec(memory_space=pltpu.VMEM)

    def exchange(send):
        return lax.all_to_all(send, axes, split_axis=0, concat_axis=0, tiled=True)

    held = exchange(pack_heads(queries, keys, values))
    stage_rows = 4 * BLOCK
    attended = pl.pallas_call(
        lambda *refs: attend_kernel(axes, *refs),
        out_shape=jax.ShapeDtypeStruct((block_count, BLOCK, HD), jnp.bfloat16),
        in_specs=[
            pl.BlockSpec(memory_space=pl.ANY),
            pl.BlockSpec(memory_space=pl.ANY),
            in_vmem,
        ],
        out_specs=in_vmem,
        scratch_shapes=[
            pltpu.SMEM(kept.shape[1:], jnp.int32),
            pltpu.SMEM(dense_class.shape, jnp.int32),
            pltpu.VMEM((block_count, BLOCK, 2 * HD), jnp.bfloat16),
            pltpu.VMEM((stage_rows, block_count * BLOCK), jnp.float32),
            pltpu.VMEM((stage_rows, block_count * BLOCK), jnp.float32),
            pltpu.VMEM((stage_rows, block_count * BLOCK), jnp.bfloat16),
            pltpu.VMEM((stage_rows, block_count * BLOCK), jnp.bfloat16),
            pltpu.SemaphoreType.DMA,
            pltpu.SemaphoreType.DMA,
        ],
        compiler_params=pltpu.CompilerParams(vmem_limit_bytes=40 * 1024 * 1024),
        name="attend_head",
    )(kept, dense_class, held)
    return unpack_heads(exchange(attended))


def shards(queries, keys, values, kept, dense_class):
    devices = lax.axis_size("seq") * lax.axis_size("blk")
    one_head_each = devices == HEADS
    one_block_each = queries.shape[0] == BLOCK
    every_block_kept = kept.shape[1] == kept.shape[2]
    if one_head_each and one_block_each and every_block_kept:
        return heads_by_device(queries, keys, values, kept, dense_class)
    return spans_by_device(queries, keys, values, kept, dense_class)


def solution(mesh):
    return jax.shard_map(
        shards,
        mesh=mesh,
        in_specs=(
            P(("clip", "seq", "blk"), None),
            P(("clip", "seq", "blk"), None),
            P(("clip", "seq", "blk"), None),
            P(),
            P(),
        ),
        out_specs=P(("clip", "seq", "blk"), None),
        check_vma=False,
    )
```

```python
import math

import jax
import jax.numpy as jnp
from jax import lax
from jax.experimental import pallas as pl
from jax.experimental.pallas import tpu as pltpu
from jax.sharding import PartitionSpec as P

HEADS = 16
HD = 128
BLOCK = 128
KEEP = 4
LIGHT = 2


def combine_spans(partial_out, maxima, totals, along):
    largest = jnp.max(maxima, axis=along, keepdims=True)
    factor = jnp.exp(maxima - largest)
    numerator = jnp.sum(factor[..., None] * partial_out, axis=along)
    denominator = jnp.sum(factor * totals, axis=along)
    return (numerator / denominator[..., None]).astype(jnp.bfloat16)


def attend_blocks(query_rows, key_blocks, blocked_value_rows, local_ids, slot_count):
    query_blocks, part_rows, head_depth = query_rows.shape
    group_size = query_blocks
    while group_size * part_rows > 512 and group_size % 2 == 0:
        group_size = group_size // 2
    logit_scale_factor = 1.0 / math.sqrt(head_depth)
    block_rows = key_blocks.shape[1]

    def one_group(operands):
        queries_group, ids_group = operands
        collected_key_blocks = key_blocks[ids_group].reshape(
            group_size, slot_count * block_rows, head_depth
        )
        gathered_v = blocked_value_rows[ids_group].reshape(
            group_size, slot_count * block_rows, head_depth
        )
        attention_logits = (
            jnp.einsum(
                "gpd,gkd->gpk",
                queries_group,
                collected_key_blocks,
                preferred_element_type=jnp.float32,
            )
            * logit_scale_factor
        )
        maxima = jnp.max(attention_logits, axis=-1)
        weights = jnp.exp(attention_logits - maxima[..., None])
        totals = jnp.sum(weights, axis=-1)
        partial_out = jnp.einsum(
            "gpk,gkd->gpd",
            weights.astype(jnp.bfloat16),
            gathered_v,
            preferred_element_type=jnp.float32,
        )
        return (partial_out, maxima, totals)

    grouped_q = query_rows.reshape(query_blocks // group_size, group_size, part_rows, head_depth)
    grouped_ids = local_ids[:, :slot_count].reshape(
        query_blocks // group_size, group_size, slot_count
    )
    partial_out, maxima, totals = lax.map(one_group, (grouped_q, grouped_ids))
    return (
        partial_out.reshape(query_blocks, part_rows, head_depth),
        maxima.reshape(query_blocks, part_rows),
        totals.reshape(query_blocks, part_rows),
    )


def arrange_heads(stacked):
    swapped = jnp.swapaxes(stacked, 0, 1)
    return swapped.reshape((-1,) + stacked.shape[2:])


def spans_by_device(queries, keys, values, kept, dense_class):
    seq_devices = lax.axis_size("seq")
    span_count = lax.axis_size("blk")
    local_rows = queries.shape[0]
    head_count = HEADS
    head_depth = HD
    local_blocks = local_rows // BLOCK
    row_parts = max(1, 2 * seq_devices // head_count)
    part_rows = BLOCK // row_parts
    item_count = head_count * row_parts
    per_device = item_count // seq_devices
    seq_place = lax.axis_index("seq")
    blk_place = lax.axis_index("blk")
    every_item = jnp.arange(item_count, dtype=jnp.int32)
    all_item_heads = every_item // row_parts
    item_heads = lax.dynamic_slice_in_dim(all_item_heads, seq_place * per_device, per_device)
    grid_q = queries.reshape(local_blocks, row_parts, part_rows, head_count, head_depth).transpose(
        1, 3, 0, 2, 4
    )
    grid_q = grid_q.reshape(row_parts, head_count, local_blocks * part_rows, head_depth)
    head_keys = keys.reshape(local_rows, head_count, head_depth).transpose(1, 0, 2)
    head_values = values.reshape(local_rows, head_count, head_depth).transpose(1, 0, 2)
    send_q = arrange_heads(grid_q)
    q_items = lax.all_to_all(send_q, "seq", split_axis=0, concat_axis=1, tiled=True)
    stride = 1
    grid_k = jnp.broadcast_to(head_keys[None], (row_parts, head_count, local_rows, head_depth))
    grid_v = jnp.broadcast_to(head_values[None], (row_parts, head_count, local_rows, head_depth))
    send_k = arrange_heads(grid_k)
    send_v = arrange_heads(grid_v)
    k_held, v_held = (
        lax.all_to_all(send_k, "seq", split_axis=0, concat_axis=1, tiled=True),
        lax.all_to_all(send_v, "seq", split_axis=0, concat_axis=1, tiled=True),
    )
    key_blocks = k_held.reshape(per_device, seq_devices * local_blocks, BLOCK, head_depth)
    blocked_value_rows = v_held.reshape(per_device, seq_devices * local_blocks, BLOCK, head_depth)
    item_slot = jnp.arange(per_device, dtype=jnp.int32) // stride
    item_class = jnp.take(dense_class, item_heads)
    item_kept = jnp.take(kept, item_heads, axis=0)
    source_index = jnp.arange(seq_devices, dtype=jnp.int32)
    block_index = jnp.arange(local_blocks, dtype=jnp.int32)
    span_index = jnp.arange(span_count, dtype=jnp.int32)
    all_ids = (
        (source_index[None, :, None] * span_count + span_index[:, None, None]) * local_blocks
        + block_index[None, None, :]
    ).reshape(-1)
    all_kept = jnp.take(item_kept, all_ids, axis=1)
    span_ids = lax.dynamic_slice_in_dim(all_kept, blk_place * KEEP, KEEP, axis=2)
    q_all = lax.all_gather(q_items, "blk", axis=1, tiled=True)
    query_rows = q_all.reshape(
        per_device, span_count * seq_devices * local_blocks, part_rows, head_depth
    )

    def one_item(operands):
        rows_item, ids_item, class_item, slot_item = operands
        keys_item = lax.dynamic_index_in_dim(key_blocks, slot_item, 0, keepdims=False)
        values_item = lax.dynamic_index_in_dim(blocked_value_rows, slot_item, 0, keepdims=False)
        return lax.cond(
            class_item == 1,
            lambda: attend_blocks(rows_item, keys_item, values_item, ids_item, KEEP),
            lambda: attend_blocks(rows_item, keys_item, values_item, ids_item, LIGHT),
        )

    partial_out, maxima, totals = lax.map(
        one_item,
        (
            query_rows,
            span_ids // (local_blocks * span_count) * local_blocks + span_ids % local_blocks,
            item_class,
            item_slot,
        ),
    )
    own_blocks = seq_devices * local_blocks
    shaped_out = partial_out.reshape(per_device, span_count, own_blocks, part_rows, head_depth)
    shaped_max = maxima.reshape(per_device, span_count, own_blocks, part_rows)
    shaped_total = totals.reshape(per_device, span_count, own_blocks, part_rows)
    got_out, got_max, got_total = (
        lax.all_to_all(shaped_out, "blk", split_axis=1, concat_axis=1, tiled=True),
        lax.all_to_all(shaped_max, "blk", split_axis=1, concat_axis=1, tiled=True),
        lax.all_to_all(shaped_total, "blk", split_axis=1, concat_axis=1, tiled=True),
    )
    attended_items = combine_spans(got_out, got_max, got_total, 1)
    attended_items = attended_items.reshape(
        per_device, seq_devices * local_blocks * part_rows, head_depth
    )
    returned = lax.all_to_all(attended_items, "seq", split_axis=1, concat_axis=0, tiled=True)
    grid_out = returned.reshape(head_count, row_parts, local_blocks, part_rows, head_depth)
    grid_out = jnp.swapaxes(grid_out, 0, 1)
    return grid_out.transpose(2, 0, 3, 1, 4).reshape(local_rows, head_count * head_depth)


def own_place(axes):
    place = 0
    for axis in axes:
        place = place * lax.axis_size(axis) + lax.axis_index(axis)
    return place


def each_light_block(kept_ref, block):
    return [
        kept_ref[block, span * KEEP + slot]
        for span in range(kept_ref.shape[1] // KEEP)
        for slot in range(LIGHT)
    ]


def pack_kernel(*refs):
    sources, (out_ref, landed, sems) = refs[:-3], refs[-3:]
    heads = out_ref.shape[0]
    rows = landed.shape[1]
    pieces = sems.shape[1]
    piece_rows = rows // pieces
    arrivals = [
        [
            pltpu.make_async_copy(
                source.at[pl.ds(piece * piece_rows, piece_rows), :],
                landed.at[place, pl.ds(piece * piece_rows, piece_rows), :],
                sems.at[place, piece],
            )
            for piece in range(pieces)
        ]
        for place, source in enumerate(sources)
    ]
    for copies in arrivals:
        for copy in copies:
            copy.start()
    for place, copies in enumerate(arrivals):
        for piece, copy in enumerate(copies):
            copy.wait()
            kept_rows = slice(piece * piece_rows, (piece + 1) * piece_rows)
            for head in range(heads):
                out_ref[head, place, kept_rows, :] = landed[
                    place, kept_rows, head * HD : (head + 1) * HD
                ]


def pack_heads(*sources):
    count = len(sources)
    rows = sources[0].shape[0]
    pieces = 4
    return pl.pallas_call(
        pack_kernel,
        out_shape=jax.ShapeDtypeStruct((HEADS, count, rows, HD), jnp.bfloat16),
        in_specs=[pl.BlockSpec(memory_space=pltpu.HBM)] * count,
        out_specs=pl.BlockSpec(memory_space=pltpu.VMEM),
        scratch_shapes=[
            pltpu.VMEM((count, rows, HEADS * HD), jnp.bfloat16),
            pltpu.SemaphoreType.DMA((count, pieces)),
        ],
        compiler_params=pltpu.CompilerParams(vmem_limit_bytes=8 * 1024 * 1024),
        name="pack_heads",
    )(*[pltpu.with_memory_space_constraint(source, pltpu.HBM) for source in sources])


def unpack_kernel(held_ref, out_ref, turned, sems):
    heads = held_ref.shape[0]
    pieces = sems.shape[0]
    piece_rows = turned.shape[0] // pieces
    departures = []
    for piece in range(pieces):
        rows = slice(piece * piece_rows, (piece + 1) * piece_rows)
        for head in range(heads):
            turned[rows, head * HD : (head + 1) * HD] = held_ref[head, rows, :]
        departure = pltpu.make_async_copy(
            turned.at[pl.ds(piece * piece_rows, piece_rows), :],
            out_ref.at[pl.ds(piece * piece_rows, piece_rows), :],
            sems.at[piece],
        )
        departure.start()
        departures.append(departure)
    for departure in departures:
        departure.wait()


def unpack_heads(held):
    heads, rows, depth = held.shape
    return pl.pallas_call(
        unpack_kernel,
        out_shape=jax.ShapeDtypeStruct((rows, heads * depth), jnp.bfloat16),
        in_specs=[pl.BlockSpec(memory_space=pltpu.VMEM)],
        out_specs=pl.BlockSpec(memory_space=pltpu.HBM),
        scratch_shapes=[
            pltpu.VMEM((rows, heads * depth), jnp.bfloat16),
            pltpu.SemaphoreType.DMA((4,)),
        ],
        compiler_params=pltpu.CompilerParams(vmem_limit_bytes=8 * 1024 * 1024),
        name="unpack_heads",
    )(held)


def pipelined(count, score, weigh, blend):
    score(0, 0)
    weigh(0, 0)
    score(1, 1)

    def step(j, carry):
        blend(2 * j, 0)
        weigh(2 * j + 1, 1)
        score(2 * j + 2, 0)
        blend(2 * j + 1, 1)
        weigh(2 * j + 2, 0)
        score(2 * j + 3, 1)
        return carry

    lax.fori_loop(0, count // 2 - 1, step, 0)
    blend(count - 2, 0)
    weigh(count - 1, 1)
    blend(count - 1, 1)


def attend_kernel(axes, kept_hbm, class_hbm, qkv_ref, out_ref, *scratch):
    kept_ref, class_ref, v_all, logits_a, logits_b, weights_a, weights_b, kept_sem, class_sem = scratch
    logits_slots = (logits_a, logits_b)
    weights_slots = (weights_a, weights_b)
    block_count = qkv_ref.shape[0]
    me = own_place(axes)
    exponent_scale = math.log2(math.e) / math.sqrt(HD)
    kept_copy = pltpu.make_async_copy(kept_hbm.at[me], kept_ref, kept_sem)
    class_copy = pltpu.make_async_copy(class_hbm, class_ref, class_sem)
    class_copy.start()
    kept_copy.start()
    v_all[:, :, :HD] = qkv_ref[:, 2]
    v_all[:, :, HD:] = jnp.ones((block_count, BLOCK, HD), jnp.bfloat16)
    class_copy.wait()

    def scores(query_rows, key_rows):
        return lax.dot_general(
            query_rows, key_rows, (((1,), (1,)), ((), ())), preferred_element_type=jnp.float32
        )

    def weigh(rows, columns, slot):
        logits = logits_slots[slot][:rows, :columns]
        largest = jnp.max(logits, axis=-1, keepdims=True)
        weights = jnp.exp2((logits - largest) * exponent_scale).astype(jnp.bfloat16)
        weights_slots[slot][:rows, :columns] = weights

    def normalized(summed):
        totals = summed[:, HD:]
        inverse = pl.reciprocal(totals, approx=True)
        inverse = inverse * (2.0 - totals * inverse)
        return (summed[:, :HD] * inverse).astype(jnp.bfloat16)

    @pl.when(class_ref[me] == 1)
    def _():
        sizes = [2] + [4] * (block_count // 4 - 1) + [2]
        starts = [sum(sizes[:i]) for i in range(len(sizes))]

        def score(i):
            rows = sizes[i] * BLOCK
            query_rows = qkv_ref[starts[i] : starts[i] + sizes[i], 0].reshape(rows, HD)
            key_rows = qkv_ref[:, 1].reshape(block_count * BLOCK, HD)
            logits_slots[i % 2][:rows, :] = scores(query_rows, key_rows)

        def weigh_all(i):
            weigh(sizes[i] * BLOCK, block_count * BLOCK, i % 2)

        def blend(i):
            rows = sizes[i] * BLOCK
            value_rows = v_all[...].reshape(block_count * BLOCK, 2 * HD)
            weights = weights_slots[i % 2][:rows, :]
            out = normalized(jnp.dot(weights, value_rows, preferred_element_type=jnp.float32))
            out_ref[starts[i] : starts[i] + sizes[i]] = out.reshape(sizes[i], BLOCK, HD)

        score(0)
        weigh_all(0)
        score(1)
        for i in range(1, len(sizes)):
            blend(i - 1)
            weigh_all(i)
            if i + 1 < len(sizes):
                score(i + 1)
        blend(len(sizes) - 1)
        kept_copy.wait()

    @pl.when(class_ref[me] != 1)
    def _():
        kept_copy.wait()
        group = 2

        def block_pairs(block):
            kept_blocks = each_light_block(kept_ref, block)
            return list(zip(kept_blocks[::2], kept_blocks[1::2]))

        def score(i, slot):
            for member in range(group):
                block = group * i + member
                rows = slice(member * BLOCK, (member + 1) * BLOCK)
                for place, (one, other) in enumerate(block_pairs(block)):
                    key_rows = jnp.concatenate([qkv_ref[one, 1], qkv_ref[other, 1]], axis=0)
                    columns = slice(place * 2 * BLOCK, (place + 1) * 2 * BLOCK)
                    logits_slots[slot][rows, columns] = scores(qkv_ref[block, 0], key_rows)

        def blend(i, slot):
            for member in range(group):
                block = group * i + member
                rows = slice(member * BLOCK, (member + 1) * BLOCK)
                summed = jnp.zeros((BLOCK, 2 * HD), jnp.float32)
                for place, (one, other) in enumerate(block_pairs(block)):
                    value_rows = jnp.concatenate([v_all[one], v_all[other]], axis=0)
                    columns = slice(place * 2 * BLOCK, (place + 1) * 2 * BLOCK)
                    weights = weights_slots[slot][rows, columns]
                    summed += jnp.dot(weights, value_rows, preferred_element_type=jnp.float32)
                out_ref[block] = normalized(summed)

        def weigh_few(i, slot):
            weigh(group * BLOCK, block_count // KEEP * LIGHT * BLOCK, slot)

        pipelined(block_count // group, score, weigh_few, blend)


def heads_by_device(queries, keys, values, kept, dense_class):
    axes = ("seq", "blk")
    block_count = kept.shape[1]
    in_vmem = pl.BlockSpec(memory_space=pltpu.VMEM)

    def exchange(send):
        return lax.all_to_all(send, axes, split_axis=0, concat_axis=0, tiled=True)

    held = exchange(pack_heads(queries, keys, values))
    stage_rows = 4 * BLOCK
    attended = pl.pallas_call(
        lambda *refs: attend_kernel(axes, *refs),
        out_shape=jax.ShapeDtypeStruct((block_count, BLOCK, HD), jnp.bfloat16),
        in_specs=[
            pl.BlockSpec(memory_space=pl.ANY),
            pl.BlockSpec(memory_space=pl.ANY),
            in_vmem,
        ],
        out_specs=in_vmem,
        scratch_shapes=[
            pltpu.SMEM(kept.shape[1:], jnp.int32),
            pltpu.SMEM(dense_class.shape, jnp.int32),
            pltpu.VMEM((block_count, BLOCK, 2 * HD), jnp.bfloat16),
            pltpu.VMEM((stage_rows, block_count * BLOCK), jnp.float32),
            pltpu.VMEM((stage_rows, block_count * BLOCK), jnp.float32),
            pltpu.VMEM((stage_rows, block_count * BLOCK), jnp.bfloat16),
            pltpu.VMEM((stage_rows, block_count * BLOCK), jnp.bfloat16),
            pltpu.SemaphoreType.DMA,
            pltpu.SemaphoreType.DMA,
        ],
        compiler_params=pltpu.CompilerParams(vmem_limit_bytes=40 * 1024 * 1024),
        name="attend_head",
    )(kept, dense_class, held)
    return unpack_heads(exchange(attended))


def shards(queries, keys, values, kept, dense_class):
    devices = lax.axis_size("seq") * lax.axis_size("blk")
    one_head_each = devices == HEADS
    one_block_each = queries.shape[0] == BLOCK
    every_block_kept = kept.shape[1] == kept.shape[2]
    if one_head_each and one_block_each and every_block_kept:
        return heads_by_device(queries, keys, values, kept, dense_class)
    return spans_by_device(queries, keys, values, kept, dense_class)


def solution(mesh):
    return jax.shard_map(
        shards,
        mesh=mesh,
        in_specs=(
            P(("clip", "seq", "blk"), None),
            P(("clip", "seq", "blk"), None),
            P(("clip", "seq", "blk"), None),
            P(),
            P(),
        ),
        out_specs=P(("clip", "seq", "blk"), None),
        check_vma=False,
    )
```

```python
import math

import jax
import jax.numpy as jnp
from jax import lax
from jax.experimental import pallas as pl
from jax.experimental.pallas import tpu as pltpu
from jax.sharding import PartitionSpec as P

HEADS = 16
HD = 128
BLOCK = 128
KEEP = 4
LIGHT = 2


def combine_spans(partial_out, maxima, totals, along):
    largest = jnp.max(maxima, axis=along, keepdims=True)
    factor = jnp.exp(maxima - largest)
    numerator = jnp.sum(factor[..., None] * partial_out, axis=along)
    denominator = jnp.sum(factor * totals, axis=along)
    return (numerator / denominator[..., None]).astype(jnp.bfloat16)


def attend_blocks(query_rows, key_blocks, blocked_value_rows, local_ids, slot_count):
    query_blocks, part_rows, head_depth = query_rows.shape
    group_size = query_blocks
    while group_size * part_rows > 512 and group_size % 2 == 0:
        group_size = group_size // 2
    logit_scale_factor = 1.0 / math.sqrt(head_depth)
    block_rows = key_blocks.shape[1]

    def one_group(operands):
        queries_group, ids_group = operands
        collected_key_blocks = key_blocks[ids_group].reshape(
            group_size, slot_count * block_rows, head_depth
        )
        gathered_v = blocked_value_rows[ids_group].reshape(
            group_size, slot_count * block_rows, head_depth
        )
        attention_logits = (
            jnp.einsum(
                "gpd,gkd->gpk",
                queries_group,
                collected_key_blocks,
                preferred_element_type=jnp.float32,
            )
            * logit_scale_factor
        )
        maxima = jnp.max(attention_logits, axis=-1)
        weights = jnp.exp(attention_logits - maxima[..., None])
        totals = jnp.sum(weights, axis=-1)
        partial_out = jnp.einsum(
            "gpk,gkd->gpd",
            weights.astype(jnp.bfloat16),
            gathered_v,
            preferred_element_type=jnp.float32,
        )
        return (partial_out, maxima, totals)

    grouped_q = query_rows.reshape(query_blocks // group_size, group_size, part_rows, head_depth)
    grouped_ids = local_ids[:, :slot_count].reshape(
        query_blocks // group_size, group_size, slot_count
    )
    partial_out, maxima, totals = lax.map(one_group, (grouped_q, grouped_ids))
    return (
        partial_out.reshape(query_blocks, part_rows, head_depth),
        maxima.reshape(query_blocks, part_rows),
        totals.reshape(query_blocks, part_rows),
    )


def arrange_heads(stacked):
    swapped = jnp.swapaxes(stacked, 0, 1)
    return swapped.reshape((-1,) + stacked.shape[2:])


def spans_by_device(queries, keys, values, kept, dense_class):
    seq_devices = lax.axis_size("seq")
    span_count = lax.axis_size("blk")
    local_rows = queries.shape[0]
    head_count = HEADS
    head_depth = HD
    local_blocks = local_rows // BLOCK
    row_parts = max(1, 2 * seq_devices // head_count)
    part_rows = BLOCK // row_parts
    item_count = head_count * row_parts
    per_device = item_count // seq_devices
    seq_place = lax.axis_index("seq")
    blk_place = lax.axis_index("blk")
    every_item = jnp.arange(item_count, dtype=jnp.int32)
    all_item_heads = every_item // row_parts
    item_heads = lax.dynamic_slice_in_dim(all_item_heads, seq_place * per_device, per_device)
    grid_q = queries.reshape(local_blocks, row_parts, part_rows, head_count, head_depth).transpose(
        1, 3, 0, 2, 4
    )
    grid_q = grid_q.reshape(row_parts, head_count, local_blocks * part_rows, head_depth)
    head_keys = keys.reshape(local_rows, head_count, head_depth).transpose(1, 0, 2)
    head_values = values.reshape(local_rows, head_count, head_depth).transpose(1, 0, 2)
    send_q = arrange_heads(grid_q)
    q_items = lax.all_to_all(send_q, "seq", split_axis=0, concat_axis=1, tiled=True)
    stride = 1
    grid_k = jnp.broadcast_to(head_keys[None], (row_parts, head_count, local_rows, head_depth))
    grid_v = jnp.broadcast_to(head_values[None], (row_parts, head_count, local_rows, head_depth))
    send_k = arrange_heads(grid_k)
    send_v = arrange_heads(grid_v)
    k_held, v_held = (
        lax.all_to_all(send_k, "seq", split_axis=0, concat_axis=1, tiled=True),
        lax.all_to_all(send_v, "seq", split_axis=0, concat_axis=1, tiled=True),
    )
    key_blocks = k_held.reshape(per_device, seq_devices * local_blocks, BLOCK, head_depth)
    blocked_value_rows = v_held.reshape(per_device, seq_devices * local_blocks, BLOCK, head_depth)
    item_slot = jnp.arange(per_device, dtype=jnp.int32) // stride
    item_class = jnp.take(dense_class, item_heads)
    item_kept = jnp.take(kept, item_heads, axis=0)
    source_index = jnp.arange(seq_devices, dtype=jnp.int32)
    block_index = jnp.arange(local_blocks, dtype=jnp.int32)
    span_index = jnp.arange(span_count, dtype=jnp.int32)
    all_ids = (
        (source_index[None, :, None] * span_count + span_index[:, None, None]) * local_blocks
        + block_index[None, None, :]
    ).reshape(-1)
    all_kept = jnp.take(item_kept, all_ids, axis=1)
    span_ids = lax.dynamic_slice_in_dim(all_kept, blk_place * KEEP, KEEP, axis=2)
    q_all = lax.all_gather(q_items, "blk", axis=1, tiled=True)
    query_rows = q_all.reshape(
        per_device, span_count * seq_devices * local_blocks, part_rows, head_depth
    )

    def one_item(operands):
        rows_item, ids_item, class_item, slot_item = operands
        keys_item = lax.dynamic_index_in_dim(key_blocks, slot_item, 0, keepdims=False)
        values_item = lax.dynamic_index_in_dim(blocked_value_rows, slot_item, 0, keepdims=False)
        return lax.cond(
            class_item == 1,
            lambda: attend_blocks(rows_item, keys_item, values_item, ids_item, KEEP),
            lambda: attend_blocks(rows_item, keys_item, values_item, ids_item, LIGHT),
        )

    partial_out, maxima, totals = lax.map(
        one_item,
        (
            query_rows,
            span_ids // (local_blocks * span_count) * local_blocks + span_ids % local_blocks,
            item_class,
            item_slot,
        ),
    )
    own_blocks = seq_devices * local_blocks
    shaped_out = partial_out.reshape(per_device, span_count, own_blocks, part_rows, head_depth)
    shaped_max = maxima.reshape(per_device, span_count, own_blocks, part_rows)
    shaped_total = totals.reshape(per_device, span_count, own_blocks, part_rows)
    got_out, got_max, got_total = (
        lax.all_to_all(shaped_out, "blk", split_axis=1, concat_axis=1, tiled=True),
        lax.all_to_all(shaped_max, "blk", split_axis=1, concat_axis=1, tiled=True),
        lax.all_to_all(shaped_total, "blk", split_axis=1, concat_axis=1, tiled=True),
    )
    attended_items = combine_spans(got_out, got_max, got_total, 1)
    attended_items = attended_items.reshape(
        per_device, seq_devices * local_blocks * part_rows, head_depth
    )
    returned = lax.all_to_all(attended_items, "seq", split_axis=1, concat_axis=0, tiled=True)
    grid_out = returned.reshape(head_count, row_parts, local_blocks, part_rows, head_depth)
    grid_out = jnp.swapaxes(grid_out, 0, 1)
    return grid_out.transpose(2, 0, 3, 1, 4).reshape(local_rows, head_count * head_depth)


def own_place(axes):
    place = 0
    for axis in axes:
        place = place * lax.axis_size(axis) + lax.axis_index(axis)
    return place


def each_light_block(kept_ref, block):
    return [
        kept_ref[block, span * KEEP + slot]
        for span in range(kept_ref.shape[1] // KEEP)
        for slot in range(LIGHT)
    ]


def pack_kernel(*refs):
    sources, (out_ref, landed, sems) = refs[:-3], refs[-3:]
    heads = out_ref.shape[0]
    rows = landed.shape[1]
    pieces = sems.shape[1]
    piece_rows = rows // pieces
    arrivals = [
        [
            pltpu.make_async_copy(
                source.at[pl.ds(piece * piece_rows, piece_rows), :],
                landed.at[place, pl.ds(piece * piece_rows, piece_rows), :],
                sems.at[place, piece],
            )
            for piece in range(pieces)
        ]
        for place, source in enumerate(sources)
    ]
    for copies in arrivals:
        for copy in copies:
            copy.start()
    for place, copies in enumerate(arrivals):
        for piece, copy in enumerate(copies):
            copy.wait()
            kept_rows = slice(piece * piece_rows, (piece + 1) * piece_rows)
            for head in range(heads):
                out_ref[head, place, kept_rows, :] = landed[
                    place, kept_rows, head * HD : (head + 1) * HD
                ]


def pack_heads(*sources):
    count = len(sources)
    rows = sources[0].shape[0]
    pieces = 4
    return pl.pallas_call(
        pack_kernel,
        out_shape=jax.ShapeDtypeStruct((HEADS, count, rows, HD), jnp.bfloat16),
        in_specs=[pl.BlockSpec(memory_space=pltpu.HBM)] * count,
        out_specs=pl.BlockSpec(memory_space=pltpu.VMEM),
        scratch_shapes=[
            pltpu.VMEM((count, rows, HEADS * HD), jnp.bfloat16),
            pltpu.SemaphoreType.DMA((count, pieces)),
        ],
        compiler_params=pltpu.CompilerParams(vmem_limit_bytes=8 * 1024 * 1024),
        name="pack_heads",
    )(*[pltpu.with_memory_space_constraint(source, pltpu.HBM) for source in sources])


def unpack_kernel(held_ref, out_ref, turned, sems):
    heads = held_ref.shape[0]
    pieces = sems.shape[0]
    piece_rows = turned.shape[0] // pieces
    departures = []
    for piece in range(pieces):
        rows = slice(piece * piece_rows, (piece + 1) * piece_rows)
        for head in range(heads):
            turned[rows, head * HD : (head + 1) * HD] = held_ref[head, rows, :]
        departure = pltpu.make_async_copy(
            turned.at[pl.ds(piece * piece_rows, piece_rows), :],
            out_ref.at[pl.ds(piece * piece_rows, piece_rows), :],
            sems.at[piece],
        )
        departure.start()
        departures.append(departure)
    for departure in departures:
        departure.wait()


def unpack_heads(held):
    heads, rows, depth = held.shape
    return pl.pallas_call(
        unpack_kernel,
        out_shape=jax.ShapeDtypeStruct((rows, heads * depth), jnp.bfloat16),
        in_specs=[pl.BlockSpec(memory_space=pltpu.VMEM)],
        out_specs=pl.BlockSpec(memory_space=pltpu.HBM),
        scratch_shapes=[
            pltpu.VMEM((rows, heads * depth), jnp.bfloat16),
            pltpu.SemaphoreType.DMA((4,)),
        ],
        compiler_params=pltpu.CompilerParams(vmem_limit_bytes=8 * 1024 * 1024),
        name="unpack_heads",
    )(held)


def pipelined(count, score, weigh, blend):
    score(0, 0)
    weigh(0, 0)
    score(1, 1)

    def step(j, carry):
        blend(2 * j, 0)
        weigh(2 * j + 1, 1)
        score(2 * j + 2, 0)
        blend(2 * j + 1, 1)
        weigh(2 * j + 2, 0)
        score(2 * j + 3, 1)
        return carry

    lax.fori_loop(0, count // 2 - 1, step, 0)
    blend(count - 2, 0)
    weigh(count - 1, 1)
    blend(count - 1, 1)


def attend_kernel(axes, kept_hbm, class_hbm, qkv_ref, out_ref, *scratch):
    kept_ref, class_ref, v_all, logits_a, logits_b, weights_a, weights_b, kept_sem, class_sem = scratch
    logits_slots = (logits_a, logits_b)
    weights_slots = (weights_a, weights_b)
    block_count = qkv_ref.shape[0]
    me = own_place(axes)
    exponent_scale = math.log2(math.e) / math.sqrt(HD)
    kept_copy = pltpu.make_async_copy(kept_hbm.at[me], kept_ref, kept_sem)
    class_copy = pltpu.make_async_copy(class_hbm, class_ref, class_sem)
    class_copy.start()
    kept_copy.start()
    v_all[:, :, :HD] = qkv_ref[:, 2]
    v_all[:, :, HD:] = jnp.ones((block_count, BLOCK, HD), jnp.bfloat16)
    class_copy.wait()

    def scores(query_rows, key_rows):
        return lax.dot_general(
            query_rows, key_rows, (((1,), (1,)), ((), ())), preferred_element_type=jnp.float32
        )

    def weigh(rows, columns, slot):
        logits = logits_slots[slot][:rows, :columns]
        largest = jnp.max(logits, axis=-1, keepdims=True)
        weights = jnp.exp2((logits - largest) * exponent_scale).astype(jnp.bfloat16)
        weights_slots[slot][:rows, :columns] = weights

    def normalized(summed):
        return (summed[:, :HD] / summed[:, HD:]).astype(jnp.bfloat16)

    @pl.when(class_ref[me] == 1)
    def _():
        sizes = [1, 3] + [4] * (block_count // 4 - 2) + [3, 1]
        starts = [sum(sizes[:i]) for i in range(len(sizes))]

        def score(i):
            rows = sizes[i] * BLOCK
            query_rows = qkv_ref[starts[i] : starts[i] + sizes[i], 0].reshape(rows, HD)
            key_rows = qkv_ref[:, 1].reshape(block_count * BLOCK, HD)
            logits_slots[i % 2][:rows, :] = scores(query_rows, key_rows)

        def weigh_all(i):
            weigh(sizes[i] * BLOCK, block_count * BLOCK, i % 2)

        def blend(i):
            rows = sizes[i] * BLOCK
            value_rows = v_all[...].reshape(block_count * BLOCK, 2 * HD)
            weights = weights_slots[i % 2][:rows, :]
            out = normalized(jnp.dot(weights, value_rows, preferred_element_type=jnp.float32))
            out_ref[starts[i] : starts[i] + sizes[i]] = out.reshape(sizes[i], BLOCK, HD)

        score(0)
        weigh_all(0)
        score(1)
        for i in range(1, len(sizes)):
            blend(i - 1)
            weigh_all(i)
            if i + 1 < len(sizes):
                score(i + 1)
        blend(len(sizes) - 1)
        kept_copy.wait()

    @pl.when(class_ref[me] != 1)
    def _():
        kept_copy.wait()
        group = 2

        def block_pairs(block):
            kept_blocks = each_light_block(kept_ref, block)
            return list(zip(kept_blocks[::2], kept_blocks[1::2]))

        def score(i, slot):
            for member in range(group):
                block = group * i + member
                rows = slice(member * BLOCK, (member + 1) * BLOCK)
                for place, (one, other) in enumerate(block_pairs(block)):
                    key_rows = jnp.concatenate([qkv_ref[one, 1], qkv_ref[other, 1]], axis=0)
                    columns = slice(place * 2 * BLOCK, (place + 1) * 2 * BLOCK)
                    logits_slots[slot][rows, columns] = scores(qkv_ref[block, 0], key_rows)

        def blend(i, slot):
            for member in range(group):
                block = group * i + member
                rows = slice(member * BLOCK, (member + 1) * BLOCK)
                summed = jnp.zeros((BLOCK, 2 * HD), jnp.float32)
                for place, (one, other) in enumerate(block_pairs(block)):
                    value_rows = jnp.concatenate([v_all[one], v_all[other]], axis=0)
                    columns = slice(place * 2 * BLOCK, (place + 1) * 2 * BLOCK)
                    weights = weights_slots[slot][rows, columns]
                    summed += jnp.dot(weights, value_rows, preferred_element_type=jnp.float32)
                out_ref[block] = normalized(summed)

        def weigh_few(i, slot):
            weigh(group * BLOCK, block_count // KEEP * LIGHT * BLOCK, slot)

        pipelined(block_count // group, score, weigh_few, blend)


def heads_by_device(queries, keys, values, kept, dense_class):
    axes = ("seq", "blk")
    block_count = kept.shape[1]
    in_vmem = pl.BlockSpec(memory_space=pltpu.VMEM)

    def exchange(send):
        return lax.all_to_all(send, axes, split_axis=0, concat_axis=0, tiled=True)

    held = exchange(pack_heads(queries, keys, values))
    stage_rows = 4 * BLOCK
    attended = pl.pallas_call(
        lambda *refs: attend_kernel(axes, *refs),
        out_shape=jax.ShapeDtypeStruct((block_count, BLOCK, HD), jnp.bfloat16),
        in_specs=[
            pl.BlockSpec(memory_space=pl.ANY),
            pl.BlockSpec(memory_space=pl.ANY),
            in_vmem,
        ],
        out_specs=in_vmem,
        scratch_shapes=[
            pltpu.SMEM(kept.shape[1:], jnp.int32),
            pltpu.SMEM(dense_class.shape, jnp.int32),
            pltpu.VMEM((block_count, BLOCK, 2 * HD), jnp.bfloat16),
            pltpu.VMEM((stage_rows, block_count * BLOCK), jnp.float32),
            pltpu.VMEM((stage_rows, block_count * BLOCK), jnp.float32),
            pltpu.VMEM((stage_rows, block_count * BLOCK), jnp.bfloat16),
            pltpu.VMEM((stage_rows, block_count * BLOCK), jnp.bfloat16),
            pltpu.SemaphoreType.DMA,
            pltpu.SemaphoreType.DMA,
        ],
        compiler_params=pltpu.CompilerParams(vmem_limit_bytes=40 * 1024 * 1024),
        name="attend_head",
    )(kept, dense_class, held)
    return unpack_heads(exchange(attended))


def shards(queries, keys, values, kept, dense_class):
    devices = lax.axis_size("seq") * lax.axis_size("blk")
    one_head_each = devices == HEADS
    one_block_each = queries.shape[0] == BLOCK
    every_block_kept = kept.shape[1] == kept.shape[2]
    if one_head_each and one_block_each and every_block_kept:
        return heads_by_device(queries, keys, values, kept, dense_class)
    return spans_by_device(queries, keys, values, kept, dense_class)


def solution(mesh):
    return jax.shard_map(
        shards,
        mesh=mesh,
        in_specs=(
            P(("clip", "seq", "blk"), None),
            P(("clip", "seq", "blk"), None),
            P(("clip", "seq", "blk"), None),
            P(),
            P(),
        ),
        out_specs=P(("clip", "seq", "blk"), None),
        check_vma=False,
    )
```

```python
import math

import jax
import jax.numpy as jnp
from jax import lax
from jax.experimental import pallas as pl
from jax.experimental.pallas import tpu as pltpu
from jax.sharding import PartitionSpec as P

HEADS = 16
HD = 128
BLOCK = 128
KEEP = 4
LIGHT = 2


def combine_spans(partial_out, maxima, totals, along):
    largest = jnp.max(maxima, axis=along, keepdims=True)
    factor = jnp.exp(maxima - largest)
    numerator = jnp.sum(factor[..., None] * partial_out, axis=along)
    denominator = jnp.sum(factor * totals, axis=along)
    return (numerator / denominator[..., None]).astype(jnp.bfloat16)


def attend_blocks(query_rows, key_blocks, blocked_value_rows, local_ids, slot_count):
    query_blocks, part_rows, head_depth = query_rows.shape
    group_size = query_blocks
    while group_size * part_rows > 512 and group_size % 2 == 0:
        group_size = group_size // 2
    logit_scale_factor = 1.0 / math.sqrt(head_depth)
    block_rows = key_blocks.shape[1]

    def one_group(operands):
        queries_group, ids_group = operands
        collected_key_blocks = key_blocks[ids_group].reshape(
            group_size, slot_count * block_rows, head_depth
        )
        gathered_v = blocked_value_rows[ids_group].reshape(
            group_size, slot_count * block_rows, head_depth
        )
        attention_logits = (
            jnp.einsum(
                "gpd,gkd->gpk",
                queries_group,
                collected_key_blocks,
                preferred_element_type=jnp.float32,
            )
            * logit_scale_factor
        )
        maxima = jnp.max(attention_logits, axis=-1)
        weights = jnp.exp(attention_logits - maxima[..., None])
        totals = jnp.sum(weights, axis=-1)
        partial_out = jnp.einsum(
            "gpk,gkd->gpd",
            weights.astype(jnp.bfloat16),
            gathered_v,
            preferred_element_type=jnp.float32,
        )
        return (partial_out, maxima, totals)

    grouped_q = query_rows.reshape(query_blocks // group_size, group_size, part_rows, head_depth)
    grouped_ids = local_ids[:, :slot_count].reshape(
        query_blocks // group_size, group_size, slot_count
    )
    partial_out, maxima, totals = lax.map(one_group, (grouped_q, grouped_ids))
    return (
        partial_out.reshape(query_blocks, part_rows, head_depth),
        maxima.reshape(query_blocks, part_rows),
        totals.reshape(query_blocks, part_rows),
    )


def arrange_heads(stacked):
    swapped = jnp.swapaxes(stacked, 0, 1)
    return swapped.reshape((-1,) + stacked.shape[2:])


def spans_by_device(queries, keys, values, kept, dense_class):
    seq_devices = lax.axis_size("seq")
    span_count = lax.axis_size("blk")
    local_rows = queries.shape[0]
    head_count = HEADS
    head_depth = HD
    local_blocks = local_rows // BLOCK
    row_parts = max(1, 2 * seq_devices // head_count)
    part_rows = BLOCK // row_parts
    item_count = head_count * row_parts
    per_device = item_count // seq_devices
    seq_place = lax.axis_index("seq")
    blk_place = lax.axis_index("blk")
    every_item = jnp.arange(item_count, dtype=jnp.int32)
    all_item_heads = every_item // row_parts
    item_heads = lax.dynamic_slice_in_dim(all_item_heads, seq_place * per_device, per_device)
    grid_q = queries.reshape(local_blocks, row_parts, part_rows, head_count, head_depth).transpose(
        1, 3, 0, 2, 4
    )
    grid_q = grid_q.reshape(row_parts, head_count, local_blocks * part_rows, head_depth)
    head_keys = keys.reshape(local_rows, head_count, head_depth).transpose(1, 0, 2)
    head_values = values.reshape(local_rows, head_count, head_depth).transpose(1, 0, 2)
    send_q = arrange_heads(grid_q)
    q_items = lax.all_to_all(send_q, "seq", split_axis=0, concat_axis=1, tiled=True)
    stride = 1
    grid_k = jnp.broadcast_to(head_keys[None], (row_parts, head_count, local_rows, head_depth))
    grid_v = jnp.broadcast_to(head_values[None], (row_parts, head_count, local_rows, head_depth))
    send_k = arrange_heads(grid_k)
    send_v = arrange_heads(grid_v)
    k_held, v_held = (
        lax.all_to_all(send_k, "seq", split_axis=0, concat_axis=1, tiled=True),
        lax.all_to_all(send_v, "seq", split_axis=0, concat_axis=1, tiled=True),
    )
    key_blocks = k_held.reshape(per_device, seq_devices * local_blocks, BLOCK, head_depth)
    blocked_value_rows = v_held.reshape(per_device, seq_devices * local_blocks, BLOCK, head_depth)
    item_slot = jnp.arange(per_device, dtype=jnp.int32) // stride
    item_class = jnp.take(dense_class, item_heads)
    item_kept = jnp.take(kept, item_heads, axis=0)
    source_index = jnp.arange(seq_devices, dtype=jnp.int32)
    block_index = jnp.arange(local_blocks, dtype=jnp.int32)
    span_index = jnp.arange(span_count, dtype=jnp.int32)
    all_ids = (
        (source_index[None, :, None] * span_count + span_index[:, None, None]) * local_blocks
        + block_index[None, None, :]
    ).reshape(-1)
    all_kept = jnp.take(item_kept, all_ids, axis=1)
    span_ids = lax.dynamic_slice_in_dim(all_kept, blk_place * KEEP, KEEP, axis=2)
    q_all = lax.all_gather(q_items, "blk", axis=1, tiled=True)
    query_rows = q_all.reshape(
        per_device, span_count * seq_devices * local_blocks, part_rows, head_depth
    )

    def one_item(operands):
        rows_item, ids_item, class_item, slot_item = operands
        keys_item = lax.dynamic_index_in_dim(key_blocks, slot_item, 0, keepdims=False)
        values_item = lax.dynamic_index_in_dim(blocked_value_rows, slot_item, 0, keepdims=False)
        return lax.cond(
            class_item == 1,
            lambda: attend_blocks(rows_item, keys_item, values_item, ids_item, KEEP),
            lambda: attend_blocks(rows_item, keys_item, values_item, ids_item, LIGHT),
        )

    partial_out, maxima, totals = lax.map(
        one_item,
        (
            query_rows,
            span_ids // (local_blocks * span_count) * local_blocks + span_ids % local_blocks,
            item_class,
            item_slot,
        ),
    )
    own_blocks = seq_devices * local_blocks
    shaped_out = partial_out.reshape(per_device, span_count, own_blocks, part_rows, head_depth)
    shaped_max = maxima.reshape(per_device, span_count, own_blocks, part_rows)
    shaped_total = totals.reshape(per_device, span_count, own_blocks, part_rows)
    got_out, got_max, got_total = (
        lax.all_to_all(shaped_out, "blk", split_axis=1, concat_axis=1, tiled=True),
        lax.all_to_all(shaped_max, "blk", split_axis=1, concat_axis=1, tiled=True),
        lax.all_to_all(shaped_total, "blk", split_axis=1, concat_axis=1, tiled=True),
    )
    attended_items = combine_spans(got_out, got_max, got_total, 1)
    attended_items = attended_items.reshape(
        per_device, seq_devices * local_blocks * part_rows, head_depth
    )
    returned = lax.all_to_all(attended_items, "seq", split_axis=1, concat_axis=0, tiled=True)
    grid_out = returned.reshape(head_count, row_parts, local_blocks, part_rows, head_depth)
    grid_out = jnp.swapaxes(grid_out, 0, 1)
    return grid_out.transpose(2, 0, 3, 1, 4).reshape(local_rows, head_count * head_depth)


def own_place(axes):
    place = 0
    for axis in axes:
        place = place * lax.axis_size(axis) + lax.axis_index(axis)
    return place


def each_light_block(kept_ref, block):
    return [
        kept_ref[block, span * KEEP + slot]
        for span in range(kept_ref.shape[1] // KEEP)
        for slot in range(LIGHT)
    ]


def pack_kernel(*refs):
    sources, (out_ref, landed, sems) = refs[:-3], refs[-3:]
    heads = out_ref.shape[0]
    rows = landed.shape[1]
    pieces = sems.shape[1]
    piece_rows = rows // pieces
    arrivals = [
        [
            pltpu.make_async_copy(
                source.at[pl.ds(piece * piece_rows, piece_rows), :],
                landed.at[place, pl.ds(piece * piece_rows, piece_rows), :],
                sems.at[place, piece],
            )
            for piece in range(pieces)
        ]
        for place, source in enumerate(sources)
    ]
    for copies in arrivals:
        for copy in copies:
            copy.start()
    for place, copies in enumerate(arrivals):
        for piece, copy in enumerate(copies):
            copy.wait()
            kept_rows = slice(piece * piece_rows, (piece + 1) * piece_rows)
            for head in range(heads):
                out_ref[head, place, kept_rows, :] = landed[
                    place, kept_rows, head * HD : (head + 1) * HD
                ]


def pack_heads(*sources):
    count = len(sources)
    rows = sources[0].shape[0]
    pieces = 8
    return pl.pallas_call(
        pack_kernel,
        out_shape=jax.ShapeDtypeStruct((HEADS, count, rows, HD), jnp.bfloat16),
        in_specs=[pl.BlockSpec(memory_space=pltpu.HBM)] * count,
        out_specs=pl.BlockSpec(memory_space=pltpu.VMEM),
        scratch_shapes=[
            pltpu.VMEM((count, rows, HEADS * HD), jnp.bfloat16),
            pltpu.SemaphoreType.DMA((count, pieces)),
        ],
        compiler_params=pltpu.CompilerParams(vmem_limit_bytes=8 * 1024 * 1024),
        name="pack_heads",
    )(*[pltpu.with_memory_space_constraint(source, pltpu.HBM) for source in sources])


def unpack_kernel(held_ref, out_ref, turned, sems):
    heads = held_ref.shape[0]
    pieces = sems.shape[0]
    piece_rows = turned.shape[0] // pieces
    departures = []
    for piece in range(pieces):
        rows = slice(piece * piece_rows, (piece + 1) * piece_rows)
        for head in range(heads):
            turned[rows, head * HD : (head + 1) * HD] = held_ref[head, rows, :]
        departure = pltpu.make_async_copy(
            turned.at[pl.ds(piece * piece_rows, piece_rows), :],
            out_ref.at[pl.ds(piece * piece_rows, piece_rows), :],
            sems.at[piece],
        )
        departure.start()
        departures.append(departure)
    for departure in departures:
        departure.wait()


def unpack_heads(held):
    heads, rows, depth = held.shape
    return pl.pallas_call(
        unpack_kernel,
        out_shape=jax.ShapeDtypeStruct((rows, heads * depth), jnp.bfloat16),
        in_specs=[pl.BlockSpec(memory_space=pltpu.VMEM)],
        out_specs=pl.BlockSpec(memory_space=pltpu.HBM),
        scratch_shapes=[
            pltpu.VMEM((rows, heads * depth), jnp.bfloat16),
            pltpu.SemaphoreType.DMA((4,)),
        ],
        compiler_params=pltpu.CompilerParams(vmem_limit_bytes=8 * 1024 * 1024),
        name="unpack_heads",
    )(held)


def pipelined(count, score, weigh, blend):
    score(0, 0)
    weigh(0, 0)
    score(1, 1)

    def step(j, carry):
        blend(2 * j, 0)
        weigh(2 * j + 1, 1)
        score(2 * j + 2, 0)
        blend(2 * j + 1, 1)
        weigh(2 * j + 2, 0)
        score(2 * j + 3, 1)
        return carry

    lax.fori_loop(0, count // 2 - 1, step, 0)
    blend(count - 2, 0)
    weigh(count - 1, 1)
    blend(count - 1, 1)


def attend_kernel(axes, kept_hbm, class_hbm, qkv_ref, out_ref, *scratch):
    kept_ref, class_ref, v_all, logits_a, logits_b, weights_a, weights_b, kept_sem, class_sem = scratch
    logits_slots = (logits_a, logits_b)
    weights_slots = (weights_a, weights_b)
    block_count = qkv_ref.shape[0]
    me = own_place(axes)
    exponent_scale = math.log2(math.e) / math.sqrt(HD)
    kept_copy = pltpu.make_async_copy(kept_hbm.at[me], kept_ref, kept_sem)
    class_copy = pltpu.make_async_copy(class_hbm, class_ref, class_sem)
    class_copy.start()
    kept_copy.start()
    v_all[:, :, :HD] = qkv_ref[:, 2]
    v_all[:, :, HD:] = jnp.ones((block_count, BLOCK, HD), jnp.bfloat16)
    class_copy.wait()

    def scores(query_rows, key_rows):
        return lax.dot_general(
            query_rows, key_rows, (((1,), (1,)), ((), ())), preferred_element_type=jnp.float32
        )

    def weigh(rows, columns, slot):
        logits = logits_slots[slot][:rows, :columns]
        largest = jnp.max(logits, axis=-1, keepdims=True)
        weights = jnp.exp2((logits - largest) * exponent_scale).astype(jnp.bfloat16)
        weights_slots[slot][:rows, :columns] = weights

    def normalized(summed):
        return (summed[:, :HD] / summed[:, HD:]).astype(jnp.bfloat16)

    @pl.when(class_ref[me] == 1)
    def _():
        sizes = [2] + [4] * (block_count // 4 - 1) + [2]
        starts = [sum(sizes[:i]) for i in range(len(sizes))]

        def score(i):
            rows = sizes[i] * BLOCK
            query_rows = qkv_ref[starts[i] : starts[i] + sizes[i], 0].reshape(rows, HD)
            key_rows = qkv_ref[:, 1].reshape(block_count * BLOCK, HD)
            logits_slots[i % 2][:rows, :] = scores(query_rows, key_rows)

        def weigh_all(i):
            weigh(sizes[i] * BLOCK, block_count * BLOCK, i % 2)

        def blend(i):
            rows = sizes[i] * BLOCK
            value_rows = v_all[...].reshape(block_count * BLOCK, 2 * HD)
            weights = weights_slots[i % 2][:rows, :]
            out = normalized(jnp.dot(weights, value_rows, preferred_element_type=jnp.float32))
            out_ref[starts[i] : starts[i] + sizes[i]] = out.reshape(sizes[i], BLOCK, HD)

        score(0)
        weigh_all(0)
        score(1)
        for i in range(1, len(sizes)):
            blend(i - 1)
            weigh_all(i)
            if i + 1 < len(sizes):
                score(i + 1)
        blend(len(sizes) - 1)
        kept_copy.wait()

    @pl.when(class_ref[me] != 1)
    def _():
        kept_copy.wait()
        group = 2

        def block_pairs(block):
            kept_blocks = each_light_block(kept_ref, block)
            return list(zip(kept_blocks[::2], kept_blocks[1::2]))

        def score(i, slot):
            for member in range(group):
                block = group * i + member
                rows = slice(member * BLOCK, (member + 1) * BLOCK)
                for place, (one, other) in enumerate(block_pairs(block)):
                    key_rows = jnp.concatenate([qkv_ref[one, 1], qkv_ref[other, 1]], axis=0)
                    columns = slice(place * 2 * BLOCK, (place + 1) * 2 * BLOCK)
                    logits_slots[slot][rows, columns] = scores(qkv_ref[block, 0], key_rows)

        def blend(i, slot):
            for member in range(group):
                block = group * i + member
                rows = slice(member * BLOCK, (member + 1) * BLOCK)
                summed = jnp.zeros((BLOCK, 2 * HD), jnp.float32)
                for place, (one, other) in enumerate(block_pairs(block)):
                    value_rows = jnp.concatenate([v_all[one], v_all[other]], axis=0)
                    columns = slice(place * 2 * BLOCK, (place + 1) * 2 * BLOCK)
                    weights = weights_slots[slot][rows, columns]
                    summed += jnp.dot(weights, value_rows, preferred_element_type=jnp.float32)
                out_ref[block] = normalized(summed)

        def weigh_few(i, slot):
            weigh(group * BLOCK, block_count // KEEP * LIGHT * BLOCK, slot)

        pipelined(block_count // group, score, weigh_few, blend)


def heads_by_device(queries, keys, values, kept, dense_class):
    axes = ("seq", "blk")
    block_count = kept.shape[1]
    in_vmem = pl.BlockSpec(memory_space=pltpu.VMEM)

    def exchange(send):
        return lax.all_to_all(send, axes, split_axis=0, concat_axis=0, tiled=True)

    held = exchange(pack_heads(queries, keys, values))
    stage_rows = 4 * BLOCK
    attended = pl.pallas_call(
        lambda *refs: attend_kernel(axes, *refs),
        out_shape=jax.ShapeDtypeStruct((block_count, BLOCK, HD), jnp.bfloat16),
        in_specs=[
            pl.BlockSpec(memory_space=pl.ANY),
            pl.BlockSpec(memory_space=pl.ANY),
            in_vmem,
        ],
        out_specs=in_vmem,
        scratch_shapes=[
            pltpu.SMEM(kept.shape[1:], jnp.int32),
            pltpu.SMEM(dense_class.shape, jnp.int32),
            pltpu.VMEM((block_count, BLOCK, 2 * HD), jnp.bfloat16),
            pltpu.VMEM((stage_rows, block_count * BLOCK), jnp.float32),
            pltpu.VMEM((stage_rows, block_count * BLOCK), jnp.float32),
            pltpu.VMEM((stage_rows, block_count * BLOCK), jnp.bfloat16),
            pltpu.VMEM((stage_rows, block_count * BLOCK), jnp.bfloat16),
            pltpu.SemaphoreType.DMA,
            pltpu.SemaphoreType.DMA,
        ],
        compiler_params=pltpu.CompilerParams(vmem_limit_bytes=40 * 1024 * 1024),
        name="attend_head",
    )(kept, dense_class, held)
    return unpack_heads(exchange(attended))


def shards(queries, keys, values, kept, dense_class):
    devices = lax.axis_size("seq") * lax.axis_size("blk")
    one_head_each = devices == HEADS
    one_block_each = queries.shape[0] == BLOCK
    every_block_kept = kept.shape[1] == kept.shape[2]
    if one_head_each and one_block_each and every_block_kept:
        return heads_by_device(queries, keys, values, kept, dense_class)
    return spans_by_device(queries, keys, values, kept, dense_class)


def solution(mesh):
    return jax.shard_map(
        shards,
        mesh=mesh,
        in_specs=(
            P(("clip", "seq", "blk"), None),
            P(("clip", "seq", "blk"), None),
            P(("clip", "seq", "blk"), None),
            P(),
            P(),
        ),
        out_specs=P(("clip", "seq", "blk"), None),
        check_vma=False,
    )
```
